32 devices in a mesh: dp: 8 (over z, core), fsdp: 4 (over y, x).
Axes of the slice: x: 2, y: 2, z: 4, core: 2. Of those that a mesh axis runs over, the one named last changes fastest.
Arguments:
- tokens: bfloat16 [32768, 768], P(('dp', 'fsdp')), may hold values from -6 to 6
- first_values: bfloat16 [32768, 384], P(('dp', 'fsdp')), may hold values from -6 to 6
- out_grad: bfloat16 [32768, 768], P(('dp', 'fsdp')), may hold values from -6 to 6
- lengths: int32 [32, 2], P(('dp', 'fsdp')), may hold values from 0 to 1024, as said below
- in_proj: bfloat16 [768, 1920], P(('dp', 'fsdp')), may hold values from -0.21875 to 0.21875
- out_proj: bfloat16 [768, 768], P(('dp', 'fsdp')), may hold values from -0.875 to 0.875
- up_proj: bfloat16 [768, 3072], P(('dp', 'fsdp')), may hold values from -0.21875 to 0.21875
- down_proj: bfloat16 [3072, 768], P(('dp', 'fsdp')), may hold values from -0.109375 to 0.109375
- vectors: bfloat16 [11, 768], P(None, ('dp', 'fsdp')), may hold values from -0.9 to 1.75, as said below
Outputs:
- output: float32 [32768, 768], P(('dp', 'fsdp'))
- input_grad: float32 [32768, 768], P(('dp', 'fsdp'))
- first_values_grad: float32 [32768, 384], P(('dp', 'fsdp'))
- in_proj_grad: float32 [768, 1920], P(('dp', 'fsdp'))
- out_proj_grad: float32 [768, 768], P(('dp', 'fsdp'))
- up_proj_grad: float32 [768, 3072], P(('dp', 'fsdp'))
- down_proj_grad: float32 [3072, 768], P(('dp', 'fsdp'))
- vectors_grad: float32 [11, 768], P(None, ('dp', 'fsdp'))
The draws below stay inside these ranges and needn't reach their ends.
Inputs may be any that keep to these rules, and one draw needn't show every extreme that they name: `lengths`: each device holds either one sequence of 1024 tokens, given as (1024, 0), or two of half that length; both kinds occur in every draw. `vectors`: rows 0 and 4 are norm gains, the others shifts and biases.
All inputs are finite; a program needn't handle non-finite values.
Results may differ from the reference program's by a relative error of at most 0.0095.
Values may be sent and summed in bfloat16 or wider, within the bound.
No kernel may reach another device: no remote copies, remote signals or barrier semaphores. Data moves between devices by JAX's collectives and lax.ppermute only.
A program may use at most 256 MiB of HBM per device.

```python
import jax
import jax.numpy as jnp
from jax import lax

D = 768
H = 12
HD = 64
VH = 6
FF = 3072
TOK_DEV = 1024
QKV = 1920
VROWS = 11
TOKENS = 32768
N_DP = 8
N_FSDP = 4


def draw_vectors(key, part):
    key = jax.random.fold_in(key, 7)
    noise_draw = jnp.clip(jax.random.normal(key, (VROWS, D), jnp.float32), -3.0, 3.0)
    row_index = jnp.arange(VROWS)[:, None]
    is_gain = (row_index == 0) | (row_index == 4)
    return jnp.where(is_gain, 1.0 + 0.25 * noise_draw, 0.3 * noise_draw).astype(jnp.bfloat16)


def draw_lengths(key, part):
    key = jax.random.fold_in(key, 11)
    device_count = N_DP * N_FSDP
    picked = jax.random.randint(key, (device_count,), 0, 2).astype(jnp.int32)
    device_index = jnp.arange(device_count, dtype=jnp.int32)
    picked = jnp.where(device_index == 0, 1, jnp.where(device_index == 1, 0, picked))
    first_len = jnp.where(picked == 1, TOK_DEV, TOK_DEV // 2).astype(jnp.int32)
    second_len = (TOK_DEV - first_len).astype(jnp.int32)
    return jnp.stack([first_len, second_len], axis=1).astype(jnp.int32)


def block_levels(rng, extent, shards, smallest, high):
    gain = 1.0
    for axis_at, parts in shards:
        heights = jax.random.uniform(jax.random.fold_in(jax.random.fold_in(rng, 6), axis_at), (parts,), jnp.float32, smallest / len(shards), high / len(shards))
        gain = gain * jnp.repeat(jnp.exp(heights), extent[axis_at] // parts).reshape((-1,) + (1,) * (len(extent) - 1 - axis_at))
    return gain


def bell_draw(rng, dims, width, limit, shards=(), held_as=jnp.bfloat16):
    values = width * jax.random.normal(rng, dims, jnp.float32)
    if shards:
        values = values * block_levels(rng, dims, shards, -0.22, 0.18)
    return jnp.clip(values, -limit, limit).astype(held_as)


def setup_inputs(seed: int = 0) -> dict:
    streams_of = jax.random.split(jax.random.key(seed), 10)
    tokens = bell_draw(streams_of[0], (TOKENS, D), 1.0, 6.0, ((0, 32),))
    first_values = bell_draw(streams_of[1], (TOKENS, VH * HD), 1.0, 6.0, ((0, 32),))
    out_grad = bell_draw(streams_of[2], (TOKENS, D), 1.0, 6.0, ((0, 32),))
    lengths = draw_lengths(jax.random.fold_in(streams_of[9], 71), 0)
    in_proj = bell_draw(streams_of[4], (D, QKV), D ** -0.5, 0.21875, ((0, 32),))
    out_proj = bell_draw(streams_of[5], (D, D), (D // 16) ** -0.5, 0.875, ((0, 32),))
    up_proj = bell_draw(streams_of[6], (D, FF), D ** -0.5, 0.21875, ((0, 32),))
    down_proj = bell_draw(streams_of[7], (FF, D), FF ** -0.5, 0.109375, ((0, 32),))
    vectors = draw_vectors(jax.random.fold_in(streams_of[9], 71), 0)
    return dict(tokens=tokens, first_values=first_values, out_grad=out_grad, lengths=lengths, in_proj=in_proj, out_proj=out_proj, up_proj=up_proj, down_proj=down_proj, vectors=vectors)


EPS = 1e-05
NEG = -1000000000.0
HIGH = lax.Precision.HIGHEST

@jax.custom_vjp
def low(v):
    return lax.optimization_barrier(v.astype(jnp.bfloat16)).astype(jnp.float32)

@jax.custom_vjp
def low_back(v):
    return v

def low_keep(v):
    return (low(v), None)

def low_pass(kept, grad):
    return (grad,)

def back_keep(v):
    return (v, None)

def back_low(kept, grad):
    return (low(grad),)
low.defvjp(low_keep, low_pass)
low_back.defvjp(back_keep, back_low)

def layer_norm(values, scale_row, shift_row):
    centred = values - lax.optimization_barrier(jnp.mean(values, axis=-1, keepdims=True))
    spread = lax.optimization_barrier(jnp.mean(centred * centred, axis=-1, keepdims=True))
    return centred * lax.rsqrt(spread + EPS) * scale_row + shift_row

def allowed_pairs(doc_lengths, row_count):
    places = jnp.arange(row_count, dtype=jnp.int32)
    bounds = jnp.cumsum(doc_lengths).astype(jnp.int32)
    segment = lax.optimization_barrier(jnp.sum((places[:, None] >= bounds[None, :]).astype(jnp.int32), axis=1))
    return (segment[:, None] == segment[None, :]) & (places[:, None] >= places[None, :])

def layer(tokens_f, values_first, params, allowed):
    in_proj, out_proj, up_proj, down_proj, vectors = params
    row_count = tokens_f.shape[0]
    normed = low(layer_norm(tokens_f, vectors[0], vectors[1]))
    projected = jnp.dot(normed, in_proj, precision=HIGH)
    queries = low(low_back(projected[:, :D] + vectors[2]))
    key_rows = low(low_back(projected[:, D:2 * D]))
    fresh = low(low_back(projected[:, 2 * D:]))
    value_rows = jnp.concatenate([fresh, values_first], axis=1)
    scores = jnp.einsum('qhd,khd->hqk', queries.reshape(row_count, H, HD), key_rows.reshape(row_count, H, HD), precision=HIGH) * HD ** (-0.5)
    scores = low_back(jnp.where(allowed[None], scores, NEG))
    attention = low(jax.nn.softmax(scores, axis=-1))
    context = jnp.einsum('hqk,khd->qhd', attention, value_rows.reshape(row_count, H, HD), precision=HIGH).reshape(row_count, D)
    context = low(low_back(context))
    branch = low_back(jnp.dot(context, out_proj, precision=HIGH) + vectors[3])
    middle = tokens_f + branch
    normed_two = low(layer_norm(middle, vectors[4], vectors[5]))
    hidden = low_back(jnp.dot(normed_two, up_proj, precision=HIGH) + vectors[7:].reshape(-1))
    active = low(jax.nn.gelu(hidden, approximate=True))
    return middle + jnp.dot(active, down_proj, precision=HIGH) + vectors[6]

def reference(tokens, first_values, out_grad, lengths, in_proj, out_proj, up_proj, down_proj, vectors):
    params = (in_proj.astype(jnp.float32), out_proj.astype(jnp.float32), up_proj.astype(jnp.float32), down_proj.astype(jnp.float32), vectors.astype(jnp.float32))
    devices = N_DP * N_FSDP
    stacked = (tokens.reshape(devices, TOK_DEV, D), first_values.reshape(devices, TOK_DEV, VH * HD), out_grad.reshape(devices, TOK_DEV, D), lengths)

    def scan_step(totals, entry_arrays):
        block_tokens, block_values, block_grad, doc_lengths = entry_arrays
        allowed = allowed_pairs(doc_lengths, TOK_DEV)

        def forward(tokens_f, values_first, weights_all):
            return layer(tokens_f, values_first, weights_all, allowed)
        result, pullback = jax.vjp(forward, block_tokens.astype(jnp.float32), block_values.astype(jnp.float32), params)
        token_grad, value_grad, param_grads = pullback(block_grad.astype(jnp.float32))
        totals = jax.tree.map(jnp.add, totals, param_grads)
        return (totals, (result, token_grad, value_grad))
    initial = tuple((jnp.zeros_like(entry) for entry in params))
    totals, outputs = lax.scan(scan_step, initial, stacked)
    results, token_grads, value_grads = outputs
    return (results.reshape(TOKENS, D), token_grads.reshape(TOKENS, D), value_grads.reshape(TOKENS, VH * HD), totals[0], totals[1], totals[2], totals[3], totals[4])
```

```python
import functools

import jax
import jax.numpy as jnp
import numpy as np
from jax import lax
from jax.experimental import pallas as pl
from jax.experimental.pallas import tpu as pltpu
from jax.sharding import PartitionSpec as P

H = 12
HD = 64
EPS = 1e-05
NEG = -1000000000.0
LANES = 128
AXES = ("dp", "fsdp")
BF = jnp.bfloat16
F32 = jnp.float32
VMEM_LIMIT = 56 * 1024 * 1024
GELU_C = 0.7978845608028654
GELU_A = 0.044715


def dot(a, b):
    return lax.dot_general(a, b, (((1,), (0,)), ((), ())), preferred_element_type=F32)


def dot_rt(a, b):
    return lax.dot_general(a, b, (((1,), (1,)), ((), ())), preferred_element_type=F32)


def dot_lt(a, b):
    return lax.dot_general(a, b, (((0,), (0,)), ((), ())), preferred_element_type=F32)


def params(grid_rank=1):
    return pltpu.CompilerParams(
        vmem_limit_bytes=VMEM_LIMIT, dimension_semantics=("arbitrary",) * grid_rank
    )


def cost(flops, nbytes, trans=0):
    return pl.CostEstimate(flops=int(flops), bytes_accessed=int(nbytes), transcendentals=int(trans))


def norm_parts(values):
    centred = values - jnp.mean(values, axis=-1, keepdims=True)
    spread = jnp.mean(centred * centred, axis=-1, keepdims=True)
    rs = lax.rsqrt(spread + EPS)
    return centred * rs, rs


def norm_back(normed, rs, gain, grad):
    scaled = grad * gain
    m1 = jnp.mean(scaled, axis=-1, keepdims=True)
    m2 = jnp.mean(scaled * normed, axis=-1, keepdims=True)
    return rs * (scaled - m1 - normed * m2)


def in_kernel(x_ref, fv_ref, w_ref, a1_ref, qkv_ref, vec_ref):
    width = x_ref.shape[1]
    cols = w_ref.shape[1] - LANES

    @pl.when(pl.program_id(0) == 0)
    def _():
        turned = jnp.transpose(w_ref[:, cols:].astype(F32))
        vec_ref[...] = turned[: vec_ref.shape[0]]

    normed, _ = norm_parts(x_ref[...].astype(F32))
    a1 = (normed * vec_ref[0:1, :] + vec_ref[1:2, :]).astype(BF)
    a1_ref[...] = a1
    proj = dot(a1, w_ref[:, :cols])
    queries = (proj[:, :width] + vec_ref[2:3, :]).astype(BF)
    qkv_ref[:, :width] = queries * jnp.asarray(HD**-0.5, BF)
    qkv_ref[:, width:cols] = proj[:, width:].astype(BF)
    qkv_ref[:, cols:] = fv_ref[...]


def in_forward(tokens, first_values, w_in):
    rows, width = tokens.shape
    half = first_values.shape[1]
    cols = w_in.shape[1] - LANES
    block = 256
    return pl.pallas_call(
        in_kernel,
        grid=(rows // block,),
        in_specs=[
            pl.BlockSpec((block, width), lambda i: (i, 0)),
            pl.BlockSpec((block, half), lambda i: (i, 0)),
            pl.BlockSpec(w_in.shape, lambda i: (0, 0)),
        ],
        out_specs=[
            pl.BlockSpec((block, width), lambda i: (i, 0)),
            pl.BlockSpec((block, cols + half), lambda i: (i, 0)),
            pl.BlockSpec((16, width), lambda i: (0, 0)),
        ],
        out_shape=[
            jax.ShapeDtypeStruct((rows, width), BF),
            jax.ShapeDtypeStruct((rows, cols + half), BF),
            jax.ShapeDtypeStruct((16, width), F32),
        ],
        compiler_params=params(),
        cost_estimate=cost(2 * rows * width * cols, 12e6),
        name="in_forward",
    )(tokens, first_values, w_in)


def lanes_of(shape):
    return lax.broadcasted_iota(jnp.int32, shape, 1)


def own_lanes(e, shape):
    lane = lanes_of(shape)
    return (lane < HD) if e == 0 else (lane >= HD)


def spare(e):
    return HD if e == 0 else 0


def split3(values):
    hi = values.astype(BF).astype(F32)
    rest = values - hi
    mid = rest.astype(BF).astype(F32)
    return hi, mid, rest - mid


def attn_fwd_kernel(bound_ref, q_ref, k_ref, v_ref, ctx_ref, qa_ref):
    rows = q_ref.shape[0]
    block = 256
    bound = bound_ref[0, 0]
    shape = (block, LANES)
    lane = lanes_of(shape)
    place = lax.broadcasted_iota(jnp.int32, (rows, LANES), 0)
    all_lane = lanes_of((rows, LANES))
    k_all = k_ref[...]
    values = jnp.concatenate([v_ref[...], jnp.ones((rows, LANES), BF)], axis=1)
    tri = lax.broadcasted_iota(jnp.int32, (block, block), 0) >= lax.broadcasted_iota(
        jnp.int32, (block, block), 1
    )
    ctxs = [[None, None] for _ in range(rows // block)]
    for e in range(2):
        sp = spare(e)
        k_aux = jnp.where((all_lane == sp) & (place < bound), 1.0, 0.0).astype(BF)
        k_aug = jnp.where(own_lanes(e, (rows, LANES)), k_all, k_aux)
        for j in range(rows // block):
            lo, hi = j * block, (j + 1) * block
            seg = lax.broadcasted_iota(jnp.int32, shape, 0) + lo >= bound
            q_aux = jnp.where((lane == sp) & seg, NEG, 0.0)
            own = own_lanes(e, shape)
            q_aug = jnp.where(own, q_ref[lo:hi, :].astype(F32), q_aux)
            s = dot_rt(q_aug.astype(BF), k_aug[:hi, :])
            s_diag = jnp.where(tri, s[:, lo:], NEG)
            s = s_diag if j == 0 else jnp.concatenate([s[:, :lo], s_diag], axis=1)
            peak = jnp.max(s, axis=-1, keepdims=True)
            p = jnp.exp(s - peak).astype(BF)
            o = dot(p, values[:hi, :])
            total = o[:, LANES:]
            ctxs[j][e] = o[:, :LANES] / total
            l_hi, l_mid, l_lo = split3(-(peak + jnp.log(total)))
            q_aug = jnp.where(
                lane == sp + 1,
                l_hi,
                jnp.where(lane == sp + 2, l_mid, jnp.where(lane == sp + 3, l_lo, q_aug)),
            )
            qa_ref[lo:hi, e * LANES : (e + 1) * LANES] = q_aug.astype(BF)
    for j in range(rows // block):
        ctx_ref[j * block : (j + 1) * block, :] = jnp.where(
            lane < HD, ctxs[j][0], ctxs[j][1]
        ).astype(BF)


def attn_forward(lengths, qkv, width):
    rows = qkv.shape[0]
    pairs = width // LANES
    slab = lambda off: pl.BlockSpec((rows, LANES), lambda j, off=off: (0, off + j))
    return pl.pallas_call(
        attn_fwd_kernel,
        grid=(pairs,),
        in_specs=[
            pl.BlockSpec(memory_space=pltpu.SMEM),
            slab(0),
            slab(pairs),
            slab(2 * pairs),
        ],
        out_specs=[slab(0), pl.BlockSpec((rows, 2 * LANES), lambda j: (0, j))],
        out_shape=[
            jax.ShapeDtypeStruct((rows, width), BF),
            jax.ShapeDtypeStruct((rows, 2 * width), BF),
        ],
        compiler_params=params(),
        cost_estimate=cost(2 * 2 * rows * rows * 256 * H * 0.63, 9e6, rows * rows * H),
        name="attn_forward",
    )(lengths, qkv, qkv, qkv)


def attn_bwd_kernel(
    bound_ref, qa_ref, k_ref, v_ref, ctx_ref, do_ref, dq_ref, dk_ref, dv_ref, fv_ref, dk_acc, dv_acc
):
    rows = k_ref.shape[0]
    block = 256
    bound = bound_ref[0, 0]
    full = (rows, LANES)
    lane = lanes_of(full)
    place = lax.broadcasted_iota(jnp.int32, full, 0)
    k_all = k_ref[...].astype(F32)
    v_all = v_ref[...].astype(F32)
    do_all = do_ref[...].astype(F32)
    prod = do_all * ctx_ref[...].astype(F32)
    tri = lax.broadcasted_iota(jnp.int32, (block, block), 0) <= lax.broadcasted_iota(
        jnp.int32, (block, block), 1
    )
    dqs = [[None, None] for _ in range(rows // block)]
    for e in range(2):
        sp = spare(e)
        own = own_lanes(e, full)
        three = (lane >= sp + 1) & (lane <= sp + 3)
        k_aux = jnp.where(three | ((lane == sp) & (place < bound)), 1.0, 0.0)
        k_aug = jnp.where(own, k_all, k_aux).astype(BF)
        v_aug = jnp.where(own, v_all, jnp.where(three, 1.0, 0.0)).astype(BF)
        delta = jnp.sum(jnp.where(own, prod, 0.0), axis=-1, keepdims=True)
        d_hi, d_mid, d_lo = split3(-delta)
        do_aug = jnp.where(
            own,
            do_all,
            jnp.where(
                lane == sp + 1,
                d_hi,
                jnp.where(lane == sp + 2, d_mid, jnp.where(lane == sp + 3, d_lo, 0.0)),
            ),
        ).astype(BF)
        qa = qa_ref[:, e * LANES : (e + 1) * LANES]
        for j in reversed(range(rows // block)):
            lo, hi = j * block, (j + 1) * block
            qa_j = qa[lo:hi, :]
            do_j = do_aug[lo:hi, :]
            s = dot_rt(k_aug[:hi, :], qa_j)
            s_diag = jnp.where(tri, s[lo:, :], NEG)
            s = s_diag if j == 0 else jnp.concatenate([s[:lo, :], s_diag], axis=0)
            p = jnp.exp(s)
            ds = (p * dot_rt(v_aug[:hi, :], do_j)).astype(BF)
            dv_j = dot(p.astype(BF), do_j)
            dk_j = dot(ds, qa_j)
            if j == rows // block - 1:
                dv_acc[e] = dv_j
                dk_acc[e] = dk_j
            else:
                dv_acc[e, :hi, :] += dv_j
                dk_acc[e, :hi, :] += dk_j
            dqs[j][e] = dot_lt(ds, k_aug[:hi, :])
    for j in range(rows // block):
        sel = lanes_of((block, LANES)) < HD
        dq_ref[j * block : (j + 1) * block, :] = (
            jnp.where(sel, dqs[j][0], dqs[j][1]) * HD**-0.5
        ).astype(BF)
    dk_ref[...] = jnp.where(lane < HD, dk_acc[0], dk_acc[1]).astype(BF)
    dv = jnp.where(lane < HD, dv_acc[0], dv_acc[1])
    fresh = pl.num_programs(0) // 2

    @pl.when(pl.program_id(0) < fresh)
    def _():
        dv_ref[...] = dv.astype(BF)

    @pl.when(pl.program_id(0) >= fresh)
    def _():
        fv_ref[...] = dv


def attn_backward(lengths, qa, qkv, ctx, dctx):
    rows, width = ctx.shape
    pairs = width // LANES
    fresh = pairs // 2
    slab = lambda off: pl.BlockSpec((rows, LANES), lambda j, off=off: (0, off + j))
    return pl.pallas_call(
        attn_bwd_kernel,
        grid=(pairs,),
        in_specs=[
            pl.BlockSpec(memory_space=pltpu.SMEM),
            pl.BlockSpec((rows, 2 * LANES), lambda j: (0, j)),
            slab(pairs),
            slab(2 * pairs),
            slab(0),
            slab(0),
        ],
        out_specs=[
            slab(0),
            slab(0),
            pl.BlockSpec((rows, LANES), lambda j: (0, jnp.minimum(j, fresh - 1))),
            pl.BlockSpec((rows, LANES), lambda j: (0, jnp.maximum(j - fresh, 0))),
        ],
        out_shape=[
            jax.ShapeDtypeStruct((rows, width), BF),
            jax.ShapeDtypeStruct((rows, width), BF),
            jax.ShapeDtypeStruct((rows, width // 2), BF),
            jax.ShapeDtypeStruct((rows, width // 2), F32),
        ],
        scratch_shapes=[
            pltpu.VMEM((2, rows, LANES), F32),
            pltpu.VMEM((2, rows, LANES), F32),
        ],
        compiler_params=params(),
        cost_estimate=cost(5 * 2 * rows * rows * 256 * H * 0.63, 15e6, rows * rows * H),
        name="attn_backward",
    )(lengths, qa, qkv, qkv, ctx, dctx)


def ffn_kernel(ctx_ref, x_ref, wo_ref, wu_ref, vec_ref, mid_ref, a2_ref, act_ref, gd_ref):
    width = x_ref.shape[1]
    branch = dot(ctx_ref[...], wo_ref[...]) + vec_ref[3:4, :]
    mid = x_ref[...].astype(F32) + branch
    mid_ref[...] = mid
    normed, _ = norm_parts(mid)
    a2 = (normed * vec_ref[4:5, :] + vec_ref[5:6, :]).astype(BF)
    a2_ref[...] = a2
    for g in range(wu_ref.shape[1] // width):
        part = slice(g * width, (g + 1) * width)
        u = dot(a2, wu_ref[:, part]) + vec_ref[7 + g : 8 + g, :]
        u2 = u * u
        t = jnp.tanh(u * (GELU_C + (GELU_C * GELU_A) * u2))
        act = u * (0.5 + 0.5 * t)
        act_ref[:, part] = act.astype(BF)
        slope = (0.5 + 0.5 * t) + act * (1.0 - t) * (GELU_C + (3.0 * GELU_C * GELU_A) * u2)
        gd_ref[:, part] = slope.astype(BF)


def ffn_forward(ctx, tokens, w_out, w_up, vec):
    rows, width = tokens.shape
    hidden = w_up.shape[1]
    block = 256
    by_rows = lambda n: pl.BlockSpec((block, n), lambda i: (i, 0))
    whole = lambda a: pl.BlockSpec(a.shape, lambda i: (0, 0))
    return pl.pallas_call(
        ffn_kernel,
        grid=(rows // block,),
        in_specs=[by_rows(width), by_rows(width), whole(w_out), whole(w_up), whole(vec)],
        out_specs=[by_rows(width), by_rows(width), by_rows(hidden), by_rows(hidden)],
        out_shape=[
            jax.ShapeDtypeStruct((rows, width), F32),
            jax.ShapeDtypeStruct((rows, width), BF),
            jax.ShapeDtypeStruct((rows, hidden), BF),
            jax.ShapeDtypeStruct((rows, hidden), BF),
        ],
        compiler_params=params(),
        cost_estimate=cost(2 * rows * width * (width + hidden), 28e6, rows * hidden),
        name="ffn_forward",
    )(ctx, tokens, w_out, w_up, vec)


def out_kernel(act_ref, mid_ref, wd_ref, vec_ref, out_ref):
    out_ref[...] = mid_ref[...] + dot(act_ref[...], wd_ref[...]) + vec_ref[6:7, :]


def out_forward(act, mid, w_down, vec):
    rows, width = mid.shape
    hidden = act.shape[1]
    block = 256
    by_rows = lambda n: pl.BlockSpec((block, n), lambda i: (i, 0))
    whole = lambda a: pl.BlockSpec(a.shape, lambda i: (0, 0))
    return pl.pallas_call(
        out_kernel,
        grid=(rows // block,),
        in_specs=[by_rows(hidden), by_rows(width), whole(w_down), whole(vec)],
        out_specs=by_rows(width),
        out_shape=jax.ShapeDtypeStruct((rows, width), F32),
        compiler_params=params(),
        cost_estimate=cost(2 * rows * width * hidden, 18e6),
        name="out_forward",
    )(act, mid, w_down, vec)


def store_units(table_ref, result, keep_ref, send_ref, units, first, core_bit, put):
    half = keep_ref.shape[0]
    size = result.shape[0] // units
    for mine in range(2):

        @pl.when(table_ref[half * 2] == mine)
        def _(mine=mine):
            for i in range(units):
                d = first + i
                place = table_ref[d]
                rows = result[i * size : (i + 1) * size, :].astype(BF)
                if ((d >> core_bit) & 1) == mine:
                    put(keep_ref, place, rows)
                else:
                    put(send_ref, place - half, rows)


def put_rows(ref, place, rows):
    ref[place] = rows


def down_grad_kernel(table_ref, act_ref, dy_ref, keep_ref, send_ref, *, core_bit):
    half, size, _ = keep_ref.shape
    units = act_ref.shape[1] // size
    result = dot_lt(act_ref[...], dy_ref[...])
    g = pl.program_id(0)
    mine = table_ref[2 * half]
    for i in range(units):
        d = g * units + i
        place = table_ref[d]
        rows = result[i * size : (i + 1) * size, :].astype(BF)
        core = lax.rem(lax.shift_right_logical(d, core_bit), 2)

        @pl.when(core == mine)
        def _():
            keep_ref[place] = rows

        @pl.when(core != mine)
        def _():
            send_ref[place - half] = rows


def down_grad(table, act, dy, n, core_bit):
    rows, hidden = act.shape
    width = dy.shape[1]
    unit = hidden // n
    block = 384
    whole = pl.BlockSpec((n // 2, unit, width), lambda g: (0, 0, 0))
    shape = jax.ShapeDtypeStruct((n // 2, unit, width), BF)
    return pl.pallas_call(
        functools.partial(down_grad_kernel, core_bit=core_bit),
        grid=(hidden // block,),
        in_specs=[
            pl.BlockSpec(memory_space=pltpu.SMEM),
            pl.BlockSpec((rows, block), lambda g: (0, g)),
            pl.BlockSpec((rows, width), lambda g: (0, 0)),
        ],
        out_specs=[whole, whole],
        out_shape=[shape, shape],
        compiler_params=params(),
        cost_estimate=cost(2 * rows * width * hidden, 13e6),
        name="down_grad",
    )(table, act, dy)


def up_grad_kernel(
    table_ref, dy_ref, wd_ref, gd_ref, a2_ref, du_ref, sums_ref, keep_ref, send_ref, a2t, *, core_bit
):
    @pl.when(pl.program_id(0) == 0)
    def _():
        a2t[...] = jnp.transpose(a2_ref[...])

    du = (dot_rt(dy_ref[...], wd_ref[...]) * gd_ref[...].astype(F32)).astype(BF)
    du_ref[...] = du
    sums_ref[...] = jnp.sum(du.astype(F32), axis=0, keepdims=True)
    result = dot(a2t[...], du)
    n = keep_ref.shape[0] * 2
    store_units(table_ref, result, keep_ref, send_ref, n, 0, core_bit, put_rows)


def up_grad(table, dy, w_down, gd, a2, n, core_bit):
    rows, width = dy.shape
    hidden = w_down.shape[0]
    unit = width // n
    block = 512
    part = pl.BlockSpec((n // 2, unit, block), lambda g: (0, 0, g))
    shape = jax.ShapeDtypeStruct((n // 2, unit, hidden), BF)
    whole = lambda a: pl.BlockSpec(a.shape, lambda g: (0, 0))
    return pl.pallas_call(
        functools.partial(up_grad_kernel, core_bit=core_bit),
        grid=(hidden // block,),
        in_specs=[
            pl.BlockSpec(memory_space=pltpu.SMEM),
            whole(dy),
            pl.BlockSpec((block, width), lambda g: (g, 0)),
            pl.BlockSpec((rows, block), lambda g: (0, g)),
            whole(a2),
        ],
        out_specs=[
            pl.BlockSpec((rows, block), lambda g: (0, g)),
            pl.BlockSpec((1, block), lambda g: (0, g)),
            part,
            part,
        ],
        out_shape=[
            jax.ShapeDtypeStruct((rows, hidden), BF),
            jax.ShapeDtypeStruct((1, hidden), F32),
            shape,
            shape,
        ],
        scratch_shapes=[pltpu.VMEM((width, rows), BF)],
        compiler_params=params(),
        cost_estimate=cost(4 * rows * width * hidden, 25e6),
        name="up_grad",
    )(table, dy, w_down, gd, a2)


def mid_back_kernel(
    table_ref,
    du_ref,
    wu_ref,
    mid_ref,
    dy_ref,
    ctx_ref,
    wo_ref,
    vec_ref,
    dmid_ref,
    dctx_ref,
    sums_ref,
    keep_ref,
    send_ref,
    acc,
    *,
    core_bit,
):
    i = pl.program_id(0)
    da2 = dot_rt(du_ref[...], wu_ref[...])
    normed, rs = norm_parts(mid_ref[...])
    dy = dy_ref[...].astype(F32)
    dmid = norm_back(normed, rs, vec_ref[4:5, :], da2) + dy
    dmid_ref[...] = dmid
    dbr = dmid.astype(BF)
    dctx_ref[...] = dot_rt(dbr, wo_ref[...]).astype(BF)
    total = lambda v: jnp.sum(v, axis=0, keepdims=True)
    sums = jnp.concatenate(
        [
            total(dbr.astype(F32)),
            total(da2 * normed),
            total(da2),
            total(dy),
            jnp.zeros((4, dy.shape[1]), F32),
        ],
        axis=0,
    )
    part = dot_lt(ctx_ref[...], dbr)

    @pl.when(i == 0)
    def _():
        sums_ref[...] = sums
        acc[...] = part

    @pl.when(i > 0)
    def _():
        sums_ref[...] += sums
        acc[...] += part

    @pl.when(i == pl.num_programs(0) - 1)
    def _():
        n = keep_ref.shape[0] * 2
        store_units(table_ref, acc, keep_ref, send_ref, n, 0, core_bit, put_rows)


def mid_back(table, du, w_up, mid, dy, ctx, w_out, vec, n, core_bit):
    rows, width = dy.shape
    hidden = du.shape[1]
    unit = width // n
    block = 256
    by_rows = lambda m: pl.BlockSpec((block, m), lambda i: (i, 0))
    whole = lambda a: pl.BlockSpec(a.shape, lambda i: (0, 0))
    units = pl.BlockSpec((n // 2, unit, width), lambda i: (0, 0, 0))
    shape = jax.ShapeDtypeStruct((n // 2, unit, width), BF)
    return pl.pallas_call(
        functools.partial(mid_back_kernel, core_bit=core_bit),
        grid=(rows // block,),
        in_specs=[
            pl.BlockSpec(memory_space=pltpu.SMEM),
            by_rows(hidden),
            whole(w_up),
            by_rows(width),
            by_rows(width),
            by_rows(width),
            whole(w_out),
            whole(vec),
        ],
        out_specs=[
            by_rows(width),
            by_rows(width),
            pl.BlockSpec((8, width), lambda i: (0, 0)),
            units,
            units,
        ],
        out_shape=[
            jax.ShapeDtypeStruct((rows, width), F32),
            jax.ShapeDtypeStruct((rows, width), BF),
            jax.ShapeDtypeStruct((8, width), F32),
            shape,
            shape,
        ],
        scratch_shapes=[pltpu.VMEM((width, width), F32)],
        compiler_params=params(),
        cost_estimate=cost(2 * rows * width * (hidden + 2 * width), 26e6),
        name="mid_back",
    )(table, du, w_up, mid, dy, ctx, w_out, vec)


def token_grad_kernel(
    x_ref, dq_ref, dk_ref, dv_ref, w_ref, dmid_ref, vec_ref, grad_ref, sums_ref
):
    width = x_ref.shape[1]
    i = pl.program_id(0)
    dq = dq_ref[...]
    dproj = jnp.concatenate([dq, dk_ref[...], dv_ref[...]], axis=1)
    da1 = dot_rt(dproj, w_ref[:, : dproj.shape[1]])
    normed, rs = norm_parts(x_ref[...].astype(F32))
    grad_ref[...] = dmid_ref[...] + norm_back(normed, rs, vec_ref[0:1, :], da1)
    total = lambda v: jnp.sum(v, axis=0, keepdims=True)
    sums = jnp.concatenate(
        [total(da1 * normed), total(da1), total(dq.astype(F32)), jnp.zeros((5, width), F32)], axis=0
    )

    @pl.when(i == 0)
    def _():
        sums_ref[...] = sums

    @pl.when(i > 0)
    def _():
        sums_ref[...] += sums


def token_grad(tokens, dq, dk, dfresh, w_in, dmid, vec):
    rows, width = tokens.shape
    half = dfresh.shape[1]
    block = 256
    by_rows = lambda m: pl.BlockSpec((block, m), lambda i: (i, 0))
    whole = lambda a: pl.BlockSpec(a.shape, lambda i: (0, 0))
    return pl.pallas_call(
        token_grad_kernel,
        grid=(rows // block,),
        in_specs=[
            by_rows(width),
            by_rows(width),
            by_rows(width),
            by_rows(half),
            whole(w_in),
            by_rows(width),
            whole(vec),
        ],
        out_specs=[by_rows(width), pl.BlockSpec((8, width), lambda i: (0, 0))],
        out_shape=[
            jax.ShapeDtypeStruct((rows, width), F32),
            jax.ShapeDtypeStruct((8, width), F32),
        ],
        compiler_params=params(),
        cost_estimate=cost(2 * rows * width * (2 * width + half), 17e6),
        name="token_grad",
    )(tokens, dq, dk, dfresh, w_in, dmid, vec)


def in_grad_kernel(
    table_ref, a1_ref, dq_ref, dk_ref, dv_ref, s1_ref, s2_ref, c1_ref, keep_ref, send_ref, *, core_bit
):
    width = a1_ref.shape[1]
    n = keep_ref.shape[0] * 2
    a1t = jnp.transpose(a1_ref[...])
    start = 0
    for ref in (dq_ref, dk_ref, dv_ref):
        for c in range(0, ref.shape[1], 384):
            result = dot(a1t, ref[:, c : c + 384])

            def put(out, place, rows, at=start):
                out[place, :, at : at + rows.shape[1]] = rows

            store_units(table_ref, result, keep_ref, send_ref, n, 0, core_bit, put)
            start += 384
    stacked = jnp.concatenate(
        [s1_ref[0:3, :], s2_ref[0:4, :]]
        + [c1_ref[0:1, g * width : (g + 1) * width] for g in range(c1_ref.shape[1] // width)]
        + [jnp.zeros((LANES - 7 - c1_ref.shape[1] // width, width), F32)],
        axis=0,
    )

    def put_last(out, place, rows):
        out[place, :, start:] = rows

    store_units(
        table_ref, jnp.transpose(stacked), keep_ref, send_ref, n, 0, core_bit, put_last
    )


def in_grad(table, a1, dq, dk, dfresh, s1, s2, c1, n, core_bit):
    rows, width = a1.shape
    cols = 2 * width + dfresh.shape[1]
    shape = jax.ShapeDtypeStruct((n // 2, width // n, cols + LANES), BF)
    vmem = pl.BlockSpec(memory_space=pltpu.VMEM)
    return pl.pallas_call(
        functools.partial(in_grad_kernel, core_bit=core_bit),
        in_specs=[pl.BlockSpec(memory_space=pltpu.SMEM)] + [vmem] * 7,
        out_specs=[vmem, vmem],
        out_shape=[shape, shape],
        compiler_params=pltpu.CompilerParams(vmem_limit_bytes=VMEM_LIMIT),
        cost_estimate=cost(2 * rows * width * cols, 12e6),
        name="in_grad",
    )(table, a1, dq, dk, dfresh, s1, s2, c1)


def stages_of(n_dp, n_fsdp):
    fsdp_bits = n_fsdp.bit_length() - 1
    dp_bits = n_dp.bit_length() - 1
    low = list(range(fsdp_bits // 2))[::-1]
    high = list(range(fsdp_bits // 2, fsdp_bits))[::-1]
    z_bits = list(range(fsdp_bits + 1, fsdp_bits + dp_bits))[::-1]
    core = fsdp_bits
    return core, ([core] + high + low + z_bits, [core] + low + high + z_bits)


def place_table(n_dp, n_fsdp):
    core, orders = stages_of(n_dp, n_fsdp)
    n = n_dp * n_fsdp
    table = np.zeros((n, n + 1), np.int32)
    for me in range(n):
        for d in range(n):
            order = orders[(d >> core) & 1]
            away = d ^ me
            place = 0
            for bit in order:
                place = place * 2 + ((away >> bit) & 1)
            table[me, d] = place
        table[me, n] = (me >> core) & 1
    return table


def swap(value, n_dp, n_fsdp, stage):
    core, orders = stages_of(n_dp, n_fsdp)
    pairs = [(i, i ^ (1 << orders[(i >> core) & 1][stage])) for i in range(n_dp * n_fsdp)]
    return lax.ppermute(value, AXES, pairs)


def reduce_units(keep, send, n_dp, n_fsdp):
    count = (n_dp * n_fsdp).bit_length() - 1
    for stage in range(count):
        got = swap(send, n_dp, n_fsdp, stage)
        total = keep.astype(F32) + got.astype(F32)
        if stage == count - 1:
            return total[0]
        half = total.shape[0] // 2
        keep = total[:half].astype(BF)
        send = total[half:].astype(BF)


def body(tokens, first_values, out_grad, lengths, in_proj, out_proj, up_proj, down_proj, vectors, *, n_dp, n_fsdp):
    n = n_dp * n_fsdp
    width = tokens.shape[1]
    hidden = up_proj.shape[1]
    vrows = vectors.shape[0]
    core_bit, _ = stages_of(n_dp, n_fsdp)
    me = lax.axis_index("dp") * n_fsdp + lax.axis_index("fsdp")
    table = lax.dynamic_slice(jnp.asarray(place_table(n_dp, n_fsdp)), (me, 0), (1, n + 1))[0]

    vec_t = jnp.pad(vectors.T, ((0, 0), (0, LANES - vrows)))
    gather = lambda a: lax.all_gather(a, AXES, axis=0, tiled=True)
    w_in = gather(jnp.concatenate([in_proj, vec_t], axis=1))
    w_out = gather(out_proj)
    w_up = gather(up_proj)
    w_down = gather(down_proj)

    a1, qkv, vec = in_forward(tokens, first_values, w_in)
    ctx, qa = attn_forward(lengths, qkv, width)
    mid, a2, act, gd = ffn_forward(ctx, tokens, w_out, w_up, vec)

    reduce = functools.partial(reduce_units, n_dp=n_dp, n_fsdp=n_fsdp)
    g_down = reduce(*down_grad(table, act, out_grad, n, core_bit))
    output = out_forward(act, mid, w_down, vec)
    du, dc1, keep, send = up_grad(table, out_grad, w_down, gd, a2, n, core_bit)
    g_up = reduce(keep, send)
    dmid, dctx, sums2, keep, send = mid_back(
        table, du, w_up, mid, out_grad, ctx, w_out, vec, n, core_bit
    )
    g_out = reduce(keep, send)
    dq, dk, dfresh, first_grad = attn_backward(lengths, qa, qkv, ctx, dctx)
    input_grad, sums1 = token_grad(tokens, dq, dk, dfresh, w_in, dmid, vec)
    g_in = reduce(*in_grad(table, a1, dq, dk, dfresh, sums1, sums2, dc1, n, core_bit))
    cols = in_proj.shape[1]
    g_vec = g_in[:, cols : cols + vrows].T
    return (output, input_grad, first_grad, g_in[:, :cols], g_out, g_up, g_down, g_vec)


def solution(mesh):
    rows = P(AXES, None)
    cols = P(None, AXES)
    return jax.shard_map(
        functools.partial(body, n_dp=mesh.shape["dp"], n_fsdp=mesh.shape["fsdp"]),
        mesh=mesh,
        in_specs=(rows,) * 8 + (cols,),
        out_specs=(rows,) * 7 + (cols,),
        check_vma=False,
    )
```

```python
import functools

import jax
import jax.numpy as jnp
import numpy as np
from jax import lax
from jax.experimental import pallas as pl
from jax.experimental.pallas import tpu as pltpu
from jax.sharding import PartitionSpec as P

H = 12
HD = 64
EPS = 1e-05
NEG = -1000000000.0
LANES = 128
AXES = ("dp", "fsdp")
BF = jnp.bfloat16
F32 = jnp.float32
VMEM_LIMIT = 56 * 1024 * 1024
GELU_C = 0.7978845608028654
GELU_A = 0.044715


def dot(a, b):
    return lax.dot_general(a, b, (((1,), (0,)), ((), ())), preferred_element_type=F32)


def dot_rt(a, b):
    return lax.dot_general(a, b, (((1,), (1,)), ((), ())), preferred_element_type=F32)


def dot_lt(a, b):
    return lax.dot_general(a, b, (((0,), (0,)), ((), ())), preferred_element_type=F32)


def params(grid_rank=1):
    return pltpu.CompilerParams(
        vmem_limit_bytes=VMEM_LIMIT, dimension_semantics=("arbitrary",) * grid_rank
    )


def cost(flops, nbytes, trans=0):
    return pl.CostEstimate(flops=int(flops), bytes_accessed=int(nbytes), transcendentals=int(trans))


def call(kernel, ins, in_specs, deps=(), **kw):
    count, extra = len(ins), len(deps)

    def run(*refs):
        kernel(*refs[:count], *refs[count + extra :])

    specs = list(in_specs) + [pl.BlockSpec(memory_space=pl.ANY)] * extra
    return pl.pallas_call(run, in_specs=specs, **kw)(*ins, *deps)


def norm_parts(values):
    centred = values - jnp.mean(values, axis=-1, keepdims=True)
    spread = jnp.mean(centred * centred, axis=-1, keepdims=True)
    rs = lax.rsqrt(spread + EPS)
    return centred * rs, rs


def norm_back(normed, rs, gain, grad):
    scaled = grad * gain
    m1 = jnp.mean(scaled, axis=-1, keepdims=True)
    m2 = jnp.mean(scaled * normed, axis=-1, keepdims=True)
    return rs * (scaled - m1 - normed * m2)


def assemble(table_ref, refs, places, whole_ref, absolute=False):
    n = whole_ref.shape[0]
    owners = 3 * n if absolute else n
    for ref, bases in zip(refs, places, strict=True):
        each = ref.shape[0] // len(bases)
        for b, base in enumerate(bases):
            for k in range(each):
                whole_ref[table_ref[owners + base + k]] = ref[b * each + k]


def flatten_units(units_ref, matrix_ref):
    size = units_ref.shape[1]
    for d in range(units_ref.shape[0]):
        matrix_ref[d * size : (d + 1) * size, :] = units_ref[d]


def const_spec(a):
    rank = len(a.shape)
    return pl.BlockSpec(a.shape, lambda *_: (0,) * rank)


def in_kernel(table_ref, x_ref, fv_ref, *refs, places):
    *parts, w_hbm, n1_ref, qkv_ref, vec_ref, units_ref, w_ref, sem = refs
    width = x_ref.shape[1]
    cols = w_ref.shape[1] - LANES
    copy = pltpu.make_async_copy(w_ref, w_hbm, sem)

    @pl.when(pl.program_id(0) == 0)
    def _():
        assemble(table_ref, parts, places, units_ref)
        flatten_units(units_ref, w_ref)
        copy.start()
        turned = jnp.transpose(w_ref[:, cols:].astype(F32))
        vec_ref[...] = turned[: vec_ref.shape[0]]

    normed, _ = norm_parts(x_ref[...].astype(F32))
    a1 = (normed * vec_ref[0:1, :] + vec_ref[1:2, :]).astype(BF)
    n1_ref[...] = normed.astype(BF)
    proj = dot(a1, w_ref[:, :cols])
    queries = (proj[:, :width] + vec_ref[2:3, :]).astype(BF)
    qkv_ref[:, :width] = queries * jnp.asarray(HD**-0.5, BF)
    qkv_ref[:, width:cols] = proj[:, width:].astype(BF)
    qkv_ref[:, cols:] = fv_ref[...]

    @pl.when(pl.program_id(0) == pl.num_programs(0) - 1)
    def _():
        copy.wait()


def in_forward(table, tokens, first_values, gathered, deps=()):
    parts, places = gathered
    rows, width = tokens.shape
    half = first_values.shape[1]
    _, size, wide = parts[0].shape
    n = width // size
    block = 256
    by_rows = lambda m: pl.BlockSpec((block, m), lambda i: (i, 0))
    const = lambda *shape: pl.BlockSpec(shape, lambda i: (0, 0))
    return call(
        functools.partial(in_kernel, places=places),
        (table, tokens, first_values, *parts),
        [pl.BlockSpec(memory_space=pltpu.SMEM), by_rows(width), by_rows(half)]
        + [const_spec(p) for p in parts],
        deps,
        grid=(rows // block,),
        out_specs=[
            pl.BlockSpec(memory_space=pl.ANY),
            by_rows(width),
            by_rows(wide - LANES + half),
            const(16, width),
        ],
        out_shape=[
            jax.ShapeDtypeStruct((width, wide), BF),
            jax.ShapeDtypeStruct((rows, width), BF),
            jax.ShapeDtypeStruct((rows, wide - LANES + half), BF),
            jax.ShapeDtypeStruct((16, width), F32),
        ],
        scratch_shapes=[
            pltpu.VMEM((n, size, wide), BF),
            pltpu.VMEM((width, wide), BF),
            pltpu.SemaphoreType.DMA(()),
        ],
        compiler_params=params(),
        cost_estimate=cost(2 * rows * width * wide, 16e6),
        name="in_forward",
    )


def lanes_of(shape):
    return lax.broadcasted_iota(jnp.int32, shape, 1)


def own_lanes(e, shape):
    lane = lanes_of(shape)
    return (lane < HD) if e == 0 else (lane >= HD)


def spare(e):
    return HD if e == 0 else 0


def split3(values):
    hi = values.astype(BF).astype(F32)
    rest = values - hi
    mid = rest.astype(BF).astype(F32)
    return hi, mid, rest - mid


def augmented(vectors, e, lane, seg, filled):
    aux = jnp.where((lane == spare(e)) & seg, filled, 0.0)
    return jnp.where(own_lanes(e, lane.shape), vectors, aux).astype(BF)


def causal(block):
    rows = lax.broadcasted_iota(jnp.int32, (block, block), 0)
    return rows <= lax.broadcasted_iota(jnp.int32, (block, block), 1)


def scores_of(keys, queries, tri, lo):
    s = dot_rt(keys, queries)
    diag = jnp.where(tri, s[lo:, :], NEG)
    return diag if lo == 0 else jnp.concatenate([s[:lo, :], diag], axis=0)


def attn_fwd_kernel(bound_ref, q_ref, k_ref, v_ref, ctx_ref, lse_ref):
    rows = q_ref.shape[0]
    block = 256
    bound = bound_ref[0, 0]
    shape = (rows, LANES)
    lane = lanes_of(shape)
    place = lax.broadcasted_iota(jnp.int32, shape, 0)
    k_all = k_ref[...].astype(F32)
    q_all = q_ref[...].astype(F32)
    values = jnp.concatenate([v_ref[...], jnp.ones(shape, BF)], axis=1)
    tri = causal(block)
    ctxs = [[None, None] for _ in range(rows // block)]
    k_augs = [augmented(k_all, e, lane, place < bound, 1.0) for e in range(2)]
    q_augs = [augmented(q_all, e, lane, place >= bound, NEG) for e in range(2)]
    chains = [(j, e) for j in range(rows // block) for e in range(2)]

    def scores(j, e):
        lo, hi = j * block, (j + 1) * block
        return scores_of(k_augs[e][:hi, :], q_augs[e][lo:hi, :], tri, lo)

    def weighted(j, e, p):
        o = dot_lt(p, values[: (j + 1) * block, :])
        ctxs[j][e] = o[:, :LANES] / o[:, LANES:]

    following = scores(*chains[0])
    waiting = None
    for i, (j, e) in enumerate(chains):
        s = following
        if i + 1 < len(chains):
            following = scores(*chains[i + 1])
        peak = jnp.max(s, axis=0, keepdims=True)
        p = jnp.exp(s - peak)
        lse = peak + jnp.log(jnp.sum(p, axis=0, keepdims=True))
        lse_ref[0, e : e + 1, j * block : (j + 1) * block] = lse
        if waiting is not None:
            weighted(*waiting)
        waiting = (j, e, p.astype(BF))
    weighted(*waiting)
    first = lanes_of((block, LANES)) < HD
    for j in range(rows // block):
        ctx_ref[j * block : (j + 1) * block, :] = jnp.where(first, *ctxs[j]).astype(BF)


def attn_forward(lengths, qkv, width, first, count, deps=()):
    rows = qkv.shape[0]
    pairs = width // LANES
    slab = lambda off: pl.BlockSpec((rows, LANES), lambda j, off=off: (0, off + j))
    return call(
        attn_fwd_kernel,
        (lengths, qkv, qkv, qkv),
        [pl.BlockSpec(memory_space=pltpu.SMEM), *(slab(first + c * pairs) for c in range(3))],
        deps,
        grid=(count,),
        out_specs=[slab(0), pl.BlockSpec((1, 8, rows), lambda j: (j, 0, 0))],
        out_shape=[
            jax.ShapeDtypeStruct((rows, count * LANES), BF),
            jax.ShapeDtypeStruct((count, 8, rows), F32),
        ],
        compiler_params=params(),
        cost_estimate=cost(2 * 2 * rows * rows * 256 * 2 * count * 0.63, 5e6, rows * rows * 2 * count),
        name="attn_forward",
    )


def attn_bwd_kernel(
    bound_ref, lse_ref, q_ref, k_ref, v_ref, ctx_ref, do_ref, dq_ref, dk_ref, dv_ref, dk_acc, dv_acc
):
    rows = k_ref.shape[0]
    block = 256
    bound = bound_ref[0, 0]
    full = (rows, LANES)
    lane = lanes_of(full)
    place = lax.broadcasted_iota(jnp.int32, full, 0)
    q_all = q_ref[...].astype(F32)
    k_all = k_ref[...].astype(F32)
    v_all = v_ref[...].astype(F32)
    do_all = do_ref[...].astype(F32)
    prod = do_all * ctx_ref[...].astype(F32)
    tri = causal(block)
    dqs = [[None, None] for _ in range(rows // block)]
    for e in range(2):
        sp = spare(e)
        own = own_lanes(e, full)
        three = (lane >= sp + 1) & (lane <= sp + 3)
        k_aug = augmented(k_all, e, lane, place < bound, 1.0)
        q_aug = augmented(q_all, e, lane, place >= bound, NEG)
        v_aug = jnp.where(own, v_all, jnp.where(three, 1.0, 0.0)).astype(BF)
        delta = jnp.sum(jnp.where(own, prod, 0.0), axis=-1, keepdims=True)
        d_hi, d_mid, d_lo = split3(-delta)
        do_aug = jnp.where(
            own,
            do_all,
            jnp.where(
                lane == sp + 1,
                d_hi,
                jnp.where(lane == sp + 2, d_mid, jnp.where(lane == sp + 3, d_lo, 0.0)),
            ),
        ).astype(BF)
        for j in reversed(range(rows // block)):
            lo, hi = j * block, (j + 1) * block
            q_j = q_aug[lo:hi, :]
            do_j = do_aug[lo:hi, :]
            p = jnp.exp(scores_of(k_aug[:hi, :], q_j, tri, lo) - lse_ref[0, e : e + 1, lo:hi])
            ds = (p * dot_rt(v_aug[:hi, :], do_j)).astype(BF)
            dv_j = dot(p.astype(BF), do_j)
            dk_j = dot(ds, q_j)
            if j == rows // block - 1:
                dv_acc[e] = dv_j
                dk_acc[e] = dk_j
            else:
                dv_acc[e, :hi, :] += dv_j
                dk_acc[e, :hi, :] += dk_j
            dqs[j][e] = dot_lt(ds, k_aug[:hi, :])
    first = lanes_of((block, LANES)) < HD
    for j in range(rows // block):
        dq_ref[j * block : (j + 1) * block, :] = (jnp.where(first, *dqs[j]) * HD**-0.5).astype(BF)
    dk_ref[...] = jnp.where(lane < HD, dk_acc[0], dk_acc[1]).astype(BF)
    dv_ref[...] = jnp.where(lane < HD, dv_acc[0], dv_acc[1]).astype(dv_ref.dtype)


def attn_backward(lengths, lse, qkv, ctx, dctx, first, count, dv_type, deps=()):
    rows, width = dctx.shape
    pairs = width // LANES
    slab = lambda off: pl.BlockSpec((rows, LANES), lambda j, off=off: (0, off + j))
    shape = lambda dtype: jax.ShapeDtypeStruct((rows, count * LANES), dtype)
    return call(
        attn_bwd_kernel,
        (lengths, lse, qkv, qkv, qkv, ctx, dctx),
        [
            pl.BlockSpec(memory_space=pltpu.SMEM),
            pl.BlockSpec((1, 8, rows), lambda j: (j, 0, 0)),
            slab(first),
            slab(pairs + first),
            slab(2 * pairs + first),
            slab(0),
            slab(first),
        ],
        deps,
        grid=(count,),
        out_specs=[slab(0)] * 3,
        out_shape=[shape(BF), shape(BF), shape(dv_type)],
        scratch_shapes=[
            pltpu.VMEM((2, rows, LANES), F32),
            pltpu.VMEM((2, rows, LANES), F32),
        ],
        compiler_params=params(),
        cost_estimate=cost(5 * 2 * rows * rows * 256 * 2 * count * 0.63, 15e6, rows * rows * 2 * count),
        name="attn_backward",
    )


def ffn_kernel(
    table_ref, ctx1_ref, ctx2_ref, x_ref, dy_ref, vec_ref, *refs, places, core_bit
):
    count = len(places)
    out_parts, up_parts = refs[:count], refs[count : 2 * count]
    (act_ref, gd_ref, mid_hbm, a2_hbm, wo_hbm, keep_hbm, send_hbm) = refs[
        2 * count : 2 * count + 7
    ]
    wo_units, wu_units, wo_ref, wu_ref, mid_ref, a2_ref, stage, once_sems, sems = refs[
        2 * count + 7 :
    ]
    g = pl.program_id(0)
    last = pl.num_programs(0) - 1
    rows, width = x_ref.shape
    chunk = act_ref.shape[1]
    n = wu_units.shape[0]
    block = 256
    once = (
        pltpu.make_async_copy(mid_ref, mid_hbm, once_sems.at[0]),
        pltpu.make_async_copy(a2_ref, a2_hbm, once_sems.at[1]),
        pltpu.make_async_copy(wo_ref, wo_hbm, once_sems.at[2]),
    )

    @pl.when(g == 0)
    def _():
        assemble(table_ref, out_parts, places, wo_units, True)
        flatten_units(wo_units, wo_ref)
        for i in range(rows // block):
            part = slice(i * block, (i + 1) * block)
            ctx = jnp.concatenate([ctx1_ref[part, :], ctx2_ref[part, :]], axis=1)
            branch = dot(ctx, wo_ref[...]) + vec_ref[3:4, :]
            mid = x_ref[part, :].astype(F32) + branch
            mid_ref[part, :] = mid
            normed, _ = norm_parts(mid)
            a2_ref[part, :] = (normed * vec_ref[4:5, :] + vec_ref[5:6, :]).astype(BF)
        for copy in once:
            copy.start()

    assemble(table_ref, up_parts, places, wu_units, True)
    flatten_units(wu_units, wu_ref)
    per_row = width // chunk
    row = vec_ref[pl.ds(7 + g // per_row, 1), :]
    bias = row[:, :chunk]
    for c in range(1, per_row):
        bias = jnp.where(g % per_row == c, row[:, c * chunk : (c + 1) * chunk], bias)
    for i in range(rows // block):
        part = slice(i * block, (i + 1) * block)
        u = dot(a2_ref[part, :], wu_ref[...]) + bias
        u2 = u * u
        t = jnp.tanh(u * (GELU_C + (GELU_C * GELU_A) * u2))
        half = 0.5 + 0.5 * t
        act = u * half
        act_ref[part, :] = act.astype(BF)
        slope = half + act * (1.0 - t) * (GELU_C + (3.0 * GELU_C * GELU_A) * u2)
        gd_ref[part, :] = slope.astype(BF)
    result = dot_lt(act_ref[...], dy_ref[...])
    units = stage.shape[1]
    size = chunk // units
    slot = lax.rem(g, 2)
    mine = table_ref[4 * n]
    sent = lambda at, i: pltpu.make_async_copy(stage.at[at, i], keep_hbm.at[0], sems.at[at, i])

    @pl.when(g >= 2)
    def _():
        for i in range(units):
            sent(slot, i).wait()

    for i in range(units):
        stage[slot, i] = result[i * size : (i + 1) * size, :].astype(BF)
        d = g * units + i
        place = table_ref[2 * n + d]
        core = lax.rem(lax.shift_right_logical(d, core_bit), 2)

        @pl.when(core == mine)
        def _(i=i, place=place):
            pltpu.make_async_copy(stage.at[slot, i], keep_hbm.at[place], sems.at[slot, i]).start()

        @pl.when(core != mine)
        def _(i=i, place=place):
            pltpu.make_async_copy(
                stage.at[slot, i], send_hbm.at[place - n // 2], sems.at[slot, i]
            ).start()

    @pl.when(g == last)
    def _():
        for copy in once:
            copy.wait()
        for i in range(units):
            sent(1 - slot, i).wait()
            sent(slot, i).wait()


def ffn_forward(table, ctx, tokens, dy, vec, gathered, core_bit, deps=()):
    parts, places = gathered
    rows, width = tokens.shape
    _, size, wide = parts[0].shape
    hidden = wide - width
    n = width // size
    chunk = hidden // 4
    unit = hidden // n
    anywhere = pl.BlockSpec(memory_space=pl.ANY)
    halves = jax.ShapeDtypeStruct((n // 2, unit, width), BF)
    return call(
        functools.partial(ffn_kernel, places=places, core_bit=core_bit),
        (table, *ctx, tokens, dy, vec, *parts, *parts),
        [pl.BlockSpec(memory_space=pltpu.SMEM)]
        + [
            pl.BlockSpec(a.shape, lambda g: (0, 0), pipeline_mode=pl.Buffered(1))
            for a in (*ctx, tokens, dy, vec)
        ]
        + [
            pl.BlockSpec(
                (p.shape[0], size, width), lambda g: (0, 0, 0), pipeline_mode=pl.Buffered(1)
            )
            for p in parts
        ]
        + [
            pl.BlockSpec((p.shape[0], size, chunk), lambda g: (0, 0, width // chunk + g))
            for p in parts
        ],
        deps,
        grid=(hidden // chunk,),
        out_specs=[pl.BlockSpec((rows, chunk), lambda g: (0, g))] * 2 + [anywhere] * 5,
        out_shape=[
            jax.ShapeDtypeStruct((rows, hidden), BF),
            jax.ShapeDtypeStruct((rows, hidden), BF),
            jax.ShapeDtypeStruct((rows, width), F32),
            jax.ShapeDtypeStruct((rows, width), BF),
            jax.ShapeDtypeStruct((width, width), BF),
            halves,
            halves,
        ],
        scratch_shapes=[
            pltpu.VMEM((n, size, width), BF),
            pltpu.VMEM((n, size, chunk), BF),
            pltpu.VMEM((width, width), BF),
            pltpu.VMEM((width, chunk), BF),
            pltpu.VMEM((rows, width), F32),
            pltpu.VMEM((rows, width), BF),
            pltpu.VMEM((2, n // 4, unit, width), BF),
            pltpu.SemaphoreType.DMA((3,)),
            pltpu.SemaphoreType.DMA((2, n // 4)),
        ],
        compiler_params=params(),
        cost_estimate=cost(2 * rows * width * (wide + hidden), 40e6, rows * hidden),
        name="ffn_forward",
    )


def out_kernel(act_ref, mid_ref, wd_ref, vec_ref, out_ref):
    w_down = wd_ref[...].reshape(-1, wd_ref.shape[2])
    out_ref[...] = mid_ref[...] + dot(act_ref[...], w_down) + vec_ref[6:7, :]


def out_forward(act, mid, w_down, vec, deps=()):
    rows, width = mid.shape
    hidden = act.shape[1]
    block = 256
    by_rows = lambda n: pl.BlockSpec((block, n), lambda i: (i, 0))
    whole = lambda a: pl.BlockSpec(a.shape, lambda i: (0, 0))
    return call(
        out_kernel,
        (act, mid, w_down, vec),
        [by_rows(hidden), by_rows(width), const_spec(w_down), whole(vec)],
        deps,
        grid=(rows // block,),
        out_specs=by_rows(width),
        out_shape=jax.ShapeDtypeStruct((rows, width), F32),
        compiler_params=params(),
        cost_estimate=cost(2 * rows * width * hidden, 18e6),
        name="out_forward",
    )


def store_units(table_ref, result, keep_ref, send_ref, core_bit, put, absolute):
    half = keep_ref.shape[0]
    units = 2 * half
    size = result.shape[0] // units
    for mine in range(2):

        @pl.when(table_ref[4 * units] == mine)
        def _(mine=mine):
            for d in range(units):
                i = d
                place = table_ref[d + 2 * units * absolute]
                rows = result[i * size : (i + 1) * size, :].astype(BF)
                if ((d >> core_bit) & 1) == mine:
                    put(keep_ref, place, rows)
                else:
                    put(send_ref, place - half, rows)


def put_rows(ref, place, rows):
    ref[place] = rows


def up_grad_kernel(table_ref, dy_ref, a2_ref, wd_ref, gd_ref, *refs, places):
    count = len(places)
    parts = refs[:count]
    sums_ref, da2_ref, keep_hbm, send_hbm = refs[count : count + 4]
    a2t, wu_units, wu_ref, du_ref, stage, sems = refs[count + 4 :]
    g = pl.program_id(0)
    last = pl.num_programs(0) - 1
    rows, chunk = du_ref.shape
    n, size, _ = wu_units.shape
    block = 256
    slot = lax.rem(g, 2)

    def sent(at, step):
        cols = pl.ds(pl.multiple_of(step * chunk, chunk), chunk)
        half = n // 2
        return [
            pltpu.make_async_copy(
                stage.at[at, pl.ds(i * half, half)], ref.at[:, :, cols], sems.at[at, i]
            )
            for i, ref in enumerate((keep_hbm, send_hbm))
        ]

    @pl.when(g == 0)
    def _():
        a2t[...] = jnp.transpose(a2_ref[...])
        da2_ref[...] = jnp.zeros_like(da2_ref)

    @pl.when(g >= 2)
    def _():
        for copy in sent(slot, g - 2):
            copy.wait()

    assemble(table_ref, parts, places, wu_units, True)
    flatten_units(wu_units, wu_ref)
    w_down = wd_ref[...].reshape(chunk, wd_ref.shape[2])
    total = jnp.zeros((1, chunk), F32)
    for i in range(rows // block):
        part = slice(i * block, (i + 1) * block)
        dh = dot_rt(dy_ref[part, :], w_down)
        du = (dh * gd_ref[part, :].astype(F32)).astype(BF)
        du_ref[part, :] = du
        total += jnp.sum(du.astype(F32), axis=0, keepdims=True)
        da2_ref[part, :] += dot_rt(du, wu_ref[...])
    sums_ref[...] = total
    for c in range(0, chunk, block):
        result = dot(a2t[...], du_ref[:, c : c + block])
        for d in range(n):
            place = table_ref[2 * n + d]
            stage[slot, place, :, c : c + block] = result[d * size : (d + 1) * size, :].astype(BF)
    for copy in sent(slot, g):
        copy.start()

    @pl.when(g == last)
    def _():
        for copy in sent(1 - slot, g - 1) + sent(slot, g):
            copy.wait()


def up_grad(table, dy, a2, w_down, gd, gathered, deps=()):
    parts, places = gathered
    rows, width = dy.shape
    hidden = gd.shape[1]
    n, deep, _ = w_down.shape
    size = width // n
    chunk = hidden // 4
    anywhere = pl.BlockSpec(memory_space=pl.ANY)
    shape = jax.ShapeDtypeStruct((n // 2, size, hidden), BF)
    once = lambda a: pl.BlockSpec(a.shape, lambda g: (0, 0), pipeline_mode=pl.Buffered(1))
    return call(
        functools.partial(up_grad_kernel, places=places),
        (table, dy, a2, w_down, gd, *parts),
        [
            pl.BlockSpec(memory_space=pltpu.SMEM),
            once(dy),
            once(a2),
            pl.BlockSpec((n // 4, deep, width), lambda g: (g, 0, 0)),
            pl.BlockSpec((rows, chunk), lambda g: (0, g)),
        ]
        + [
            pl.BlockSpec((p.shape[0], size, chunk), lambda g: (0, 0, width // chunk + g))
            for p in parts
        ],
        deps,
        grid=(hidden // chunk,),
        out_specs=[
            pl.BlockSpec((1, chunk), lambda g: (0, g)),
            pl.BlockSpec((rows, width), lambda g: (0, 0)),
            anywhere,
            anywhere,
        ],
        out_shape=[
            jax.ShapeDtypeStruct((1, hidden), F32),
            jax.ShapeDtypeStruct((rows, width), F32),
            shape,
            shape,
        ],
        scratch_shapes=[
            pltpu.VMEM((width, rows), BF),
            pltpu.VMEM((n, size, chunk), BF),
            pltpu.VMEM((width, chunk), BF),
            pltpu.VMEM((rows, chunk), BF),
            pltpu.VMEM((2, n, size, chunk), BF),
            pltpu.SemaphoreType.DMA((2, 2)),
        ],
        compiler_params=params(),
        cost_estimate=cost(6 * rows * width * hidden, 25e6),
        name="up_grad",
    )


def mid_back_kernel(
    table_ref,
    da2_ref,
    w_ref,
    mid_ref,
    dy_ref,
    ctx1_ref,
    ctx2_ref,
    vec_ref,
    dmid_ref,
    dctx_ref,
    sums_ref,
    keep_ref,
    send_ref,
    acc,
    *,
    core_bit,
):
    i = pl.program_id(0)
    da2 = da2_ref[...]
    normed, rs = norm_parts(mid_ref[...])
    dy = dy_ref[...].astype(F32)
    dmid = norm_back(normed, rs, vec_ref[4:5, :], da2) + dy
    dmid_ref[...] = dmid
    dbr = dmid.astype(BF)
    dctx_ref[...] = dot_rt(dbr, w_ref[...]).astype(BF)
    total = lambda v: jnp.sum(v, axis=0, keepdims=True)
    sums = jnp.concatenate(
        [
            total(dbr.astype(F32)),
            total(da2 * normed),
            total(da2),
            total(dy),
            jnp.zeros((4, dy.shape[1]), F32),
        ],
        axis=0,
    )
    part = dot_lt(jnp.concatenate([ctx1_ref[...], ctx2_ref[...]], axis=1), dbr)

    @pl.when(i == 0)
    def _():
        sums_ref[...] = sums
        acc[...] = part

    @pl.when(i > 0)
    def _():
        sums_ref[...] += sums
        acc[...] += part

    @pl.when(i == pl.num_programs(0) - 1)
    def _():
        store_units(table_ref, acc, keep_ref, send_ref, core_bit, put_rows, True)


def mid_back(table, da2, w_out, mid, dy, ctx, vec, n, core_bit, deps=()):
    rows, width = dy.shape
    unit = width // n
    block = 256
    by_rows = lambda m: pl.BlockSpec((block, m), lambda i: (i, 0))
    whole = lambda a: pl.BlockSpec(a.shape, lambda i: (0, 0))
    units = pl.BlockSpec((n // 2, unit, width), lambda i: (0, 0, 0))
    shape = jax.ShapeDtypeStruct((n // 2, unit, width), BF)
    return call(
        functools.partial(mid_back_kernel, core_bit=core_bit),
        (table, da2, w_out, mid, dy, *ctx, vec),
        [
            pl.BlockSpec(memory_space=pltpu.SMEM),
            by_rows(width),
            whole(w_out),
            by_rows(width),
            by_rows(width),
            *(by_rows(c.shape[1]) for c in ctx),
            whole(vec),
        ],
        deps,
        grid=(rows // block,),
        out_specs=[
            by_rows(width),
            by_rows(width),
            pl.BlockSpec((8, width), lambda i: (0, 0)),
            units,
            units,
        ],
        out_shape=[
            jax.ShapeDtypeStruct((rows, width), F32),
            jax.ShapeDtypeStruct((rows, width), BF),
            jax.ShapeDtypeStruct((8, width), F32),
            shape,
            shape,
        ],
        scratch_shapes=[pltpu.VMEM((width, width), F32)],
        compiler_params=params(),
        cost_estimate=cost(4 * rows * width * width, 16e6),
        name="mid_back",
    )


def token_grad_kernel(x_ref, *refs):
    *parts, w_ref, dmid_ref, vec_ref, grad_ref = refs
    dproj = jnp.concatenate([ref[...] for ref in parts], axis=1)
    da1 = dot_rt(dproj, w_ref[:, : dproj.shape[1]])
    normed, rs = norm_parts(x_ref[...].astype(F32))
    grad_ref[...] = dmid_ref[...] + norm_back(normed, rs, vec_ref[0:1, :], da1)


def token_grad(tokens, parts, w_in, dmid, vec, deps=()):
    rows, width = tokens.shape
    block = 256
    by_rows = lambda m: pl.BlockSpec((block, m), lambda i: (i, 0))
    whole = lambda a: pl.BlockSpec(a.shape, lambda i: (0, 0))
    return call(
        token_grad_kernel,
        (tokens, *parts, w_in, dmid, vec),
        [by_rows(width)]
        + [by_rows(p.shape[1]) for p in parts]
        + [whole(w_in), by_rows(width), whole(vec)],
        deps,
        grid=(rows // block,),
        out_specs=by_rows(width),
        out_shape=jax.ShapeDtypeStruct((rows, width), F32),
        compiler_params=params(),
        cost_estimate=cost(2 * rows * width * w_in.shape[1], 17e6),
        name="token_grad",
    )


def in_grad_kernel(table_ref, n1_ref, w_ref, *refs, starts, core_bit):
    count = len(starts)
    parts = refs[:count]
    s2_ref, c1_ref, keep_ref, send_ref = refs[count:]
    width = n1_ref.shape[1]
    turned = jnp.transpose(n1_ref[...])
    vec_at = w_ref.shape[1] - LANES
    gain = w_ref[:, vec_at : vec_at + 1].astype(F32)
    shift = w_ref[:, vec_at + 1 : vec_at + 2].astype(F32)
    dgain = jnp.zeros((width, 1), F32)
    dshift = jnp.zeros((width, 1), F32)
    query_sums = []
    for ref, start in zip(parts, starts, strict=True):
        size = ref.shape[1]
        grads = ref[...]
        sums = jnp.sum(grads.astype(F32), axis=0, keepdims=True)
        if start < width:
            query_sums.append(sums)
        weights = w_ref[:, start : start + size].astype(F32)
        product = dot(turned, grads)
        dgain += jnp.sum(weights * product, axis=1, keepdims=True)
        dshift += jnp.sum(weights * sums, axis=1, keepdims=True)

        def put(out, place, rows, at=start, size=size):
            out[place, :, at : at + size] = rows

        store_units(
            table_ref, gain * product + shift * sums, keep_ref, send_ref, core_bit, put, False
        )
    hidden_rows = c1_ref.shape[1] // width
    stacked = jnp.concatenate(
        [jnp.zeros((2, width), F32), jnp.concatenate(query_sums, axis=1), s2_ref[0:4, :]]
        + [c1_ref[0:1, g * width : (g + 1) * width] for g in range(hidden_rows)]
        + [jnp.zeros((LANES - 7 - hidden_rows, width), F32)],
        axis=0,
    )
    lane = lanes_of((width, LANES))
    own = jnp.where(lane == 0, dgain, jnp.where(lane == 1, dshift, 0.0))

    def put_last(out, place, rows):
        out[place, :, vec_at:] = rows

    store_units(
        table_ref, jnp.transpose(stacked) + own, keep_ref, send_ref, core_bit, put_last, False
    )


def in_grad(table, n1, w_in, parts, starts, s2, c1, n, core_bit, deps=()):
    rows, width = n1.shape
    shape = jax.ShapeDtypeStruct((n // 2, width // n, w_in.shape[1]), BF)
    vmem = pl.BlockSpec(memory_space=pltpu.VMEM)
    ins = (table, n1, w_in, *parts, s2, c1)
    return call(
        functools.partial(in_grad_kernel, starts=starts, core_bit=core_bit),
        ins,
        [pl.BlockSpec(memory_space=pltpu.SMEM)] + [vmem] * (len(ins) - 1),
        deps,
        out_specs=[vmem] * 2,
        out_shape=[shape, shape],
        compiler_params=pltpu.CompilerParams(vmem_limit_bytes=VMEM_LIMIT),
        cost_estimate=cost(2 * rows * width * w_in.shape[1], 12e6),
        name="in_grad",
    )


def stages_of(n_dp, n_fsdp):
    fsdp_bits = n_fsdp.bit_length() - 1
    dp_bits = n_dp.bit_length() - 1
    low = list(range(fsdp_bits // 2))[::-1]
    high = list(range(fsdp_bits // 2, fsdp_bits))[::-1]
    z_bits = list(range(fsdp_bits + 1, fsdp_bits + dp_bits))[::-1]
    core = fsdp_bits
    return core, ([core] + high + low + z_bits, [core] + low + high + z_bits)


def place_table(n_dp, n_fsdp):
    core, orders = stages_of(n_dp, n_fsdp)
    n = n_dp * n_fsdp
    table = np.zeros((n, 4 * n + 1), np.int32)
    for me in range(n):
        for absolute in range(2):
            base = 2 * n * absolute
            for d in range(n):
                away = d ^ me
                place = 0
                for bit in orders[(d >> core) & 1]:
                    of = d if absolute and bit > core else away
                    place = place * 2 + ((of >> bit) & 1)
                table[me, base + d] = place
                table[me, base + n + place] = d
        table[me, 4 * n] = (me >> core) & 1
    return table


def tied_columns_kernel(*refs):
    *parts, out_ref = refs
    at, size = 0, parts[0].shape[0]
    for ref in parts:
        out_ref[:size, at : at + ref.shape[1]] = ref[...]
        at += ref.shape[1]
    if out_ref.shape[0] > size:
        out_ref[size:, :] = jnp.zeros((out_ref.shape[0] - size, at), BF)


def tied_columns(parts, deps, rows):
    vmem = pl.BlockSpec(memory_space=pltpu.VMEM)
    shape = (rows, sum(p.shape[1] for p in parts))
    return call(
        tied_columns_kernel,
        parts,
        [vmem] * len(parts),
        deps,
        out_specs=vmem,
        out_shape=jax.ShapeDtypeStruct(shape, BF),
        cost_estimate=cost(0, 4 * shape[0] * shape[1]),
        name="tied_columns",
    )


def merge_kernel(*refs):
    *parts, out_ref = refs
    at = 0
    for ref in parts:
        out_ref[at : at + ref.shape[0]] = ref[:, : out_ref.shape[1]]
        at += ref.shape[0]


def merge(parts, deps, size=None):
    if not deps:
        return jnp.concatenate(parts, axis=0)
    vmem = pl.BlockSpec(memory_space=pltpu.VMEM)
    shape = (sum(p.shape[0] for p in parts), size or parts[0].shape[1], parts[0].shape[2])
    return call(
        merge_kernel,
        parts,
        [vmem] * len(parts),
        deps,
        out_specs=vmem,
        out_shape=jax.ShapeDtypeStruct(shape, BF),
        compiler_params=pltpu.CompilerParams(vmem_limit_bytes=VMEM_LIMIT),
        cost_estimate=cost(0, 4 * shape[0] * shape[1] * shape[2]),
        name="merge",
    )


class Exchange:
    def __init__(self, n_dp, n_fsdp):
        self.n = n_dp * n_fsdp
        self.count = self.n.bit_length() - 1
        self.core_bit, self.orders = stages_of(n_dp, n_fsdp)
        me = lax.axis_index("dp") * n_fsdp + lax.axis_index("fsdp")
        self.z = n_dp // 2
        self.z_groups = [list(range(c, n_dp, 2)) for c in range(2)]
        table = jnp.asarray(place_table(n_dp, n_fsdp))
        self.table = lax.dynamic_slice(table, (me, 0), (1, table.shape[1]))[0]

    def swap(self, value, stage):
        bits = [self.orders[(i >> self.core_bit) & 1][stage] for i in range(self.n)]
        return lax.ppermute(value, AXES, [(i, i ^ (1 << b)) for i, b in enumerate(bits)])

    def over_z(self, value, away):
        mask = away << (self.core_bit + 1)
        return lax.ppermute(value, AXES, [(i, i ^ mask) for i in range(self.n)])

    def gather_z(self, rows, deps=()):
        held = rows[None]
        return merge([held] + [self.over_z(held, k) for k in range(1, self.z)], deps)

    def gather_z_apart(self, parts, after, deps):
        size, width = parts[0].shape[0], sum(p.shape[1] for p in parts)
        need = -(-(17 << 16) // (self.z * width * 2))
        padded = tied_columns(parts, after, max(size, -(-need // 4) * 4))
        got = lax.all_gather(padded, "dp", axis=0, axis_index_groups=self.z_groups)
        return merge((got,), deps, size)

    def gather_plane(self, held, stage, deps=()):
        return merge((held, self.swap(held, stage)), deps)

    def with_core(self, parts, places):
        half = self.n // 2
        others = [self.swap(p, 0) for p in parts]
        return (
            tuple(parts) + tuple(others),
            tuple(places) + tuple(tuple(b + half for b in bases) for bases in places),
        )


def fold_kernel(keep_ref, got_ref, stay_ref, go_ref):
    half = stay_ref.shape[0]
    total = keep_ref[...].astype(F32) + got_ref[...].astype(F32)
    stay_ref[...] = total[:half].astype(BF)
    go_ref[...] = total[half:].astype(BF)


def fold(keep, got, deps):
    count, size, width = keep.shape
    vmem = pl.BlockSpec(memory_space=pltpu.VMEM)
    shape = jax.ShapeDtypeStruct((count // 2, size, width), BF)
    return call(
        fold_kernel,
        (keep, got),
        [vmem] * 2,
        deps,
        out_specs=[vmem] * 2,
        out_shape=[shape, shape],
        compiler_params=pltpu.CompilerParams(vmem_limit_bytes=VMEM_LIMIT),
        cost_estimate=cost(count * size * width, 6 * count * size * width),
        name="fold",
    )


class Halving:
    def __init__(self, exchange, keep, send):
        self.exchange, self.keep, self.send, self.stage = exchange, keep, send, 0

    def step(self, apart=False, after=()):
        got = self.exchange.swap(self.send, self.stage)
        if after:
            self.stage += 1
            self.keep, self.send = fold(self.keep, got, after)
            return (self.send,)
        total = self.keep.astype(F32) + got.astype(F32)
        self.stage += 1
        half = total.shape[0] // 2
        if half < self.exchange.z and apart:
            self.keep = total
            return (total,)
        if half < self.exchange.z:
            self.keep = [total[k : k + 1].astype(BF) for k in range(total.shape[0])]
            return tuple(self.keep)
        self.keep = total[:half].astype(BF)
        self.send = total[half:].astype(BF)
        return (self.send,)

    def join(self, other):
        self.keep = jnp.concatenate([self.keep, other.keep], axis=2)
        self.send = jnp.concatenate([self.send, other.send], axis=2)
        return (self.send,)

    def last_apart(self):
        self.keep = [
            lax.psum_scatter(
                self.keep, "dp", scatter_dimension=0, tiled=True,
                axis_index_groups=self.exchange.z_groups,
            )
        ]
        self.got = ()

    def last(self):
        self.got = tuple(self.exchange.over_z(k, i + 1) for i, k in enumerate(self.keep[1:]))
        return self.got

    def result(self):
        return sum((g.astype(F32) for g in self.got), self.keep[0].astype(F32))[0]


def body(
    tokens, first_values, out_grad, lengths, in_proj, out_proj, up_proj, down_proj, vectors,
    *, n_dp, n_fsdp
):
    width = tokens.shape[1]
    cols = in_proj.shape[1]
    vrows = vectors.shape[0]
    exchange = Exchange(n_dp, n_fsdp)
    n, core_bit, table = exchange.n, exchange.core_bit, exchange.table

    z = exchange.z
    planes = exchange.count - z.bit_length()
    quarter = n // 8

    vec_t = jnp.pad(vectors.T, ((0, 0), (0, LANES - vrows)))
    held = exchange.gather_z(jnp.concatenate([in_proj, vec_t], axis=1))
    if planes == 2:
        got_a, got_b = exchange.swap(held, 1), exchange.swap(held, 2)
        got_ba = exchange.swap(got_a, 2)
        in_parts = exchange.with_core(
            (held, got_b, got_a, got_ba), tuple((q * quarter,) for q in range(4))
        )
    else:
        for stage in range(planes, 0, -1):
            held = exchange.gather_plane(held, stage)
        in_parts = exchange.with_core((held,), ((0,),))

    w_down = lax.all_gather(down_proj, AXES, axis=0, tiled=False)
    half = width // LANES // 2
    w_in, n1, qkv, vec = in_forward(table, tokens, first_values, in_parts)
    held_mid = exchange.gather_z_apart((out_proj, up_proj), (held,), (n1,))
    ctx1, lse1 = attn_forward(lengths, qkv, width, 0, half, (held_mid,))
    for stage in range(planes, 1, -1):
        held_mid = exchange.gather_plane(held_mid, stage, (ctx1,))
    ctx2, lse2 = attn_forward(lengths, qkv, width, half, half, (held_mid,))
    got_mid = merge((exchange.swap(held_mid, 1),), (ctx2,))
    mid_parts = exchange.with_core((held_mid, got_mid), ((0,), (n // 4,)))
    ctx = (ctx1, ctx2)
    act, gd, mid, a2, w_out, *halves = ffn_forward(
        table, ctx, tokens, out_grad, vec, mid_parts, core_bit
    )
    h_down = Halving(exchange, *halves)
    deps = h_down.step()
    dc1, da2, *halves = up_grad(table, out_grad, a2, w_down, gd, mid_parts, deps)
    h_up = Halving(exchange, *halves)
    deps = h_down.step()
    dmid, dctx, sums2, *halves = mid_back(
        table, da2, w_out, mid, out_grad, ctx, vec, n, core_bit, deps
    )
    h_out = Halving(exchange, *halves)
    deps = h_up.step() + h_out.step() + h_up.join(h_out)
    dq1, dk1, dv1 = attn_backward(lengths, lse1, qkv, ctx1, dctx, 0, half, BF, deps)
    for _ in range(planes - 2):
        h_down.step(), h_up.step()
    deps = h_up.step() + (dq1,)
    dq2, dk2, first_grad = attn_backward(
        lengths, lse2, qkv, ctx2, dctx, half, half, F32, deps
    )
    h_down.step(True)
    h_down.last_apart()
    deps = h_up.step(True) + (h_down.keep[0],)
    h_up.last_apart()
    split = half * LANES
    parts = (dq1, dq2, dk1, dk2, dv1)
    starts = (0, split, width, width + split, 2 * width)
    h_in = Halving(
        exchange, *in_grad(table, n1, w_in, parts, starts, sums2, dc1, n, core_bit, deps)
    )
    deps = h_in.step()
    input_grad = token_grad(tokens, parts, w_in, dmid, vec, deps)
    for _ in range(planes - 1):
        deps = h_in.step(after=(input_grad,))
    output = out_forward(act, mid, w_down, vec, deps + (h_up.keep[0],))
    h_in.step()
    h_in.last()
    g_in, g_mid = h_in.result(), h_up.result()
    hidden = up_proj.shape[1]
    return (
        output, input_grad, first_grad, g_in[:, :cols], g_mid[:, hidden:], g_mid[:, :hidden],
        h_down.result(), g_in[:, cols : cols + vrows].T,
    )


def solution(mesh):
    rows = P(AXES, None)
    cols = P(None, AXES)
    return jax.shard_map(
        functools.partial(body, n_dp=mesh.shape["dp"], n_fsdp=mesh.shape["fsdp"]),
        mesh=mesh,
        in_specs=(rows,) * 8 + (cols,),
        out_specs=(rows,) * 7 + (cols,),
        check_vma=False,
    )
```

```python
import functools

import jax
import jax.numpy as jnp
import numpy as np
from jax import lax
from jax.experimental import pallas as pl
from jax.experimental.pallas import tpu as pltpu
from jax.sharding import PartitionSpec as P

H = 12
HD = 64
EPS = 1e-05
NEG = -1000000000.0
LANES = 128
AXES = ("dp", "fsdp")
BF = jnp.bfloat16
F32 = jnp.float32
VMEM_LIMIT = 56 * 1024 * 1024
GELU_C = 0.7978845608028654
GELU_A = 0.044715


def dot(a, b):
    return lax.dot_general(a, b, (((1,), (0,)), ((), ())), preferred_element_type=F32)


def dot_rt(a, b):
    return lax.dot_general(a, b, (((1,), (1,)), ((), ())), preferred_element_type=F32)


def dot_lt(a, b):
    return lax.dot_general(a, b, (((0,), (0,)), ((), ())), preferred_element_type=F32)


def params(grid_rank=1):
    return pltpu.CompilerParams(
        vmem_limit_bytes=VMEM_LIMIT, dimension_semantics=("arbitrary",) * grid_rank
    )


def cost(flops, nbytes, trans=0):
    return pl.CostEstimate(flops=int(flops), bytes_accessed=int(nbytes), transcendentals=int(trans))


def call(kernel, ins, in_specs, deps=(), **kw):
    count, extra = len(ins), len(deps)

    def run(*refs):
        kernel(*refs[:count], *refs[count + extra :])

    specs = list(in_specs) + [pl.BlockSpec(memory_space=pl.ANY)] * extra
    return pl.pallas_call(run, in_specs=specs, **kw)(*ins, *deps)


def norm_parts(values):
    centred = values - jnp.mean(values, axis=-1, keepdims=True)
    spread = jnp.mean(centred * centred, axis=-1, keepdims=True)
    rs = lax.rsqrt(spread + EPS)
    return centred * rs, rs


def norm_back(normed, rs, gain, grad):
    scaled = grad * gain
    m1 = jnp.mean(scaled, axis=-1, keepdims=True)
    m2 = jnp.mean(scaled * normed, axis=-1, keepdims=True)
    return rs * (scaled - m1 - normed * m2)


def assemble(table_ref, refs, places, whole_ref):
    n = whole_ref.shape[0]
    for ref, bases in zip(refs, places, strict=True):
        each = ref.shape[0] // len(bases)
        for b, base in enumerate(bases):
            for k in range(each):
                whole_ref[table_ref[n + base + k]] = ref[b * each + k]


def flatten_units(units_ref, matrix_ref):
    size = units_ref.shape[1]
    for d in range(units_ref.shape[0]):
        matrix_ref[d * size : (d + 1) * size, :] = units_ref[d]


def const_spec(a):
    rank = len(a.shape)
    return pl.BlockSpec(a.shape, lambda *_: (0,) * rank)


def in_kernel(table_ref, x_ref, fv_ref, *refs, places):
    *parts, w_hbm, n1_ref, qkv_ref, vec_ref, units_ref, w_ref, sem = refs
    width = x_ref.shape[1]
    cols = w_ref.shape[1] - LANES
    copy = pltpu.make_async_copy(w_ref, w_hbm, sem)

    @pl.when(pl.program_id(0) == 0)
    def _():
        assemble(table_ref, parts, places, units_ref)
        flatten_units(units_ref, w_ref)
        copy.start()
        turned = jnp.transpose(w_ref[:, cols:].astype(F32))
        vec_ref[...] = turned[: vec_ref.shape[0]]

    normed, _ = norm_parts(x_ref[...].astype(F32))
    a1 = (normed * vec_ref[0:1, :] + vec_ref[1:2, :]).astype(BF)
    n1_ref[...] = normed.astype(BF)
    proj = dot(a1, w_ref[:, :cols])
    queries = (proj[:, :width] + vec_ref[2:3, :]).astype(BF)
    qkv_ref[:, :width] = queries * jnp.asarray(HD**-0.5, BF)
    qkv_ref[:, width:cols] = proj[:, width:].astype(BF)
    qkv_ref[:, cols:] = fv_ref[...]

    @pl.when(pl.program_id(0) == pl.num_programs(0) - 1)
    def _():
        copy.wait()


def in_forward(table, tokens, first_values, gathered, deps=()):
    parts, places = gathered
    rows, width = tokens.shape
    half = first_values.shape[1]
    _, size, wide = parts[0].shape
    n = width // size
    block = 256
    by_rows = lambda m: pl.BlockSpec((block, m), lambda i: (i, 0))
    const = lambda *shape: pl.BlockSpec(shape, lambda i: (0, 0))
    return call(
        functools.partial(in_kernel, places=places),
        (table, tokens, first_values, *parts),
        [pl.BlockSpec(memory_space=pltpu.SMEM), by_rows(width), by_rows(half)]
        + [const_spec(p) for p in parts],
        deps,
        grid=(rows // block,),
        out_specs=[
            pl.BlockSpec(memory_space=pl.ANY),
            by_rows(width),
            by_rows(wide - LANES + half),
            const(16, width),
        ],
        out_shape=[
            jax.ShapeDtypeStruct((width, wide), BF),
            jax.ShapeDtypeStruct((rows, width), BF),
            jax.ShapeDtypeStruct((rows, wide - LANES + half), BF),
            jax.ShapeDtypeStruct((16, width), F32),
        ],
        scratch_shapes=[
            pltpu.VMEM((n, size, wide), BF),
            pltpu.VMEM((width, wide), BF),
            pltpu.SemaphoreType.DMA(()),
        ],
        compiler_params=params(),
        cost_estimate=cost(2 * rows * width * wide, 16e6),
        name="in_forward",
    )


def lanes_of(shape):
    return lax.broadcasted_iota(jnp.int32, shape, 1)


def own_lanes(e, shape):
    lane = lanes_of(shape)
    return (lane < HD) if e == 0 else (lane >= HD)


def spare(e):
    return HD if e == 0 else 0


def split3(values):
    hi = values.astype(BF).astype(F32)
    rest = values - hi
    mid = rest.astype(BF).astype(F32)
    return hi, mid, rest - mid


def augmented(vectors, e, lane, seg, filled):
    aux = jnp.where((lane == spare(e)) & seg, filled, 0.0)
    return jnp.where(own_lanes(e, lane.shape), vectors, aux).astype(BF)


def causal(block):
    rows = lax.broadcasted_iota(jnp.int32, (block, block), 0)
    return rows <= lax.broadcasted_iota(jnp.int32, (block, block), 1)


def scores_of(keys, queries, tri, lo):
    s = dot_rt(keys, queries)
    diag = jnp.where(tri, s[lo:, :], NEG)
    return diag if lo == 0 else jnp.concatenate([s[:lo, :], diag], axis=0)


def attn_fwd_kernel(bound_ref, q_ref, k_ref, v_ref, ctx_ref, lse_ref):
    rows = q_ref.shape[0]
    block = 256
    bound = bound_ref[0, 0]
    shape = (rows, LANES)
    lane = lanes_of(shape)
    place = lax.broadcasted_iota(jnp.int32, shape, 0)
    k_all = k_ref[...].astype(F32)
    q_all = q_ref[...].astype(F32)
    values = jnp.concatenate([v_ref[...], jnp.ones(shape, BF)], axis=1)
    tri = causal(block)
    ctxs = [[None, None] for _ in range(rows // block)]
    k_augs = [augmented(k_all, e, lane, place < bound, 1.0) for e in range(2)]
    q_augs = [augmented(q_all, e, lane, place >= bound, NEG) for e in range(2)]
    chains = [(j, e) for j in range(rows // block) for e in range(2)]

    def scores(j, e):
        lo, hi = j * block, (j + 1) * block
        return scores_of(k_augs[e][:hi, :], q_augs[e][lo:hi, :], tri, lo)

    def weighted(j, e, p):
        o = dot_lt(p, values[: (j + 1) * block, :])
        ctxs[j][e] = o[:, :LANES] / o[:, LANES:]

    following = scores(*chains[0])
    waiting = None
    for i, (j, e) in enumerate(chains):
        s = following
        if i + 1 < len(chains):
            following = scores(*chains[i + 1])
        peak = jnp.max(s, axis=0, keepdims=True)
        p = jnp.exp(s - peak)
        lse = peak + jnp.log(jnp.sum(p, axis=0, keepdims=True))
        lse_ref[0, e : e + 1, j * block : (j + 1) * block] = lse
        if waiting is not None:
            weighted(*waiting)
        waiting = (j, e, p.astype(BF))
    weighted(*waiting)
    first = lanes_of((block, LANES)) < HD
    for j in range(rows // block):
        ctx_ref[j * block : (j + 1) * block, :] = jnp.where(first, *ctxs[j]).astype(BF)


def attn_forward(lengths, qkv, width, deps=()):
    rows = qkv.shape[0]
    pairs = width // LANES
    half = pairs // 2
    slab = lambda off: pl.BlockSpec((rows, LANES), lambda j: (0, off + j))

    def kernel(bound_ref, q_ref, k_ref, v_ref, ctx1_ref, ctx2_ref, lse1_ref, lse2_ref, ctx_ref, lse_ref):
        attn_fwd_kernel(bound_ref, q_ref, k_ref, v_ref, ctx_ref, lse_ref)
        for k, (ctx, lse) in enumerate(((ctx1_ref, lse1_ref), (ctx2_ref, lse2_ref))):

            @pl.when(pl.program_id(0) // half == k)
            def _(ctx=ctx, lse=lse):
                ctx[...] = ctx_ref[...]
                lse[...] = lse_ref[...]

    first = lambda j: jnp.minimum(j, half - 1)
    second = lambda j: jnp.maximum(j - half, 0)
    ctx_spec = lambda of: pl.BlockSpec((rows, LANES), lambda j: (0, of(j)))
    lse_spec = lambda of: pl.BlockSpec((1, 8, rows), lambda j: (of(j), 0, 0))
    ctx_shape = jax.ShapeDtypeStruct((rows, half * LANES), BF)
    lse_shape = jax.ShapeDtypeStruct((half, 8, rows), F32)
    return call(
        kernel,
        (lengths, qkv, qkv, qkv),
        [pl.BlockSpec(memory_space=pltpu.SMEM), *(slab(c * pairs) for c in range(3))],
        deps,
        grid=(pairs,),
        out_specs=[ctx_spec(first), ctx_spec(second), lse_spec(first), lse_spec(second)],
        out_shape=[ctx_shape, ctx_shape, lse_shape, lse_shape],
        scratch_shapes=[pltpu.VMEM((rows, LANES), BF), pltpu.VMEM((1, 8, rows), F32)],
        compiler_params=params(),
        cost_estimate=cost(2 * 2 * rows * rows * 256 * H * 0.63, 9e6, rows * rows * H),
        name="attn_forward",
    )


def attn_bwd_kernel(
    bound_ref, lse_ref, q_ref, k_ref, v_ref, ctx_ref, do_ref, dq_ref, dk_ref, dv_ref, dk_acc, dv_acc
):
    rows = k_ref.shape[0]
    block = 256
    bound = bound_ref[0, 0]
    full = (rows, LANES)
    lane = lanes_of(full)
    place = lax.broadcasted_iota(jnp.int32, full, 0)
    q_all = q_ref[...].astype(F32)
    k_all = k_ref[...].astype(F32)
    v_all = v_ref[...].astype(F32)
    do_all = do_ref[...].astype(F32)
    prod = do_all * ctx_ref[...].astype(F32)
    tri = causal(block)
    dqs = [[None, None] for _ in range(rows // block)]
    for e in range(2):
        sp = spare(e)
        own = own_lanes(e, full)
        three = (lane >= sp + 1) & (lane <= sp + 3)
        k_aug = augmented(k_all, e, lane, place < bound, 1.0)
        q_aug = augmented(q_all, e, lane, place >= bound, NEG)
        v_aug = jnp.where(own, v_all, jnp.where(three, 1.0, 0.0)).astype(BF)
        delta = jnp.sum(jnp.where(own, prod, 0.0), axis=-1, keepdims=True)
        d_hi, d_mid, d_lo = split3(-delta)
        do_aug = jnp.where(
            own,
            do_all,
            jnp.where(
                lane == sp + 1,
                d_hi,
                jnp.where(lane == sp + 2, d_mid, jnp.where(lane == sp + 3, d_lo, 0.0)),
            ),
        ).astype(BF)
        for j in reversed(range(rows // block)):
            lo, hi = j * block, (j + 1) * block
            q_j = q_aug[lo:hi, :]
            do_j = do_aug[lo:hi, :]
            p = jnp.exp(scores_of(k_aug[:hi, :], q_j, tri, lo) - lse_ref[0, e : e + 1, lo:hi])
            ds = (p * dot_rt(v_aug[:hi, :], do_j)).astype(BF)
            dv_j = dot(p.astype(BF), do_j)
            dk_j = dot(ds, q_j)
            if j == rows // block - 1:
                dv_acc[e] = dv_j
                dk_acc[e] = dk_j
            else:
                dv_acc[e, :hi, :] += dv_j
                dk_acc[e, :hi, :] += dk_j
            dqs[j][e] = dot_lt(ds, k_aug[:hi, :])
    first = lanes_of((block, LANES)) < HD
    for j in range(rows // block):
        dq_ref[j * block : (j + 1) * block, :] = (jnp.where(first, *dqs[j]) * HD**-0.5).astype(BF)
    dk_ref[...] = jnp.where(lane < HD, dk_acc[0], dk_acc[1]).astype(BF)
    dv_ref[...] = jnp.where(lane < HD, dv_acc[0], dv_acc[1]).astype(dv_ref.dtype)


def attn_backward(lengths, lse, qkv, ctx, dctx, first, count, dv_type, deps=()):
    rows, width = dctx.shape
    pairs = width // LANES
    slab = lambda off: pl.BlockSpec((rows, LANES), lambda j, off=off: (0, off + j))
    shape = lambda dtype: jax.ShapeDtypeStruct((rows, count * LANES), dtype)
    return call(
        attn_bwd_kernel,
        (lengths, lse, qkv, qkv, qkv, ctx, dctx),
        [
            pl.BlockSpec(memory_space=pltpu.SMEM),
            pl.BlockSpec((1, 8, rows), lambda j: (j, 0, 0)),
            slab(first),
            slab(pairs + first),
            slab(2 * pairs + first),
            slab(0),
            slab(first),
        ],
        deps,
        grid=(count,),
        out_specs=[slab(0)] * 3,
        out_shape=[shape(BF), shape(BF), shape(dv_type)],
        scratch_shapes=[
            pltpu.VMEM((2, rows, LANES), F32),
            pltpu.VMEM((2, rows, LANES), F32),
        ],
        compiler_params=params(),
        cost_estimate=cost(5 * 2 * rows * rows * 256 * 2 * count * 0.63, 15e6, rows * rows * 2 * count),
        name="attn_backward",
    )


def ffn_kernel(
    table_ref, ctx1_ref, ctx2_ref, x_ref, dy_ref, vec_ref, *refs, places, core_bit
):
    count = len(places)
    out_parts, up_parts = refs[:count], refs[count : 2 * count]
    (act_ref, gd_ref, mid_hbm, a2_hbm, wo_hbm, keep_hbm, send_hbm) = refs[
        2 * count : 2 * count + 7
    ]
    wo_units, wu_units, wo_ref, wu_ref, mid_ref, a2_ref, stage, once_sems, sems = refs[
        2 * count + 7 :
    ]
    g = pl.program_id(0)
    last = pl.num_programs(0) - 1
    rows, width = x_ref.shape
    chunk = act_ref.shape[1]
    n = wu_units.shape[0]
    block = 256
    once = (
        pltpu.make_async_copy(mid_ref, mid_hbm, once_sems.at[0]),
        pltpu.make_async_copy(a2_ref, a2_hbm, once_sems.at[1]),
        pltpu.make_async_copy(wo_ref, wo_hbm, once_sems.at[2]),
    )

    @pl.when(g == 0)
    def _():
        assemble(table_ref, out_parts, places, wo_units)
        flatten_units(wo_units, wo_ref)
        for i in range(rows // block):
            part = slice(i * block, (i + 1) * block)
            ctx = jnp.concatenate([ctx1_ref[part, :], ctx2_ref[part, :]], axis=1)
            branch = dot(ctx, wo_ref[...]) + vec_ref[3:4, :]
            mid = x_ref[part, :].astype(F32) + branch
            mid_ref[part, :] = mid
            normed, _ = norm_parts(mid)
            a2_ref[part, :] = (normed * vec_ref[4:5, :] + vec_ref[5:6, :]).astype(BF)
        for copy in once:
            copy.start()

    assemble(table_ref, up_parts, places, wu_units)
    flatten_units(wu_units, wu_ref)
    per_row = width // chunk
    row = vec_ref[pl.ds(7 + g // per_row, 1), :]
    bias = row[:, :chunk]
    for c in range(1, per_row):
        bias = jnp.where(g % per_row == c, row[:, c * chunk : (c + 1) * chunk], bias)
    for i in range(rows // block):
        part = slice(i * block, (i + 1) * block)
        u = dot(a2_ref[part, :], wu_ref[...]) + bias
        u2 = u * u
        t = jnp.tanh(u * (GELU_C + (GELU_C * GELU_A) * u2))
        half = 0.5 + 0.5 * t
        act = u * half
        act_ref[part, :] = act.astype(BF)
        slope = half + act * (1.0 - t) * (GELU_C + (3.0 * GELU_C * GELU_A) * u2)
        gd_ref[part, :] = slope.astype(BF)
    result = dot_lt(act_ref[...], dy_ref[...])
    units = stage.shape[1]
    size = chunk // units
    slot = lax.rem(g, 2)
    mine = table_ref[4 * n]
    sent = lambda at, i: pltpu.make_async_copy(stage.at[at, i], keep_hbm.at[0], sems.at[at, i])

    @pl.when(g >= 2)
    def _():
        for i in range(units):
            sent(slot, i).wait()

    for i in range(units):
        stage[slot, i] = result[i * size : (i + 1) * size, :].astype(BF)
        d = g * units + i
        place = table_ref[2 * n + d]
        core = lax.rem(lax.shift_right_logical(d, core_bit), 2)

        @pl.when(core == mine)
        def _(i=i, place=place):
            pltpu.make_async_copy(stage.at[slot, i], keep_hbm.at[place], sems.at[slot, i]).start()

        @pl.when(core != mine)
        def _(i=i, place=place):
            pltpu.make_async_copy(
                stage.at[slot, i], send_hbm.at[place - n // 2], sems.at[slot, i]
            ).start()

    @pl.when(g == last)
    def _():
        for copy in once:
            copy.wait()
        for i in range(units):
            sent(1 - slot, i).wait()
            sent(slot, i).wait()


def ffn_forward(table, ctx, tokens, dy, vec, gathered, core_bit, deps=()):
    parts, places = gathered
    rows, width = tokens.shape
    _, size, wide = parts[0].shape
    hidden = wide - width
    n = width // size
    chunk = hidden // 4
    unit = hidden // n
    anywhere = pl.BlockSpec(memory_space=pl.ANY)
    halves = jax.ShapeDtypeStruct((n // 2, unit, width), BF)
    return call(
        functools.partial(ffn_kernel, places=places, core_bit=core_bit),
        (table, *ctx, tokens, dy, vec, *parts, *parts),
        [pl.BlockSpec(memory_space=pltpu.SMEM)]
        + [
            pl.BlockSpec(a.shape, lambda g: (0, 0), pipeline_mode=pl.Buffered(1))
            for a in (*ctx, tokens, dy, vec)
        ]
        + [
            pl.BlockSpec(
                (p.shape[0], size, width), lambda g: (0, 0, 0), pipeline_mode=pl.Buffered(1)
            )
            for p in parts
        ]
        + [
            pl.BlockSpec((p.shape[0], size, chunk), lambda g: (0, 0, width // chunk + g))
            for p in parts
        ],
        deps,
        grid=(hidden // chunk,),
        out_specs=[pl.BlockSpec((rows, chunk), lambda g: (0, g))] * 2 + [anywhere] * 5,
        out_shape=[
            jax.ShapeDtypeStruct((rows, hidden), BF),
            jax.ShapeDtypeStruct((rows, hidden), BF),
            jax.ShapeDtypeStruct((rows, width), F32),
            jax.ShapeDtypeStruct((rows, width), BF),
            jax.ShapeDtypeStruct((width, width), BF),
            halves,
            halves,
        ],
        scratch_shapes=[
            pltpu.VMEM((n, size, width), BF),
            pltpu.VMEM((n, size, chunk), BF),
            pltpu.VMEM((width, width), BF),
            pltpu.VMEM((width, chunk), BF),
            pltpu.VMEM((rows, width), F32),
            pltpu.VMEM((rows, width), BF),
            pltpu.VMEM((2, n // 4, unit, width), BF),
            pltpu.SemaphoreType.DMA((3,)),
            pltpu.SemaphoreType.DMA((2, n // 4)),
        ],
        compiler_params=params(),
        cost_estimate=cost(2 * rows * width * (wide + hidden), 40e6, rows * hidden),
        name="ffn_forward",
    )


def out_kernel(act_ref, mid_ref, wd_ref, vec_ref, *refs):
    out_ref = refs[-1]
    w_down = wd_ref[...].reshape(-1, wd_ref.shape[2])
    out_ref[...] = mid_ref[...] + dot(act_ref[...], w_down) + vec_ref[6:7, :]


def out_forward(act, mid, w_down, vec, half, into=(), deps=()):
    rows, width = mid.shape
    hidden = act.shape[1]
    block = 256
    steps = rows // block // 2
    by_rows = lambda n: pl.BlockSpec((block, n), lambda i: (i + half * steps, 0))
    whole = lambda a: pl.BlockSpec(a.shape, lambda i: (0, 0))
    return call(
        out_kernel,
        (act, mid, w_down, vec, *into),
        [by_rows(hidden), by_rows(width), const_spec(w_down), whole(vec)]
        + [pl.BlockSpec(memory_space=pl.ANY)] * len(into),
        deps,
        grid=(steps,),
        out_specs=by_rows(width),
        out_shape=jax.ShapeDtypeStruct((rows, width), F32),
        input_output_aliases={4: 0} if into else {},
        compiler_params=params(),
        cost_estimate=cost(rows * width * hidden, 12e6),
        name="out_forward",
    )


def store_units(table_ref, result, keep_ref, send_ref, core_bit, put, absolute):
    half = keep_ref.shape[0]
    units = 2 * half
    size = result.shape[0] // units
    for mine in range(2):

        @pl.when(table_ref[4 * units] == mine)
        def _(mine=mine):
            for d in range(units):
                i = d
                place = table_ref[d + 2 * units * absolute]
                rows = result[i * size : (i + 1) * size, :].astype(BF)
                if ((d >> core_bit) & 1) == mine:
                    put(keep_ref, place, rows)
                else:
                    put(send_ref, place - half, rows)


def put_rows(ref, place, rows):
    ref[place] = rows


def up_grad_kernel(table_ref, dy_ref, a2_ref, wd_ref, gd_ref, *refs, places):
    count = len(places)
    parts = refs[:count]
    sums_ref, da2_ref, keep_hbm, send_hbm = refs[count : count + 4]
    a2t, wu_units, wu_ref, du_ref, stage, sems = refs[count + 4 :]
    g = pl.program_id(0)
    last = pl.num_programs(0) - 1
    rows, chunk = du_ref.shape
    n, size, _ = wu_units.shape
    block = 256
    slot = lax.rem(g, 2)

    def sent(at, step):
        cols = pl.ds(pl.multiple_of(step * chunk, chunk), chunk)
        half = n // 2
        return [
            pltpu.make_async_copy(
                stage.at[at, pl.ds(i * half, half)], ref.at[:, :, cols], sems.at[at, i]
            )
            for i, ref in enumerate((keep_hbm, send_hbm))
        ]

    @pl.when(g == 0)
    def _():
        a2t[...] = jnp.transpose(a2_ref[...])
        da2_ref[...] = jnp.zeros_like(da2_ref)

    @pl.when(g >= 2)
    def _():
        for copy in sent(slot, g - 2):
            copy.wait()

    assemble(table_ref, parts, places, wu_units)
    flatten_units(wu_units, wu_ref)
    w_down = wd_ref[...].reshape(chunk, wd_ref.shape[2])
    total = jnp.zeros((1, chunk), F32)
    for i in range(rows // block):
        part = slice(i * block, (i + 1) * block)
        dh = dot_rt(dy_ref[part, :], w_down)
        du = (dh * gd_ref[part, :].astype(F32)).astype(BF)
        du_ref[part, :] = du
        total += jnp.sum(du.astype(F32), axis=0, keepdims=True)
        da2_ref[part, :] += dot_rt(du, wu_ref[...])
    sums_ref[...] = total
    for c in range(0, chunk, block):
        result = dot(a2t[...], du_ref[:, c : c + block])
        for d in range(n):
            place = table_ref[2 * n + d]
            stage[slot, place, :, c : c + block] = result[d * size : (d + 1) * size, :].astype(BF)
    for copy in sent(slot, g):
        copy.start()

    @pl.when(g == last)
    def _():
        for copy in sent(1 - slot, g - 1) + sent(slot, g):
            copy.wait()


def up_grad(table, dy, a2, w_down, gd, gathered, deps=()):
    parts, places = gathered
    rows, width = dy.shape
    hidden = gd.shape[1]
    n, deep, _ = w_down.shape
    size = width // n
    chunk = hidden // 4
    anywhere = pl.BlockSpec(memory_space=pl.ANY)
    shape = jax.ShapeDtypeStruct((n // 2, size, hidden), BF)
    once = lambda a: pl.BlockSpec(a.shape, lambda g: (0, 0), pipeline_mode=pl.Buffered(1))
    return call(
        functools.partial(up_grad_kernel, places=places),
        (table, dy, a2, w_down, gd, *parts),
        [
            pl.BlockSpec(memory_space=pltpu.SMEM),
            once(dy),
            once(a2),
            pl.BlockSpec((n // 4, deep, width), lambda g: (g, 0, 0)),
            pl.BlockSpec((rows, chunk), lambda g: (0, g)),
        ]
        + [
            pl.BlockSpec((p.shape[0], size, chunk), lambda g: (0, 0, width // chunk + g))
            for p in parts
        ],
        deps,
        grid=(hidden // chunk,),
        out_specs=[
            pl.BlockSpec((1, chunk), lambda g: (0, g)),
            pl.BlockSpec((rows, width), lambda g: (0, 0)),
            anywhere,
            anywhere,
        ],
        out_shape=[
            jax.ShapeDtypeStruct((1, hidden), F32),
            jax.ShapeDtypeStruct((rows, width), F32),
            shape,
            shape,
        ],
        scratch_shapes=[
            pltpu.VMEM((width, rows), BF),
            pltpu.VMEM((n, size, chunk), BF),
            pltpu.VMEM((width, chunk), BF),
            pltpu.VMEM((rows, chunk), BF),
            pltpu.VMEM((2, n, size, chunk), BF),
            pltpu.SemaphoreType.DMA((2, 2)),
        ],
        compiler_params=params(),
        cost_estimate=cost(6 * rows * width * hidden, 25e6),
        name="up_grad",
    )


def mid_back_kernel(
    table_ref,
    da2_ref,
    w_ref,
    mid_ref,
    dy_ref,
    ctx1_ref,
    ctx2_ref,
    vec_ref,
    dmid_ref,
    dctx_ref,
    sums_ref,
    keep_ref,
    send_ref,
    acc,
    *,
    core_bit,
):
    i = pl.program_id(0)
    da2 = da2_ref[...]
    normed, rs = norm_parts(mid_ref[...])
    dy = dy_ref[...].astype(F32)
    dmid = norm_back(normed, rs, vec_ref[4:5, :], da2) + dy
    dmid_ref[...] = dmid
    dbr = dmid.astype(BF)
    dctx_ref[...] = dot_rt(dbr, w_ref[...]).astype(BF)
    total = lambda v: jnp.sum(v, axis=0, keepdims=True)
    sums = jnp.concatenate(
        [
            total(dbr.astype(F32)),
            total(da2 * normed),
            total(da2),
            total(dy),
            jnp.zeros((4, dy.shape[1]), F32),
        ],
        axis=0,
    )
    part = dot_lt(jnp.concatenate([ctx1_ref[...], ctx2_ref[...]], axis=1), dbr)

    @pl.when(i == 0)
    def _():
        sums_ref[...] = sums
        acc[...] = part

    @pl.when(i > 0)
    def _():
        sums_ref[...] += sums
        acc[...] += part

    @pl.when(i == pl.num_programs(0) - 1)
    def _():
        store_units(table_ref, acc, keep_ref, send_ref, core_bit, put_rows, True)


def mid_back(table, da2, w_out, mid, dy, ctx, vec, n, core_bit, deps=()):
    rows, width = dy.shape
    unit = width // n
    block = 256
    by_rows = lambda m: pl.BlockSpec((block, m), lambda i: (i, 0))
    whole = lambda a: pl.BlockSpec(a.shape, lambda i: (0, 0))
    units = pl.BlockSpec((n // 2, unit, width), lambda i: (0, 0, 0))
    shape = jax.ShapeDtypeStruct((n // 2, unit, width), BF)
    return call(
        functools.partial(mid_back_kernel, core_bit=core_bit),
        (table, da2, w_out, mid, dy, *ctx, vec),
        [
            pl.BlockSpec(memory_space=pltpu.SMEM),
            by_rows(width),
            whole(w_out),
            by_rows(width),
            by_rows(width),
            *(by_rows(c.shape[1]) for c in ctx),
            whole(vec),
        ],
        deps,
        grid=(rows // block,),
        out_specs=[
            by_rows(width),
            by_rows(width),
            pl.BlockSpec((8, width), lambda i: (0, 0)),
            units,
            units,
        ],
        out_shape=[
            jax.ShapeDtypeStruct((rows, width), F32),
            jax.ShapeDtypeStruct((rows, width), BF),
            jax.ShapeDtypeStruct((8, width), F32),
            shape,
            shape,
        ],
        scratch_shapes=[pltpu.VMEM((width, width), F32)],
        compiler_params=params(),
        cost_estimate=cost(4 * rows * width * width, 16e6),
        name="mid_back",
    )


def token_grad_kernel(x_ref, *refs):
    *parts, w_ref, dmid_ref, vec_ref, grad_ref = refs
    dproj = jnp.concatenate([ref[...] for ref in parts], axis=1)
    da1 = dot_rt(dproj, w_ref[:, : dproj.shape[1]])
    normed, rs = norm_parts(x_ref[...].astype(F32))
    grad_ref[...] = dmid_ref[...] + norm_back(normed, rs, vec_ref[0:1, :], da1)


def token_grad(tokens, parts, w_in, dmid, vec, deps=()):
    rows, width = tokens.shape
    block = 256
    by_rows = lambda m: pl.BlockSpec((block, m), lambda i: (i, 0))
    whole = lambda a: pl.BlockSpec(a.shape, lambda i: (0, 0))
    return call(
        token_grad_kernel,
        (tokens, *parts, w_in, dmid, vec),
        [by_rows(width)]
        + [by_rows(p.shape[1]) for p in parts]
        + [whole(w_in), by_rows(width), whole(vec)],
        deps,
        grid=(rows // block,),
        out_specs=by_rows(width),
        out_shape=jax.ShapeDtypeStruct((rows, width), F32),
        compiler_params=params(),
        cost_estimate=cost(2 * rows * width * w_in.shape[1], 17e6),
        name="token_grad",
    )


def in_grad_kernel(table_ref, n1_hbm, w_hbm, *refs, starts):
    count = len(starts)
    parts, refs = refs[:count], refs[count:]
    s2_ref, c1_ref, keep_hbm, send_hbm, n1_ref, w_ref, grads_ref, stage, in_sems, out_sems = refs
    rows, width = n1_ref.shape
    n, size, wide = stage.shape
    vec_at = wide - LANES
    pieces = [(at, min(width, vec_at - at)) for at in range(0, vec_at, width)]
    loads = [pltpu.make_async_copy(n1_hbm, n1_ref, in_sems.at[0])]
    loads.append(
        pltpu.make_async_copy(
            w_hbm.at[:, pl.ds(vec_at, LANES)], w_ref.at[:, pl.ds(vec_at, LANES)], in_sems.at[1]
        )
    )
    wanted = []
    for at, extent in pieces:
        cols = pl.ds(at, extent)
        group = [
            pltpu.make_async_copy(
                ref,
                grads_ref.at[:, pl.ds(start, ref.shape[1])],
                in_sems.at[2 + len(pieces) + i],
            )
            for i, (ref, start) in enumerate(zip(parts, starts, strict=True))
            if at <= start < at + extent
        ]
        group.append(
            pltpu.make_async_copy(
                w_hbm.at[:, cols], w_ref.at[:, cols], in_sems.at[2 + len(wanted)]
            )
        )
        wanted.append(group)
    for copy in loads + [c for group in wanted for c in group]:
        copy.start()
    for copy in loads:
        copy.wait()
    turned = jnp.transpose(n1_ref[...])
    gain = w_ref[:, vec_at : vec_at + 1].astype(F32)
    shift = w_ref[:, vec_at + 1 : vec_at + 2].astype(F32)
    dgain = jnp.zeros((width, 1), F32)
    dshift = jnp.zeros((width, 1), F32)
    places = [table_ref[d] for d in range(n)]
    sent = []

    def store(result, at, extent):
        for d in range(n):
            stage[places[d], :, at : at + extent] = result[d * size : (d + 1) * size, :].astype(BF)
        for i, ref in enumerate((keep_hbm, send_hbm)):
            copy = pltpu.make_async_copy(
                stage.at[pl.ds(i * (n // 2), n // 2), :, pl.ds(at, extent)],
                ref.at[:, :, pl.ds(at, extent)],
                out_sems.at[len(sent)],
            )
            copy.start()
            sent.append(copy)

    query_sums = None
    for (at, extent), group in zip(pieces, wanted, strict=True):
        for copy in group:
            copy.wait()
        grads = grads_ref[:, at : at + extent]
        sums = jnp.sum(grads.astype(F32), axis=0, keepdims=True)
        if at == 0:
            query_sums = sums
        weights = w_ref[:, at : at + extent].astype(F32)
        product = dot(turned, grads)
        dgain += jnp.sum(weights * product, axis=1, keepdims=True)
        dshift += jnp.sum(weights * sums, axis=1, keepdims=True)
        store(gain * product + shift * sums, at, extent)
    hidden_rows = c1_ref.shape[1] // width
    stacked = jnp.concatenate(
        [jnp.zeros((2, width), F32), query_sums, s2_ref[0:4, :]]
        + [c1_ref[0:1, g * width : (g + 1) * width] for g in range(hidden_rows)]
        + [jnp.zeros((LANES - 7 - hidden_rows, width), F32)],
        axis=0,
    )
    lane = lanes_of((width, LANES))
    own = jnp.where(lane == 0, dgain, jnp.where(lane == 1, dshift, 0.0))
    store(jnp.transpose(stacked) + own, vec_at, LANES)
    for copy in sent:
        copy.wait()


def in_grad(table, n1, w_in, parts, starts, s2, c1, deps=()):
    rows, width = n1.shape
    wide = w_in.shape[1]
    n = (table.shape[0] - 1) // 4
    pieces = -(-(wide - LANES) // width)
    shape = jax.ShapeDtypeStruct((n // 2, width // n, wide), BF)
    vmem = pl.BlockSpec(memory_space=pltpu.VMEM)
    anywhere = pl.BlockSpec(memory_space=pl.ANY)
    return call(
        functools.partial(in_grad_kernel, starts=starts),
        (table, n1, w_in, *parts, s2, c1),
        [pl.BlockSpec(memory_space=pltpu.SMEM)]
        + [anywhere] * (2 + len(parts))
        + [vmem] * 2,
        deps,
        out_specs=[anywhere] * 2,
        out_shape=[shape, shape],
        scratch_shapes=[
            pltpu.VMEM((rows, width), BF),
            pltpu.VMEM((width, wide), BF),
            pltpu.VMEM((rows, wide - LANES), BF),
            pltpu.VMEM((n, width // n, wide), BF),
            pltpu.SemaphoreType.DMA((2 + pieces + len(parts),)),
            pltpu.SemaphoreType.DMA((2 * (pieces + 1),)),
        ],
        compiler_params=pltpu.CompilerParams(vmem_limit_bytes=VMEM_LIMIT),
        cost_estimate=cost(2 * rows * width * wide, 12e6),
        name="in_grad",
    )


def stages_of(n_dp, n_fsdp):
    fsdp_bits = n_fsdp.bit_length() - 1
    dp_bits = n_dp.bit_length() - 1
    low = list(range(fsdp_bits // 2))[::-1]
    high = list(range(fsdp_bits // 2, fsdp_bits))[::-1]
    z_bits = list(range(fsdp_bits + 1, fsdp_bits + dp_bits))[::-1]
    core = fsdp_bits
    return core, ([core] + high + low + z_bits, [core] + low + high + z_bits)


def place_table(n_dp, n_fsdp):
    core, orders = stages_of(n_dp, n_fsdp)
    n = n_dp * n_fsdp
    table = np.zeros((n, 4 * n + 1), np.int32)
    for me in range(n):
        for absolute in range(2):
            base = 2 * n * absolute
            for d in range(n):
                away = d ^ me
                place = 0
                for bit in orders[(d >> core) & 1]:
                    of = d if absolute and bit > core else away
                    place = place * 2 + ((of >> bit) & 1)
                table[me, base + d] = place
                table[me, base + n + place] = d
        table[me, 4 * n] = (me >> core) & 1
    return table


def tied_columns_kernel(*refs):
    *parts, out_ref = refs
    at, size = 0, parts[0].shape[0]
    for ref in parts:
        out_ref[:size, at : at + ref.shape[1]] = ref[...]
        at += ref.shape[1]
    if out_ref.shape[0] > size:
        out_ref[size:, :] = jnp.zeros((out_ref.shape[0] - size, at), BF)


def tied_columns(parts, deps, rows):
    vmem = pl.BlockSpec(memory_space=pltpu.VMEM)
    shape = (rows, sum(p.shape[1] for p in parts))
    return call(
        tied_columns_kernel,
        parts,
        [vmem] * len(parts),
        deps,
        out_specs=vmem,
        out_shape=jax.ShapeDtypeStruct(shape, BF),
        cost_estimate=cost(0, 4 * shape[0] * shape[1]),
        name="tied_columns",
    )


def after(value, deps):
    lost = False
    for dep in deps:
        one = lax.slice(dep, (0,) * dep.ndim, (1,) * dep.ndim).reshape(())
        lost = lost | (one != one)
    return jnp.where(lost, jnp.zeros_like(value), value)


def merge_kernel(*refs):
    *parts, out_ref = refs
    at = 0
    for ref in parts:
        out_ref[at : at + ref.shape[0]] = ref[:, : out_ref.shape[1]]
        at += ref.shape[0]


def merge(parts, deps, size=None):
    if not deps:
        return jnp.concatenate(parts, axis=0)
    vmem = pl.BlockSpec(memory_space=pltpu.VMEM)
    shape = (sum(p.shape[0] for p in parts), size or parts[0].shape[1], parts[0].shape[2])
    return call(
        merge_kernel,
        parts,
        [vmem] * len(parts),
        deps,
        out_specs=vmem,
        out_shape=jax.ShapeDtypeStruct(shape, BF),
        compiler_params=pltpu.CompilerParams(vmem_limit_bytes=VMEM_LIMIT),
        cost_estimate=cost(0, 4 * shape[0] * shape[1] * shape[2]),
        name="merge",
    )


class Exchange:
    def __init__(self, n_dp, n_fsdp):
        self.n = n_dp * n_fsdp
        self.count = self.n.bit_length() - 1
        self.core_bit, self.orders = stages_of(n_dp, n_fsdp)
        me = lax.axis_index("dp") * n_fsdp + lax.axis_index("fsdp")
        self.z = n_dp // 2
        self.z_groups = [list(range(c, n_dp, 2)) for c in range(2)]
        table = jnp.asarray(place_table(n_dp, n_fsdp))
        self.table = lax.dynamic_slice(table, (me, 0), (1, table.shape[1]))[0]

    def swap(self, value, stage):
        bits = [self.orders[(i >> self.core_bit) & 1][stage] for i in range(self.n)]
        return lax.ppermute(value, AXES, [(i, i ^ (1 << b)) for i, b in enumerate(bits)])

    def over_z(self, value, away):
        mask = away << (self.core_bit + 1)
        return lax.ppermute(value, AXES, [(i, i ^ mask) for i in range(self.n)])

    def over_plane(self, value, place):
        count = self.count - self.z.bit_length()

        def mask(core):
            bits = self.orders[core][1 : 1 + count]
            return sum(1 << b for k, b in enumerate(bits) if (place >> (count - 1 - k)) & 1)

        pairs = [(i, i ^ mask((i >> self.core_bit) & 1)) for i in range(self.n)]
        return lax.ppermute(value, AXES, pairs)

    def gather_z(self, rows, deps=()):
        held = rows[None]
        return merge([held] + [self.over_z(held, k) for k in range(1, self.z)], deps)

    def gather_plane(self, held, stage, deps=()):
        return merge((held, self.swap(held, stage)), deps)

    def with_core(self, parts, places):
        half = self.n // 2
        others = [self.swap(p, 0) for p in parts]
        return (
            tuple(parts) + tuple(others),
            tuple(places) + tuple(tuple(b + half for b in bases) for bases in places),
        )


class Halving:
    def __init__(self, exchange, keep, send):
        self.exchange, self.keep, self.send, self.stage = exchange, keep, send, 0

    def added(self, got, first, count):
        part = slice(first, first + count)
        return self.keep[part].astype(F32) + got[part].astype(F32)

    def step(self):
        got = self.exchange.swap(self.send, self.stage)
        self.stage += 1
        half = self.keep.shape[0] // 2
        self.keep, self.send = (self.added(got, k, half).astype(BF) for k in (0, half))
        return (self.send,)

    def to_plane(self):
        got = self.exchange.swap(self.send, 0)
        z = self.exchange.z
        self.keep = [
            self.added(got, k, z).astype(BF) for k in range(0, self.keep.shape[0], z)
        ]
        return tuple(self.keep)

    def plane(self, after):
        got = [self.exchange.over_plane(k, i) for i, k in enumerate(self.keep) if i]
        self.keep = combine([self.keep[0], *got], after)
        return tuple(self.keep)

    def ask(self):
        got = self.exchange.swap(self.send, self.stage)
        self.stage += 1
        return got

    def join(self, other):
        self.keep = jnp.concatenate([self.keep, other.keep], axis=2)
        self.send = jnp.concatenate([self.send, other.send], axis=2)
        return (self.send,)

    def last(self):
        self.got = tuple(self.exchange.over_z(k, i + 1) for i, k in enumerate(self.keep[1:]))
        return self.got

def join_along_z(wide, deep, exchange, deps):
    ins = (wide.keep, wide.ask(), deep.keep, deep.ask())
    z, size, columns = wide.keep.shape
    _, tall, width = deep.keep.shape
    blocks = columns // width

    def kernel(*refs):
        wide_ref, wide_came, deep_ref, deep_came, out_ref = refs
        total = (wide_ref[0].astype(F32) + wide_came[0].astype(F32)).astype(BF)
        for b in range(blocks):
            out_ref[0, b * size : (b + 1) * size, :] = total[:, b * width : (b + 1) * width]
        total = (deep_ref[0].astype(F32) + deep_came[0].astype(F32)).astype(BF)
        out_ref[0, blocks * size :, :] = total

    one = lambda *dims: pl.BlockSpec((1, *dims), lambda i: (i, 0, 0))
    rows = blocks * size + tall
    joined = call(
        kernel,
        ins,
        [one(size, columns)] * 2 + [one(tall, width)] * 2,
        deps,
        grid=(z,),
        out_specs=one(rows, width),
        out_shape=jax.ShapeDtypeStruct((z, rows, width), BF),
        compiler_params=params(),
        cost_estimate=cost(1e6, 5e6),
        name="join_along_z",
    )
    return joined, lax.psum_scatter(
        joined, "dp", scatter_dimension=0, tiled=True, axis_index_groups=exchange.z_groups
    )


def combine(parts, deps):
    count, size, width = parts[0].shape

    def kernel(*refs):
        ins, outs = refs[: len(parts)], refs[len(parts) :]
        for k, out in enumerate(outs):
            out[0] = sum(r[k].astype(F32) for r in ins).astype(BF)

    vmem = pl.BlockSpec(memory_space=pltpu.VMEM)
    shape = jax.ShapeDtypeStruct((1, size, width), BF)
    return call(
        kernel,
        parts,
        [vmem] * len(parts),
        deps,
        out_specs=[vmem] * count,
        out_shape=[shape] * count,
        compiler_params=pltpu.CompilerParams(vmem_limit_bytes=VMEM_LIMIT),
        cost_estimate=cost(len(parts) * count * size * width, 8 * count * size * width),
        name="combine",
    )


def finish(in_parts, others, cols, vrows, hidden, deps):
    size = in_parts[0].shape[1]
    width = others.shape[2]
    blocks = hidden // width
    tall = others.shape[1] - (blocks + 1) * size

    def kernel(*refs):
        *ins, others_ref, in_ref, vec_ref, out_ref, up_ref, down_ref = refs
        total = sum(r[0].astype(F32) for r in ins)
        in_ref[...] = total[:, :cols]
        table = jnp.concatenate([total[:, cols:], jnp.zeros((LANES - size, LANES), F32)], axis=0)
        vec_ref[...] = jnp.transpose(table)[:vrows, :size]
        for b in range(blocks):
            rows = others_ref[0, b * size : (b + 1) * size, :]
            up_ref[:, b * width : (b + 1) * width] = rows.astype(F32)
        at = blocks * size
        out_ref[...] = others_ref[0, at : at + size, :].astype(F32)
        down_ref[...] = others_ref[0, at + size :, :].astype(F32)

    vmem = pl.BlockSpec(memory_space=pltpu.VMEM)
    shape = lambda *dims: jax.ShapeDtypeStruct(dims, F32)
    return call(
        kernel,
        (*in_parts, others),
        [vmem] * (len(in_parts) + 1),
        deps,
        out_specs=[vmem] * 5,
        out_shape=[
            shape(size, cols),
            shape(vrows, size),
            shape(size, width),
            shape(size, hidden),
            shape(tall, width),
        ],
        cost_estimate=cost(1, 3e6),
        name="finish",
    )


def body(
    tokens, first_values, out_grad, lengths, in_proj, out_proj, up_proj, down_proj, vectors,
    *, n_dp, n_fsdp
):
    width = tokens.shape[1]
    cols = in_proj.shape[1]
    vrows = vectors.shape[0]
    exchange = Exchange(n_dp, n_fsdp)
    n, core_bit, table = exchange.n, exchange.core_bit, exchange.table

    z = exchange.z
    planes = exchange.count - z.bit_length()
    quarter = n // 8

    vec_t = jnp.pad(vectors.T, ((0, 0), (0, LANES - vrows)))
    held = exchange.gather_z(jnp.concatenate([in_proj, vec_t], axis=1))
    early = tied_columns((out_proj, up_proj), (held, table), out_proj.shape[0])[None]
    others = [exchange.over_z(early, k) for k in range(1, z)]
    if planes == 2:
        got_a, got_b = exchange.swap(held, 1), exchange.swap(held, 2)
        got_ba = exchange.swap(merge((got_a,), tuple(others)), 2)
        in_parts = exchange.with_core(
            (held, got_b, got_a, got_ba), tuple((q * quarter,) for q in range(4))
        )
    else:
        for stage in range(planes, 0, -1):
            held = exchange.gather_plane(held, stage)
        in_parts = exchange.with_core((held,), ((0,),))

    w_down = lax.all_gather(down_proj, AXES, axis=0, tiled=False)
    half = width // LANES // 2
    held_mid = jnp.concatenate([early, *others], axis=0)
    w_in, n1, qkv, vec = in_forward(table, tokens, first_values, in_parts, (held_mid,))
    for stage in range(planes, 1, -1):
        held_mid = exchange.gather_plane(held_mid, stage, (n1,))
    ctx1, ctx2, lse1, lse2 = attn_forward(lengths, qkv, width, (held_mid,))
    got_mid = after(exchange.swap(held_mid, 1), (ctx1,))
    mid_parts = exchange.with_core((held_mid, got_mid), ((0,), (n // 4,)))
    ctx = (ctx1, ctx2)
    act, gd, mid, a2, w_out, *halves = ffn_forward(
        table, ctx, tokens, out_grad, vec, mid_parts, core_bit
    )
    h_down = Halving(exchange, *halves)
    deps = h_down.step()
    dc1, da2, *halves = up_grad(table, out_grad, a2, w_down, gd, mid_parts, deps)
    h_up = Halving(exchange, *halves)
    deps = h_down.step()
    dmid, dctx, sums2, *halves = mid_back(
        table, da2, w_out, mid, out_grad, ctx, vec, n, core_bit, deps
    )
    h_out = Halving(exchange, *halves)
    h_up.step()
    h_out.step()
    deps = h_up.join(h_out)
    dq1, dk1, dv1 = attn_backward(lengths, lse1, qkv, ctx1, dctx, 0, half, BF, deps)
    for _ in range(planes - 2):
        h_down.step(), h_up.step()
    deps = h_up.step() + (dq1,)
    h_down.send = merge((h_down.send,), (dq1,))
    dq2, dk2, first_grad = attn_backward(
        lengths, lse2, qkv, ctx2, dctx, half, half, F32, deps
    )
    joined, others = join_along_z(h_up, h_down, exchange, (dq2,))
    deps = (joined,)
    split = half * LANES
    parts = (dq1, dq2, dk1, dk2, dv1)
    starts = (0, split, width, width + split, 2 * width)
    h_in = Halving(
        exchange, *in_grad(table, n1, w_in, parts, starts, sums2, dc1, deps)
    )
    deps = h_in.to_plane()
    input_grad = token_grad(tokens, parts, w_in, dmid, vec, deps)
    first = out_forward(act, mid, w_down, vec, 0, (), deps + (input_grad,))
    deps = h_in.plane((first,))
    output = out_forward(act, mid, w_down, vec, 1, (first,), deps + (others,))
    g_in, g_vec, g_out, g_up, g_down = finish(
        (h_in.keep[0], *h_in.last()), others, cols, vrows, up_proj.shape[1], (output,)
    )
    return (output, input_grad, first_grad, g_in, g_out, g_up, g_down, g_vec)


def solution(mesh):
    rows = P(AXES, None)
    cols = P(None, AXES)
    return jax.shard_map(
        functools.partial(body, n_dp=mesh.shape["dp"], n_fsdp=mesh.shape["fsdp"]),
        mesh=mesh,
        in_specs=(rows,) * 8 + (cols,),
        out_specs=(rows,) * 7 + (cols,),
        check_vma=False,
    )
```

```python
import functools

import jax
import jax.numpy as jnp
import numpy as np
from jax import lax
from jax.experimental import pallas as pl
from jax.experimental.pallas import tpu as pltpu
from jax.sharding import PartitionSpec as P

H = 12
HD = 64
EPS = 1e-05
NEG = -1000000000.0
LANES = 128
AXES = ("dp", "fsdp")
BF = jnp.bfloat16
F32 = jnp.float32
VMEM_LIMIT = 56 * 1024 * 1024
SMALL_LIMIT = 16 * 1024 * 1024
GELU_C = 0.7978845608028654
GELU_A = 0.044715


def dot(a, b):
    return lax.dot_general(a, b, (((1,), (0,)), ((), ())), preferred_element_type=F32)


def dot_rt(a, b):
    return lax.dot_general(a, b, (((1,), (1,)), ((), ())), preferred_element_type=F32)


def dot_lt(a, b):
    return lax.dot_general(a, b, (((0,), (0,)), ((), ())), preferred_element_type=F32)


def params(grid_rank=1):
    return pltpu.CompilerParams(
        vmem_limit_bytes=VMEM_LIMIT, dimension_semantics=("arbitrary",) * grid_rank
    )


def cost(flops, nbytes, trans=0):
    return pl.CostEstimate(flops=int(flops), bytes_accessed=int(nbytes), transcendentals=int(trans))


def call(kernel, ins, in_specs, deps=(), **kw):
    count, extra = len(ins), len(deps)

    def run(*refs):
        kernel(*refs[:count], *refs[count + extra :])

    specs = list(in_specs) + [pl.BlockSpec(memory_space=pl.ANY)] * extra
    return pl.pallas_call(run, in_specs=specs, **kw)(*ins, *deps)


def norm_parts(values):
    centred = values - jnp.mean(values, axis=-1, keepdims=True)
    spread = jnp.mean(centred * centred, axis=-1, keepdims=True)
    rs = lax.rsqrt(spread + EPS)
    return centred * rs, rs


def norm_back(normed, rs, gain, grad):
    scaled = grad * gain
    m1 = jnp.mean(scaled, axis=-1, keepdims=True)
    m2 = jnp.mean(scaled * normed, axis=-1, keepdims=True)
    return rs * (scaled - m1 - normed * m2)


def assemble(table_ref, refs, places, whole_ref):
    n = whole_ref.shape[0]
    for ref, bases in zip(refs, places, strict=True):
        each = ref.shape[0] // len(bases)
        for b, base in enumerate(bases):
            for k in range(each):
                whole_ref[table_ref[n + base + k]] = ref[b * each + k]


def flatten_units(units_ref, matrix_ref):
    size = units_ref.shape[1]
    for d in range(units_ref.shape[0]):
        matrix_ref[d * size : (d + 1) * size, :] = units_ref[d]


def const_spec(a):
    rank = len(a.shape)
    return pl.BlockSpec(a.shape, lambda *_: (0,) * rank)


def in_kernel(table_ref, x_ref, fv_ref, *refs, places):
    *parts, w_hbm, n1_ref, qkv_ref, vec_ref, units_ref, w_ref, sem = refs
    width = x_ref.shape[1]
    cols = w_ref.shape[1] - LANES
    copy = pltpu.make_async_copy(w_ref, w_hbm, sem)

    @pl.when(pl.program_id(0) == 0)
    def _():
        assemble(table_ref, parts, places, units_ref)
        flatten_units(units_ref, w_ref)
        copy.start()
        turned = jnp.transpose(w_ref[:, cols:].astype(F32))
        vec_ref[...] = turned[: vec_ref.shape[0]]

    normed, _ = norm_parts(x_ref[...].astype(F32))
    a1 = (normed * vec_ref[0:1, :] + vec_ref[1:2, :]).astype(BF)
    n1_ref[...] = normed.astype(BF)
    proj = dot(a1, w_ref[:, :cols])
    queries = (proj[:, :width] + vec_ref[2:3, :]).astype(BF)
    qkv_ref[:, :width] = queries * jnp.asarray(HD**-0.5, BF)
    qkv_ref[:, width:cols] = proj[:, width:].astype(BF)
    qkv_ref[:, cols:] = fv_ref[...]

    @pl.when(pl.program_id(0) == pl.num_programs(0) - 1)
    def _():
        copy.wait()


def in_forward(table, tokens, first_values, gathered, deps=()):
    parts, places = gathered
    rows, width = tokens.shape
    half = first_values.shape[1]
    _, size, wide = parts[0].shape
    n = width // size
    block = 256
    by_rows = lambda m: pl.BlockSpec((block, m), lambda i: (i, 0))
    const = lambda *shape: pl.BlockSpec(shape, lambda i: (0, 0))
    return call(
        functools.partial(in_kernel, places=places),
        (table, tokens, first_values, *parts),
        [pl.BlockSpec(memory_space=pltpu.SMEM), by_rows(width), by_rows(half)]
        + [const_spec(p) for p in parts],
        deps,
        grid=(rows // block,),
        out_specs=[
            pl.BlockSpec(memory_space=pl.ANY),
            by_rows(width),
            by_rows(wide - LANES + half),
            const(16, width),
        ],
        out_shape=[
            jax.ShapeDtypeStruct((width, wide), BF),
            jax.ShapeDtypeStruct((rows, width), BF),
            jax.ShapeDtypeStruct((rows, wide - LANES + half), BF),
            jax.ShapeDtypeStruct((16, width), F32),
        ],
        scratch_shapes=[
            pltpu.VMEM((n, size, wide), BF),
            pltpu.VMEM((width, wide), BF),
            pltpu.SemaphoreType.DMA(()),
        ],
        compiler_params=params(),
        cost_estimate=cost(2 * rows * width * wide, 16e6),
        name="in_forward",
    )


def lanes_of(shape):
    return lax.broadcasted_iota(jnp.int32, shape, 1)


def own_lanes(e, shape):
    lane = lanes_of(shape)
    return (lane < HD) if e == 0 else (lane >= HD)


def spare(e):
    return HD if e == 0 else 0


def split3(values):
    hi = values.astype(BF).astype(F32)
    rest = values - hi
    mid = rest.astype(BF).astype(F32)
    return hi, mid, rest - mid


def augmented(vectors, e, lane, seg, filled):
    aux = jnp.where((lane == spare(e)) & seg, filled, 0.0)
    return jnp.where(own_lanes(e, lane.shape), vectors, aux).astype(BF)


def causal(block):
    rows = lax.broadcasted_iota(jnp.int32, (block, block), 0)
    return rows <= lax.broadcasted_iota(jnp.int32, (block, block), 1)


def scores_of(keys, queries, tri, lo):
    s = dot_rt(keys, queries)
    diag = jnp.where(tri, s[lo:, :], NEG)
    return diag if lo == 0 else jnp.concatenate([s[:lo, :], diag], axis=0)


def attn_fwd_kernel(bound_ref, q_ref, k_ref, v_ref, ctx_ref, lse_ref):
    rows = q_ref.shape[0]
    block = 256
    bound = bound_ref[0, 0]
    shape = (rows, LANES)
    lane = lanes_of(shape)
    place = lax.broadcasted_iota(jnp.int32, shape, 0)
    k_all = k_ref[...].astype(F32)
    q_all = q_ref[...].astype(F32)
    values = jnp.concatenate([v_ref[...], jnp.ones(shape, BF)], axis=1)
    tri = causal(block)
    ctxs = [[None, None] for _ in range(rows // block)]
    k_augs = [augmented(k_all, e, lane, place < bound, 1.0) for e in range(2)]
    q_augs = [augmented(q_all, e, lane, place >= bound, NEG) for e in range(2)]
    chains = [(j, e) for j in range(rows // block) for e in range(2)]

    def scores(j, e):
        lo, hi = j * block, (j + 1) * block
        return scores_of(k_augs[e][:hi, :], q_augs[e][lo:hi, :], tri, lo)

    def weighted(j, e, p):
        o = dot_lt(p, values[: (j + 1) * block, :])
        ctxs[j][e] = o[:, :LANES] / o[:, LANES:]

    following = scores(*chains[0])
    waiting = None
    for i, (j, e) in enumerate(chains):
        s = following
        if i + 1 < len(chains):
            following = scores(*chains[i + 1])
        peak = jnp.max(s, axis=0, keepdims=True)
        p = jnp.exp(s - peak)
        lse = peak + jnp.log(jnp.sum(p, axis=0, keepdims=True))
        lse_ref[0, e : e + 1, j * block : (j + 1) * block] = lse
        if waiting is not None:
            weighted(*waiting)
        waiting = (j, e, p.astype(BF))
    weighted(*waiting)
    first = lanes_of((block, LANES)) < HD
    for j in range(rows // block):
        ctx_ref[j * block : (j + 1) * block, :] = jnp.where(first, *ctxs[j]).astype(BF)


def attn_forward(lengths, qkv, width, deps=()):
    rows = qkv.shape[0]
    pairs = width // LANES
    half = pairs // 2
    slab = lambda off: pl.BlockSpec((rows, LANES), lambda j: (0, off + j))

    def kernel(bound_ref, q_ref, k_ref, v_ref, ctx1_ref, ctx2_ref, lse1_ref, lse2_ref, ctx_ref, lse_ref):
        attn_fwd_kernel(bound_ref, q_ref, k_ref, v_ref, ctx_ref, lse_ref)
        for k, (ctx, lse) in enumerate(((ctx1_ref, lse1_ref), (ctx2_ref, lse2_ref))):

            @pl.when(pl.program_id(0) // half == k)
            def _(ctx=ctx, lse=lse):
                ctx[...] = ctx_ref[...]
                lse[...] = lse_ref[...]

    first = lambda j: jnp.minimum(j, half - 1)
    second = lambda j: jnp.maximum(j - half, 0)
    ctx_spec = lambda of: pl.BlockSpec((rows, LANES), lambda j: (0, of(j)))
    lse_spec = lambda of: pl.BlockSpec((1, 8, rows), lambda j: (of(j), 0, 0))
    ctx_shape = jax.ShapeDtypeStruct((rows, half * LANES), BF)
    lse_shape = jax.ShapeDtypeStruct((half, 8, rows), F32)
    return call(
        kernel,
        (lengths, qkv, qkv, qkv),
        [pl.BlockSpec(memory_space=pltpu.SMEM), *(slab(c * pairs) for c in range(3))],
        deps,
        grid=(pairs,),
        out_specs=[ctx_spec(first), ctx_spec(second), lse_spec(first), lse_spec(second)],
        out_shape=[ctx_shape, ctx_shape, lse_shape, lse_shape],
        scratch_shapes=[pltpu.VMEM((rows, LANES), BF), pltpu.VMEM((1, 8, rows), F32)],
        compiler_params=params(),
        cost_estimate=cost(2 * 2 * rows * rows * 256 * H * 0.63, 9e6, rows * rows * H),
        name="attn_forward",
    )


def attn_bwd_kernel(
    bound_ref, lse_ref, q_ref, k_ref, v_ref, ctx_ref, do_ref, dq_ref, dk_ref, dv_ref, dk_acc, dv_acc
):
    rows = k_ref.shape[0]
    block = 256
    bound = bound_ref[0, 0]
    full = (rows, LANES)
    lane = lanes_of(full)
    place = lax.broadcasted_iota(jnp.int32, full, 0)
    q_all = q_ref[...].astype(F32)
    k_all = k_ref[...].astype(F32)
    v_all = v_ref[...].astype(F32)
    do_all = do_ref[...].astype(F32)
    prod = do_all * ctx_ref[...].astype(F32)
    tri = causal(block)
    dqs = [[None, None] for _ in range(rows // block)]
    k_augs, q_augs, v_augs, do_augs = [], [], [], []
    for e in range(2):
        sp = spare(e)
        own = own_lanes(e, full)
        three = (lane >= sp + 1) & (lane <= sp + 3)
        k_augs.append(augmented(k_all, e, lane, place < bound, 1.0))
        q_augs.append(augmented(q_all, e, lane, place >= bound, NEG))
        v_augs.append(jnp.where(own, v_all, jnp.where(three, 1.0, 0.0)).astype(BF))
        delta = jnp.sum(jnp.where(own, prod, 0.0), axis=-1, keepdims=True)
        d_hi, d_mid, d_lo = split3(-delta)
        do_augs.append(
            jnp.where(
                own,
                do_all,
                jnp.where(
                    lane == sp + 1,
                    d_hi,
                    jnp.where(lane == sp + 2, d_mid, jnp.where(lane == sp + 3, d_lo, 0.0)),
                ),
            ).astype(BF)
        )
    chains = [(j, e) for j in reversed(range(rows // block)) for e in range(2)]

    def products(j, e):
        lo, hi = j * block, (j + 1) * block
        s = scores_of(k_augs[e][:hi, :], q_augs[e][lo:hi, :], tri, lo)
        return s, dot_rt(v_augs[e][:hi, :], do_augs[e][lo:hi, :])

    def finish_chain(j, e, p, ds):
        lo, hi = j * block, (j + 1) * block
        dv_j = dot(p, do_augs[e][lo:hi, :])
        dk_j = dot(ds, q_augs[e][lo:hi, :])
        if j == rows // block - 1:
            dv_acc[e] = dv_j
            dk_acc[e] = dk_j
        else:
            dv_acc[e, :hi, :] += dv_j
            dk_acc[e, :hi, :] += dk_j
        dqs[j][e] = dot_lt(ds, k_augs[e][:hi, :])

    following = products(*chains[0])
    for i, (j, e) in enumerate(chains):
        s, dp = following
        if i + 1 < len(chains):
            following = products(*chains[i + 1])
        p = jnp.exp(s - lse_ref[0, e : e + 1, j * block : (j + 1) * block])
        finish_chain(j, e, p.astype(BF), (p * dp).astype(BF))
    first = lanes_of((block, LANES)) < HD
    for j in range(rows // block):
        dq_ref[j * block : (j + 1) * block, :] = (jnp.where(first, *dqs[j]) * HD**-0.5).astype(BF)
    dk_ref[...] = jnp.where(lane < HD, dk_acc[0], dk_acc[1]).astype(BF)
    dv_ref[...] = jnp.where(lane < HD, dv_acc[0], dv_acc[1]).astype(dv_ref.dtype)


def attn_backward(lengths, lse, qkv, ctx, dctx, first, count, dv_type, deps=()):
    rows, width = dctx.shape
    pairs = width // LANES
    slab = lambda off: pl.BlockSpec((rows, LANES), lambda j, off=off: (0, off + j))
    shape = lambda dtype: jax.ShapeDtypeStruct((rows, count * LANES), dtype)
    return call(
        attn_bwd_kernel,
        (lengths, lse, qkv, qkv, qkv, ctx, dctx),
        [
            pl.BlockSpec(memory_space=pltpu.SMEM),
            pl.BlockSpec((1, 8, rows), lambda j: (j, 0, 0)),
            slab(first),
            slab(pairs + first),
            slab(2 * pairs + first),
            slab(0),
            slab(first),
        ],
        deps,
        grid=(count,),
        out_specs=[slab(0)] * 3,
        out_shape=[shape(BF), shape(BF), shape(dv_type)],
        scratch_shapes=[
            pltpu.VMEM((2, rows, LANES), F32),
            pltpu.VMEM((2, rows, LANES), F32),
        ],
        compiler_params=params(),
        cost_estimate=cost(5 * 2 * rows * rows * 256 * 2 * count * 0.63, 15e6, rows * rows * 2 * count),
        name="attn_backward",
    )


def gelu_half(u, u2):
    return 0.5 + 0.5 * jnp.tanh(u * (GELU_C + (GELU_C * GELU_A) * u2))


def gelu_slope(u):
    u2 = u * u
    half = gelu_half(u, u2)
    act = u * half
    return half + (act - act * half) * (2.0 * GELU_C + (6.0 * GELU_C * GELU_A) * u2)


def ffn_kernel(
    table_ref, ctx1_ref, ctx2_ref, x_ref, dy_ref, vec_ref, *refs, places, core_bit
):
    count = len(places)
    out_parts, up_parts = refs[:count], refs[count : 2 * count]
    u_ref, mid_hbm, a2_hbm, wo_hbm, keep_hbm, send_hbm = refs[2 * count : 2 * count + 6]
    wo_units, wu_units, wo_ref, wu_ref, mid_ref, a2_ref, act_ref, stage, once_sems, sems = refs[
        2 * count + 6 :
    ]
    g = pl.program_id(0)
    last = pl.num_programs(0) - 1
    rows, width = x_ref.shape
    chunk = act_ref.shape[1]
    n = wu_units.shape[0]
    block = 256
    once = (
        pltpu.make_async_copy(mid_ref, mid_hbm, once_sems.at[0]),
        pltpu.make_async_copy(a2_ref, a2_hbm, once_sems.at[1]),
        pltpu.make_async_copy(wo_ref, wo_hbm, once_sems.at[2]),
    )

    @pl.when(g == 0)
    def _():
        assemble(table_ref, out_parts, places, wo_units)
        flatten_units(wo_units, wo_ref)
        for i in range(rows // block):
            part = slice(i * block, (i + 1) * block)
            ctx = jnp.concatenate([ctx1_ref[part, :], ctx2_ref[part, :]], axis=1)
            branch = dot(ctx, wo_ref[...]) + vec_ref[3:4, :]
            mid = x_ref[part, :].astype(F32) + branch
            mid_ref[part, :] = mid
            normed, _ = norm_parts(mid)
            a2_ref[part, :] = (normed * vec_ref[4:5, :] + vec_ref[5:6, :]).astype(BF)
        for copy in once:
            copy.start()

    assemble(table_ref, up_parts, places, wu_units)
    flatten_units(wu_units, wu_ref)
    per_row = width // chunk
    row = vec_ref[pl.ds(7 + g // per_row, 1), :]
    bias = row[:, :chunk]
    for c in range(1, per_row):
        bias = jnp.where(g % per_row == c, row[:, c * chunk : (c + 1) * chunk], bias)
    for i in range(rows // block):
        part = slice(i * block, (i + 1) * block)
        u = dot(a2_ref[part, :], wu_ref[...]) + bias
        u_ref[part, :] = u.astype(BF)
        act_ref[part, :] = (u * gelu_half(u, u * u)).astype(BF)
    result = dot_lt(act_ref[...], dy_ref[...])
    units = stage.shape[1]
    size = chunk // units
    slot = lax.rem(g, 2)
    mine = table_ref[4 * n]
    sent = lambda at, i: pltpu.make_async_copy(stage.at[at, i], keep_hbm.at[0], sems.at[at, i])

    @pl.when(g >= 2)
    def _():
        for i in range(units):
            sent(slot, i).wait()

    for i in range(units):
        stage[slot, i] = result[i * size : (i + 1) * size, :].astype(BF)
        d = g * units + i
        place = table_ref[2 * n + d]
        core = lax.rem(lax.shift_right_logical(d, core_bit), 2)

        @pl.when(core == mine)
        def _(i=i, place=place):
            pltpu.make_async_copy(stage.at[slot, i], keep_hbm.at[place], sems.at[slot, i]).start()

        @pl.when(core != mine)
        def _(i=i, place=place):
            pltpu.make_async_copy(
                stage.at[slot, i], send_hbm.at[place - n // 2], sems.at[slot, i]
            ).start()

    @pl.when(g == last)
    def _():
        for copy in once:
            copy.wait()
        for i in range(units):
            sent(1 - slot, i).wait()
            sent(slot, i).wait()


def ffn_forward(table, ctx, tokens, dy, vec, gathered, core_bit, deps=()):
    parts, places = gathered
    rows, width = tokens.shape
    _, size, wide = parts[0].shape
    hidden = wide - width
    n = width // size
    chunk = hidden // 4
    unit = hidden // n
    anywhere = pl.BlockSpec(memory_space=pl.ANY)
    halves = jax.ShapeDtypeStruct((n // 2, unit, width), BF)
    return call(
        functools.partial(ffn_kernel, places=places, core_bit=core_bit),
        (table, *ctx, tokens, dy, vec, *parts, *parts),
        [pl.BlockSpec(memory_space=pltpu.SMEM)]
        + [
            pl.BlockSpec(a.shape, lambda g: (0, 0), pipeline_mode=pl.Buffered(1))
            for a in (*ctx, tokens, dy, vec)
        ]
        + [
            pl.BlockSpec(
                (p.shape[0], size, width), lambda g: (0, 0, 0), pipeline_mode=pl.Buffered(1)
            )
            for p in parts
        ]
        + [
            pl.BlockSpec((p.shape[0], size, chunk), lambda g: (0, 0, width // chunk + g))
            for p in parts
        ],
        deps,
        grid=(hidden // chunk,),
        out_specs=[pl.BlockSpec((rows, chunk), lambda g: (0, g))] + [anywhere] * 5,
        out_shape=[
            jax.ShapeDtypeStruct((rows, hidden), BF),
            jax.ShapeDtypeStruct((rows, width), F32),
            jax.ShapeDtypeStruct((rows, width), BF),
            jax.ShapeDtypeStruct((width, width), BF),
            halves,
            halves,
        ],
        scratch_shapes=[
            pltpu.VMEM((n, size, width), BF),
            pltpu.VMEM((n, size, chunk), BF),
            pltpu.VMEM((width, width), BF),
            pltpu.VMEM((width, chunk), BF),
            pltpu.VMEM((rows, width), F32),
            pltpu.VMEM((rows, width), BF),
            pltpu.VMEM((rows, chunk), BF),
            pltpu.VMEM((2, n // 4, unit, width), BF),
            pltpu.SemaphoreType.DMA((3,)),
            pltpu.SemaphoreType.DMA((2, n // 4)),
        ],
        compiler_params=params(),
        cost_estimate=cost(2 * rows * width * (wide + hidden), 40e6, rows * hidden),
        name="ffn_forward",
    )


def out_kernel(u_ref, mid_ref, wd_ref, vec_ref, *refs):
    out_ref = refs[-1]
    u = u_ref[...].astype(F32)
    act = (u * gelu_half(u, u * u)).astype(BF)
    w_down = wd_ref[...].reshape(-1, wd_ref.shape[2])
    out_ref[...] = mid_ref[...] + dot(act, w_down) + vec_ref[6:7, :]


def out_forward(u, mid, w_down, vec, half, into=(), deps=()):
    rows, width = mid.shape
    hidden = u.shape[1]
    block = 256
    steps = rows // block // 2
    by_rows = lambda n: pl.BlockSpec((block, n), lambda i: (i + half * steps, 0))
    whole = lambda a: pl.BlockSpec(a.shape, lambda i: (0, 0))
    return call(
        out_kernel,
        (u, mid, w_down, vec, *into),
        [by_rows(hidden), by_rows(width), const_spec(w_down), whole(vec)]
        + [pl.BlockSpec(memory_space=pl.ANY)] * len(into),
        deps,
        grid=(steps,),
        out_specs=by_rows(width),
        out_shape=jax.ShapeDtypeStruct((rows, width), F32),
        input_output_aliases={4: 0} if into else {},
        compiler_params=params(),
        cost_estimate=cost(rows * width * hidden, 12e6),
        name="out_forward",
    )


def store_units(table_ref, result, keep_ref, send_ref, core_bit, put, absolute):
    half = keep_ref.shape[0]
    units = 2 * half
    size = result.shape[0] // units
    for mine in range(2):

        @pl.when(table_ref[4 * units] == mine)
        def _(mine=mine):
            for d in range(units):
                i = d
                place = table_ref[d + 2 * units * absolute]
                rows = result[i * size : (i + 1) * size, :].astype(BF)
                if ((d >> core_bit) & 1) == mine:
                    put(keep_ref, place, rows)
                else:
                    put(send_ref, place - half, rows)


def put_rows(ref, place, rows):
    ref[place] = rows


def up_grad_kernel(table_ref, dy_ref, a2_ref, wd_ref, u_ref, *refs, places):
    count = len(places)
    parts = refs[:count]
    sums_ref, da2_ref, keep_hbm, send_hbm = refs[count : count + 4]
    a2t, wu_units, wu_ref, du_ref, stage, sems = refs[count + 4 :]
    g = pl.program_id(0)
    last = pl.num_programs(0) - 1
    rows, chunk = du_ref.shape
    n, size, _ = wu_units.shape
    block = 256
    slot = lax.rem(g, 2)

    def sent(at, step):
        cols = pl.ds(pl.multiple_of(step * chunk, chunk), chunk)
        half = n // 2
        return [
            pltpu.make_async_copy(
                stage.at[at, pl.ds(i * half, half)], ref.at[:, :, cols], sems.at[at, i]
            )
            for i, ref in enumerate((keep_hbm, send_hbm))
        ]

    @pl.when(g == 0)
    def _():
        a2t[: a2_ref.shape[1], :] = jnp.transpose(a2_ref[...])
        a2t[a2_ref.shape[1] :, :] = jnp.ones((16, rows), BF)
        da2_ref[...] = jnp.zeros_like(da2_ref)

    @pl.when(g >= 2)
    def _():
        for copy in sent(slot, g - 2):
            copy.wait()

    assemble(table_ref, parts, places, wu_units)
    flatten_units(wu_units, wu_ref)
    w_down = wd_ref[...].reshape(chunk, wd_ref.shape[2])
    for i in range(rows // block):
        part = slice(i * block, (i + 1) * block)
        dh = dot_rt(dy_ref[part, :], w_down)
        du = (dh * gelu_slope(u_ref[part, :].astype(F32))).astype(BF)
        du_ref[part, :] = du
        da2_ref[part, :] += dot_rt(du, wu_ref[...])
    for c in range(0, chunk, block):
        result = dot(a2t[...], du_ref[:, c : c + block])
        sums_ref[:, c : c + block] = result[n * size : n * size + 1, :]
        for d in range(n):
            place = table_ref[2 * n + d]
            stage[slot, place, :, c : c + block] = result[d * size : (d + 1) * size, :].astype(BF)
    for copy in sent(slot, g):
        copy.start()

    @pl.when(g == last)
    def _():
        for copy in sent(1 - slot, g - 1) + sent(slot, g):
            copy.wait()


def up_grad(table, dy, a2, w_down, u, gathered, deps=()):
    parts, places = gathered
    rows, width = dy.shape
    hidden = u.shape[1]
    n, deep, _ = w_down.shape
    size = width // n
    chunk = hidden // 4
    anywhere = pl.BlockSpec(memory_space=pl.ANY)
    shape = jax.ShapeDtypeStruct((n // 2, size, hidden), BF)
    once = lambda a: pl.BlockSpec(a.shape, lambda g: (0, 0), pipeline_mode=pl.Buffered(1))
    return call(
        functools.partial(up_grad_kernel, places=places),
        (table, dy, a2, w_down, u, *parts),
        [
            pl.BlockSpec(memory_space=pltpu.SMEM),
            once(dy),
            once(a2),
            pl.BlockSpec((n // 4, deep, width), lambda g: (g, 0, 0)),
            pl.BlockSpec((rows, chunk), lambda g: (0, g)),
        ]
        + [
            pl.BlockSpec((p.shape[0], size, chunk), lambda g: (0, 0, width // chunk + g))
            for p in parts
        ],
        deps,
        grid=(hidden // chunk,),
        out_specs=[
            pl.BlockSpec((1, chunk), lambda g: (0, g)),
            pl.BlockSpec((rows, width), lambda g: (0, 0)),
            anywhere,
            anywhere,
        ],
        out_shape=[
            jax.ShapeDtypeStruct((1, hidden), F32),
            jax.ShapeDtypeStruct((rows, width), F32),
            shape,
            shape,
        ],
        scratch_shapes=[
            pltpu.VMEM((width + 16, rows), BF),
            pltpu.VMEM((n, size, chunk), BF),
            pltpu.VMEM((width, chunk), BF),
            pltpu.VMEM((rows, chunk), BF),
            pltpu.VMEM((2, n, size, chunk), BF),
            pltpu.SemaphoreType.DMA((2, 2)),
        ],
        compiler_params=params(),
        cost_estimate=cost(6 * rows * width * hidden, 25e6),
        name="up_grad",
    )


def mid_back_kernel(
    table_ref,
    da2_ref,
    w_ref,
    mid_ref,
    dy_ref,
    ctx1_ref,
    ctx2_ref,
    vec_ref,
    dmid_ref,
    dctx_ref,
    sums_ref,
    keep_ref,
    send_ref,
    acc,
    *,
    core_bit,
):
    i = pl.program_id(0)
    da2 = da2_ref[...]
    normed, rs = norm_parts(mid_ref[...])
    dy = dy_ref[...].astype(F32)
    dmid = norm_back(normed, rs, vec_ref[4:5, :], da2) + dy
    dmid_ref[...] = dmid
    dbr = dmid.astype(BF)
    dctx_ref[...] = dot_rt(dbr, w_ref[...]).astype(BF)
    total = lambda v: jnp.sum(v, axis=0, keepdims=True)
    sums = jnp.concatenate(
        [
            total(dbr.astype(F32)),
            total(da2 * normed),
            total(da2),
            total(dy),
            jnp.zeros((4, dy.shape[1]), F32),
        ],
        axis=0,
    )
    part = dot_lt(jnp.concatenate([ctx1_ref[...], ctx2_ref[...]], axis=1), dbr)

    @pl.when(i == 0)
    def _():
        sums_ref[...] = sums
        acc[...] = part

    @pl.when(i > 0)
    def _():
        sums_ref[...] += sums
        acc[...] += part

    @pl.when(i == pl.num_programs(0) - 1)
    def _():
        store_units(table_ref, acc, keep_ref, send_ref, core_bit, put_rows, True)


def mid_back(table, da2, w_out, mid, dy, ctx, vec, n, core_bit, deps=()):
    rows, width = dy.shape
    unit = width // n
    block = 256
    by_rows = lambda m: pl.BlockSpec((block, m), lambda i: (i, 0))
    whole = lambda a: pl.BlockSpec(a.shape, lambda i: (0, 0))
    units = pl.BlockSpec((n // 2, unit, width), lambda i: (0, 0, 0))
    shape = jax.ShapeDtypeStruct((n // 2, unit, width), BF)
    return call(
        functools.partial(mid_back_kernel, core_bit=core_bit),
        (table, da2, w_out, mid, dy, *ctx, vec),
        [
            pl.BlockSpec(memory_space=pltpu.SMEM),
            by_rows(width),
            whole(w_out),
            by_rows(width),
            by_rows(width),
            *(by_rows(c.shape[1]) for c in ctx),
            whole(vec),
        ],
        deps,
        grid=(rows // block,),
        out_specs=[
            by_rows(width),
            by_rows(width),
            pl.BlockSpec((8, width), lambda i: (0, 0)),
            units,
            units,
        ],
        out_shape=[
            jax.ShapeDtypeStruct((rows, width), F32),
            jax.ShapeDtypeStruct((rows, width), BF),
            jax.ShapeDtypeStruct((8, width), F32),
            shape,
            shape,
        ],
        scratch_shapes=[pltpu.VMEM((width, width), F32)],
        compiler_params=params(),
        cost_estimate=cost(4 * rows * width * width, 16e6),
        name="mid_back",
    )


def token_grad_kernel(x_ref, *refs):
    *parts, w_ref, dmid_ref, vec_ref, grad_ref = refs
    dproj = jnp.concatenate([ref[...] for ref in parts], axis=1)
    da1 = dot_rt(dproj, w_ref[:, : dproj.shape[1]])
    normed, rs = norm_parts(x_ref[...].astype(F32))
    grad_ref[...] = dmid_ref[...] + norm_back(normed, rs, vec_ref[0:1, :], da1)


def token_grad(tokens, parts, w_in, dmid, vec, deps=()):
    rows, width = tokens.shape
    block = 256
    by_rows = lambda m: pl.BlockSpec((block, m), lambda i: (i, 0))
    whole = lambda a: pl.BlockSpec(a.shape, lambda i: (0, 0))
    return call(
        token_grad_kernel,
        (tokens, *parts, w_in, dmid, vec),
        [by_rows(width)]
        + [by_rows(p.shape[1]) for p in parts]
        + [whole(w_in), by_rows(width), whole(vec)],
        deps,
        grid=(rows // block,),
        out_specs=by_rows(width),
        out_shape=jax.ShapeDtypeStruct((rows, width), F32),
        compiler_params=params(),
        cost_estimate=cost(2 * rows * width * w_in.shape[1], 17e6),
        name="token_grad",
    )


def in_grad_kernel(table_ref, n1_hbm, w_hbm, *refs, starts):
    count = len(starts)
    parts, refs = refs[:count], refs[count:]
    s2_ref, c1_ref, keep_hbm, send_hbm, n1_ref, w_ref, grads_ref, stage, in_sems, out_sems = refs
    rows, width = n1_ref.shape
    n, size, wide = stage.shape
    vec_at = wide - LANES
    pieces = [(at, min(width, vec_at - at)) for at in range(0, vec_at, width)]
    loads = [pltpu.make_async_copy(n1_hbm, n1_ref, in_sems.at[0])]
    loads.append(
        pltpu.make_async_copy(
            w_hbm.at[:, pl.ds(vec_at, LANES)], w_ref.at[:, pl.ds(vec_at, LANES)], in_sems.at[1]
        )
    )
    wanted = []
    for at, extent in pieces:
        cols = pl.ds(at, extent)
        group = [
            pltpu.make_async_copy(
                ref,
                grads_ref.at[:, pl.ds(start, ref.shape[1])],
                in_sems.at[2 + len(pieces) + i],
            )
            for i, (ref, start) in enumerate(zip(parts, starts, strict=True))
            if at <= start < at + extent
        ]
        group.append(
            pltpu.make_async_copy(
                w_hbm.at[:, cols], w_ref.at[:, cols], in_sems.at[2 + len(wanted)]
            )
        )
        wanted.append(group)
    for copy in loads + [c for group in wanted for c in group]:
        copy.start()
    for copy in loads:
        copy.wait()
    turned = jnp.transpose(n1_ref[...])
    gain = w_ref[:, vec_at : vec_at + 1].astype(F32)
    shift = w_ref[:, vec_at + 1 : vec_at + 2].astype(F32)
    dgain = jnp.zeros((width, 1), F32)
    dshift = jnp.zeros((width, 1), F32)
    places = [table_ref[d] for d in range(n)]
    sent = []

    def store(result, at, extent):
        for d in range(n):
            stage[places[d], :, at : at + extent] = result[d * size : (d + 1) * size, :].astype(BF)
        for i, ref in enumerate((keep_hbm, send_hbm)):
            copy = pltpu.make_async_copy(
                stage.at[pl.ds(i * (n // 2), n // 2), :, pl.ds(at, extent)],
                ref.at[:, :, pl.ds(at, extent)],
                out_sems.at[len(sent)],
            )
            copy.start()
            sent.append(copy)

    query_sums = None
    for (at, extent), group in zip(pieces, wanted, strict=True):
        for copy in group:
            copy.wait()
        grads = grads_ref[:, at : at + extent]
        sums = jnp.sum(grads.astype(F32), axis=0, keepdims=True)
        if at == 0:
            query_sums = sums
        weights = w_ref[:, at : at + extent].astype(F32)
        product = dot(turned, grads)
        dgain += jnp.sum(weights * product, axis=1, keepdims=True)
        dshift += jnp.sum(weights * sums, axis=1, keepdims=True)
        store(gain * product + shift * sums, at, extent)
    hidden_rows = c1_ref.shape[1] // width
    stacked = jnp.concatenate(
        [jnp.zeros((2, width), F32), query_sums, s2_ref[0:4, :]]
        + [c1_ref[0:1, g * width : (g + 1) * width] for g in range(hidden_rows)]
        + [jnp.zeros((LANES - 7 - hidden_rows, width), F32)],
        axis=0,
    )
    lane = lanes_of((width, LANES))
    own = jnp.where(lane == 0, dgain, jnp.where(lane == 1, dshift, 0.0))
    store(jnp.transpose(stacked) + own, vec_at, LANES)
    for copy in sent:
        copy.wait()


def in_grad(table, n1, w_in, parts, starts, s2, c1, deps=()):
    rows, width = n1.shape
    wide = w_in.shape[1]
    n = (table.shape[0] - 1) // 4
    pieces = -(-(wide - LANES) // width)
    shape = jax.ShapeDtypeStruct((n // 2, width // n, wide), BF)
    vmem = pl.BlockSpec(memory_space=pltpu.VMEM)
    anywhere = pl.BlockSpec(memory_space=pl.ANY)
    return call(
        functools.partial(in_grad_kernel, starts=starts),
        (table, n1, w_in, *parts, s2, c1),
        [pl.BlockSpec(memory_space=pltpu.SMEM)]
        + [anywhere] * (2 + len(parts))
        + [vmem] * 2,
        deps,
        out_specs=[anywhere] * 2,
        out_shape=[shape, shape],
        scratch_shapes=[
            pltpu.VMEM((rows, width), BF),
            pltpu.VMEM((width, wide), BF),
            pltpu.VMEM((rows, wide - LANES), BF),
            pltpu.VMEM((n, width // n, wide), BF),
            pltpu.SemaphoreType.DMA((2 + pieces + len(parts),)),
            pltpu.SemaphoreType.DMA((2 * (pieces + 1),)),
        ],
        compiler_params=pltpu.CompilerParams(vmem_limit_bytes=VMEM_LIMIT),
        cost_estimate=cost(2 * rows * width * wide, 12e6),
        name="in_grad",
    )


def stages_of(n_dp, n_fsdp):
    fsdp_bits = n_fsdp.bit_length() - 1
    dp_bits = n_dp.bit_length() - 1
    low = list(range(fsdp_bits // 2))[::-1]
    high = list(range(fsdp_bits // 2, fsdp_bits))[::-1]
    z_bits = list(range(fsdp_bits + 1, fsdp_bits + dp_bits))[::-1]
    core = fsdp_bits
    return core, ([core] + high + low + z_bits, [core] + low + high + z_bits)


def place_table(n_dp, n_fsdp):
    core, orders = stages_of(n_dp, n_fsdp)
    n = n_dp * n_fsdp
    table = np.zeros((n, 4 * n + 1), np.int32)
    for me in range(n):
        for absolute in range(2):
            base = 2 * n * absolute
            for d in range(n):
                away = d ^ me
                place = 0
                for bit in orders[(d >> core) & 1]:
                    of = d if absolute and bit > core else away
                    place = place * 2 + ((of >> bit) & 1)
                table[me, base + d] = place
                table[me, base + n + place] = d
        table[me, 4 * n] = (me >> core) & 1
    return table


def tied_columns_kernel(*refs):
    *parts, out_ref = refs
    at, size = 0, parts[0].shape[0]
    for ref in parts:
        out_ref[:size, at : at + ref.shape[1]] = ref[...]
        at += ref.shape[1]
    if out_ref.shape[0] > size:
        out_ref[size:, :] = jnp.zeros((out_ref.shape[0] - size, at), BF)


def tied_columns(parts, deps, rows):
    vmem = pl.BlockSpec(memory_space=pltpu.VMEM)
    shape = (rows, sum(p.shape[1] for p in parts))
    return call(
        tied_columns_kernel,
        parts,
        [vmem] * len(parts),
        deps,
        out_specs=vmem,
        out_shape=jax.ShapeDtypeStruct(shape, BF),
        cost_estimate=cost(0, 4 * shape[0] * shape[1]),
        name="tied_columns",
    )


def merge_kernel(*refs):
    *parts, out_ref = refs
    at = 0
    for ref in parts:
        out_ref[at : at + ref.shape[0]] = ref[:, : out_ref.shape[1]]
        at += ref.shape[0]


def merge(parts, deps, size=None):
    if not deps:
        return jnp.concatenate(parts, axis=0)
    vmem = pl.BlockSpec(memory_space=pltpu.VMEM)
    shape = (sum(p.shape[0] for p in parts), size or parts[0].shape[1], parts[0].shape[2])
    return call(
        merge_kernel,
        parts,
        [vmem] * len(parts),
        deps,
        out_specs=vmem,
        out_shape=jax.ShapeDtypeStruct(shape, BF),
        compiler_params=pltpu.CompilerParams(vmem_limit_bytes=SMALL_LIMIT),
        cost_estimate=cost(0, 4 * shape[0] * shape[1] * shape[2]),
        name="merge",
    )


class Exchange:
    def __init__(self, n_dp, n_fsdp):
        self.n = n_dp * n_fsdp
        self.count = self.n.bit_length() - 1
        self.core_bit, self.orders = stages_of(n_dp, n_fsdp)
        me = lax.axis_index("dp") * n_fsdp + lax.axis_index("fsdp")
        self.z = n_dp // 2
        self.z_groups = [list(range(c, n_dp, 2)) for c in range(2)]
        table = jnp.asarray(place_table(n_dp, n_fsdp))
        self.table = lax.dynamic_slice(table, (me, 0), (1, table.shape[1]))[0]

    def swap(self, value, stage):
        bits = [self.orders[(i >> self.core_bit) & 1][stage] for i in range(self.n)]
        return lax.ppermute(value, AXES, [(i, i ^ (1 << b)) for i, b in enumerate(bits)])

    def over_z(self, value, away):
        mask = away << (self.core_bit + 1)
        return lax.ppermute(value, AXES, [(i, i ^ mask) for i in range(self.n)])

    def over_plane(self, value, place):
        count = self.count - self.z.bit_length()

        def mask(core):
            bits = self.orders[core][1 : 1 + count]
            return sum(1 << b for k, b in enumerate(bits) if (place >> (count - 1 - k)) & 1)

        pairs = [(i, i ^ mask((i >> self.core_bit) & 1)) for i in range(self.n)]
        return lax.ppermute(value, AXES, pairs)

    def gather_z(self, rows, deps=()):
        held = rows[None]
        return merge([held] + [self.over_z(held, k) for k in range(1, self.z)], deps)

    def gather_plane(self, held, stage, deps=()):
        return merge((held, self.swap(held, stage)), deps)

    def with_core(self, parts, places):
        half = self.n // 2
        others = [self.swap(p, 0) for p in parts]
        return (
            tuple(parts) + tuple(others),
            tuple(places) + tuple(tuple(b + half for b in bases) for bases in places),
        )


class Halving:
    def __init__(self, exchange, keep, send):
        self.exchange, self.keep, self.send, self.stage = exchange, keep, send, 0

    def added(self, got, first, count):
        part = slice(first, first + count)
        return self.keep[part].astype(F32) + got[part].astype(F32)

    def step(self):
        got = self.exchange.swap(self.send, self.stage)
        self.stage += 1
        half = self.keep.shape[0] // 2
        self.keep, self.send = (self.added(got, k, half).astype(BF) for k in (0, half))
        return (self.send,)

    def to_plane(self):
        self.keep = parted(self.keep, self.exchange.swap(self.send, 0), self.exchange.z)
        return tuple(self.keep)

    def plane(self, after):
        got = [self.exchange.over_plane(k, i) for i, k in enumerate(self.keep) if i]
        self.keep = combine([self.keep[0], *got], after)
        return tuple(self.keep)

    def ask(self):
        got = self.exchange.swap(self.send, self.stage)
        self.stage += 1
        return got

    def join(self, other):
        self.keep = jnp.concatenate([self.keep, other.keep], axis=2)
        self.send = jnp.concatenate([self.send, other.send], axis=2)
        return (self.send,)

    def last(self):
        self.got = tuple(self.exchange.over_z(k, i + 1) for i, k in enumerate(self.keep[1:]))
        return self.got

def fold_both(first, second, deps):
    got = (first.ask(), second.ask())
    steps = 4

    def kernel(*refs):
        ins, outs = refs[:8], refs[8:]
        for k in range(4):
            keep, came = ins[2 * k], ins[2 * k + 1]
            outs[k][...] = (keep[...].astype(F32) + came[...].astype(F32)).astype(BF)

    ins, specs, out_specs, shapes = [], [], [], []
    for halving, came in zip((first, second), got, strict=True):
        count, size, width = halving.keep.shape
        half = count // 2
        block = half // steps
        for k in range(2):
            spec = pl.BlockSpec((block, size, width), lambda i, k=k: (i + k * steps, 0, 0))
            ins += [halving.keep, came]
            specs += [spec, spec]
            out_specs.append(pl.BlockSpec((block, size, width), lambda i: (i, 0, 0)))
            shapes.append(jax.ShapeDtypeStruct((half, size, width), BF))
    out = call(
        kernel,
        ins,
        specs,
        deps,
        grid=(steps,),
        out_specs=out_specs,
        out_shape=shapes,
        compiler_params=pltpu.CompilerParams(
            vmem_limit_bytes=SMALL_LIMIT, dimension_semantics=("arbitrary",)
        ),
        cost_estimate=cost(1e6, 12e6),
        name="fold_both",
    )
    first.keep, first.send, second.keep, second.send = out
    return (out[1], out[3])


def parted(keep, came, each):
    count, size, width = keep.shape

    def kernel(keep_ref, came_ref, *outs):
        for k, out in enumerate(outs):
            part = slice(k * each, (k + 1) * each)
            out[...] = (keep_ref[part].astype(F32) + came_ref[part].astype(F32)).astype(BF)

    vmem = pl.BlockSpec(memory_space=pltpu.VMEM)
    shape = jax.ShapeDtypeStruct((each, size, width), BF)
    return call(
        kernel,
        (keep, came),
        [vmem] * 2,
        (),
        out_specs=[vmem] * (count // each),
        out_shape=[shape] * (count // each),
        compiler_params=pltpu.CompilerParams(vmem_limit_bytes=SMALL_LIMIT),
        cost_estimate=cost(count * size * width, 6 * count * size * width),
        name="parted",
    )


def join_along_z(wide, deep, exchange, deps):
    ins = (wide.keep, wide.ask(), deep.keep, deep.ask())
    z, size, columns = wide.keep.shape
    _, tall, width = deep.keep.shape
    blocks = columns // width

    def kernel(*refs):
        wide_ref, wide_came, deep_ref, deep_came, out_ref = refs
        total = (wide_ref[0].astype(F32) + wide_came[0].astype(F32)).astype(BF)
        for b in range(blocks):
            out_ref[0, b * size : (b + 1) * size, :] = total[:, b * width : (b + 1) * width]
        total = (deep_ref[0].astype(F32) + deep_came[0].astype(F32)).astype(BF)
        out_ref[0, blocks * size :, :] = total

    one = lambda *dims: pl.BlockSpec((1, *dims), lambda i: (i, 0, 0))
    rows = blocks * size + tall
    joined = call(
        kernel,
        ins,
        [one(size, columns)] * 2 + [one(tall, width)] * 2,
        deps,
        grid=(z,),
        out_specs=one(rows, width),
        out_shape=jax.ShapeDtypeStruct((z, rows, width), BF),
        compiler_params=pltpu.CompilerParams(
            vmem_limit_bytes=SMALL_LIMIT, dimension_semantics=("arbitrary",)
        ),
        cost_estimate=cost(1e6, 5e6),
        name="join_along_z",
    )
    return joined, lax.psum_scatter(
        joined, "dp", scatter_dimension=0, tiled=True, axis_index_groups=exchange.z_groups
    )


def combine(parts, deps):
    count, size, width = parts[0].shape

    def kernel(*refs):
        ins, outs = refs[: len(parts)], refs[len(parts) :]
        for k, out in enumerate(outs):
            out[0] = sum(r[k].astype(F32) for r in ins).astype(BF)

    vmem = pl.BlockSpec(memory_space=pltpu.VMEM)
    shape = jax.ShapeDtypeStruct((1, size, width), BF)
    return call(
        kernel,
        parts,
        [vmem] * len(parts),
        deps,
        out_specs=[vmem] * count,
        out_shape=[shape] * count,
        compiler_params=pltpu.CompilerParams(vmem_limit_bytes=SMALL_LIMIT),
        cost_estimate=cost(len(parts) * count * size * width, 8 * count * size * width),
        name="combine",
    )


def finish(in_parts, others, cols, vrows, hidden, deps):
    size = in_parts[0].shape[1]
    width = others.shape[2]
    blocks = hidden // width
    tall = others.shape[1] - (blocks + 1) * size

    def kernel(*refs):
        *ins, others_ref, in_ref, vec_ref, out_ref, up_ref, down_ref = refs
        total = sum(r[0].astype(F32) for r in ins)
        in_ref[...] = total[:, :cols]
        table = jnp.concatenate([total[:, cols:], jnp.zeros((LANES - size, LANES), F32)], axis=0)
        vec_ref[...] = jnp.transpose(table)[:vrows, :size]
        for b in range(blocks):
            rows = others_ref[0, b * size : (b + 1) * size, :]
            up_ref[:, b * width : (b + 1) * width] = rows.astype(F32)
        at = blocks * size
        out_ref[...] = others_ref[0, at : at + size, :].astype(F32)
        down_ref[...] = others_ref[0, at + size :, :].astype(F32)

    vmem = pl.BlockSpec(memory_space=pltpu.VMEM)
    shape = lambda *dims: jax.ShapeDtypeStruct(dims, F32)
    return call(
        kernel,
        (*in_parts, others),
        [vmem] * (len(in_parts) + 1),
        deps,
        out_specs=[vmem] * 5,
        out_shape=[
            shape(size, cols),
            shape(vrows, size),
            shape(size, width),
            shape(size, hidden),
            shape(tall, width),
        ],
        cost_estimate=cost(1, 3e6),
        name="finish",
    )


def body(
    tokens, first_values, out_grad, lengths, in_proj, out_proj, up_proj, down_proj, vectors,
    *, n_dp, n_fsdp
):
    width = tokens.shape[1]
    cols = in_proj.shape[1]
    vrows = vectors.shape[0]
    exchange = Exchange(n_dp, n_fsdp)
    n, core_bit, table = exchange.n, exchange.core_bit, exchange.table

    z = exchange.z
    planes = exchange.count - z.bit_length()
    quarter = n // 8

    vec_t = jnp.pad(vectors.T, ((0, 0), (0, LANES - vrows)))
    early = tied_columns((out_proj, up_proj), (table,), out_proj.shape[0])[None]
    held = exchange.gather_z(jnp.concatenate([in_proj, vec_t], axis=1), (early,))
    others = [exchange.over_z(early, k) for k in range(1, z)]
    if planes == 2:
        got_a, got_b = exchange.swap(held, 1), exchange.swap(held, 2)
        got_ba = exchange.swap(merge((got_a,), tuple(others)), 2)
        in_parts = exchange.with_core(
            (held, got_b, got_a, got_ba), tuple((q * quarter,) for q in range(4))
        )
    else:
        for stage in range(planes, 0, -1):
            held = exchange.gather_plane(held, stage)
        in_parts = exchange.with_core((held,), ((0,),))

    w_down = lax.all_gather(down_proj, AXES, axis=0, tiled=False)
    half = width // LANES // 2
    held_mid = jnp.concatenate([early, *others], axis=0)
    w_in, n1, qkv, vec = in_forward(table, tokens, first_values, in_parts, (held_mid,))
    for stage in range(planes, 1, -1):
        held_mid = exchange.gather_plane(held_mid, stage, (n1,))
    ctx1, ctx2, lse1, lse2 = attn_forward(lengths, qkv, width, (held_mid,))
    got_mid = merge((exchange.swap(held_mid, 1),), (ctx1,))
    mid_parts = exchange.with_core((held_mid, got_mid), ((0,), (n // 4,)))
    ctx = (ctx1, ctx2)
    u, mid, a2, w_out, *halves = ffn_forward(
        table, ctx, tokens, out_grad, vec, mid_parts, core_bit
    )
    h_down = Halving(exchange, *halves)
    dc1, da2, *halves = up_grad(
        table, out_grad, a2, w_down, u, mid_parts, (h_down.keep,)
    )
    h_up = Halving(exchange, *halves)
    deps = h_down.step()
    dmid, dctx, sums2, *halves = mid_back(
        table, da2, w_out, mid, out_grad, ctx, vec, n, core_bit, deps
    )
    h_out = Halving(exchange, *halves)
    fold_both(h_up, h_down, (sums2,))
    h_out.step()
    deps = h_up.join(h_out)
    dq1, dk1, dv1 = attn_backward(lengths, lse1, qkv, ctx1, dctx, 0, half, BF, deps)
    for _ in range(planes - 2):
        h_down.step(), h_up.step()
    deps = h_up.step() + (dq1,)
    h_down.send = merge((h_down.send,), (dq1,))
    dq2, dk2, first_grad = attn_backward(
        lengths, lse2, qkv, ctx2, dctx, half, half, F32, deps
    )
    joined, others = join_along_z(h_up, h_down, exchange, (dq2,))
    deps = (joined,)
    split = half * LANES
    parts = (dq1, dq2, dk1, dk2, dv1)
    starts = (0, split, width, width + split, 2 * width)
    h_in = Halving(
        exchange, *in_grad(table, n1, w_in, parts, starts, sums2, dc1, deps)
    )
    deps = h_in.to_plane()
    input_grad = token_grad(tokens, parts, w_in, dmid, vec, deps)
    first = out_forward(u, mid, w_down, vec, 0, (), deps + (input_grad,))
    deps = h_in.plane((first,))
    output = out_forward(u, mid, w_down, vec, 1, (first,), deps + (others,))
    g_in, g_vec, g_out, g_up, g_down = finish(
        (h_in.keep[0], *h_in.last()), others, cols, vrows, up_proj.shape[1], (output,)
    )
    return (output, input_grad, first_grad, g_in, g_out, g_up, g_down, g_vec)


def solution(mesh):
    rows = P(AXES, None)
    cols = P(None, AXES)
    return jax.shard_map(
        functools.partial(body, n_dp=mesh.shape["dp"], n_fsdp=mesh.shape["fsdp"]),
        mesh=mesh,
        in_specs=(rows,) * 8 + (cols,),
        out_specs=(rows,) * 7 + (cols,),
        check_vma=False,
    )
```

```python
import functools

import jax
import jax.numpy as jnp
import numpy as np
from jax import lax
from jax.experimental import pallas as pl
from jax.experimental.pallas import tpu as pltpu
from jax.sharding import PartitionSpec as P

H = 12
HD = 64
EPS = 1e-05
NEG = -1000000000.0
LANES = 128
AXES = ("dp", "fsdp")
BF = jnp.bfloat16
F32 = jnp.float32
VMEM_LIMIT = 56 * 1024 * 1024
SMALL_LIMIT = 28 * 1024 * 1024
GELU_C = 0.7978845608028654
GELU_A = 0.044715


def dot(a, b):
    return lax.dot_general(a, b, (((1,), (0,)), ((), ())), preferred_element_type=F32)


def dot_rt(a, b):
    return lax.dot_general(a, b, (((1,), (1,)), ((), ())), preferred_element_type=F32)


def dot_lt(a, b):
    return lax.dot_general(a, b, (((0,), (0,)), ((), ())), preferred_element_type=F32)


def params(grid_rank=1):
    return pltpu.CompilerParams(
        vmem_limit_bytes=VMEM_LIMIT, dimension_semantics=("arbitrary",) * grid_rank
    )


def cost(flops, nbytes, trans=0):
    return pl.CostEstimate(flops=int(flops), bytes_accessed=int(nbytes), transcendentals=int(trans))


def call(kernel, ins, in_specs, deps=(), **kw):
    count, extra = len(ins), len(deps)

    def run(*refs):
        kernel(*refs[:count], *refs[count + extra :])

    specs = list(in_specs) + [pl.BlockSpec(memory_space=pl.ANY)] * extra
    return pl.pallas_call(run, in_specs=specs, **kw)(*ins, *deps)


def norm_parts(values):
    centred = values - jnp.mean(values, axis=-1, keepdims=True)
    spread = jnp.mean(centred * centred, axis=-1, keepdims=True)
    rs = lax.rsqrt(spread + EPS)
    return centred * rs, rs


def norm_back(normed, rs, gain, grad):
    scaled = grad * gain
    m1 = jnp.mean(scaled, axis=-1, keepdims=True)
    m2 = jnp.mean(scaled * normed, axis=-1, keepdims=True)
    return rs * (scaled - m1 - normed * m2)


def assemble(table_ref, refs, places, whole_ref):
    n = whole_ref.shape[0]
    for ref, bases in zip(refs, places, strict=True):
        each = ref.shape[0] // len(bases)
        for b, base in enumerate(bases):
            for k in range(each):
                whole_ref[table_ref[n + base + k]] = ref[b * each + k]


def flatten_units(units_ref, matrix_ref):
    size = units_ref.shape[1]
    for d in range(units_ref.shape[0]):
        matrix_ref[d * size : (d + 1) * size, :] = units_ref[d]


def const_spec(a):
    rank = len(a.shape)
    return pl.BlockSpec(a.shape, lambda *_: (0,) * rank)


def in_kernel(table_ref, x_ref, fv_ref, *refs, places):
    *parts, w_hbm, n1_ref, qkv_ref, vec_ref, units_ref, w_ref, sem = refs
    width = x_ref.shape[1]
    cols = w_ref.shape[1] - LANES
    copy = pltpu.make_async_copy(w_ref, w_hbm, sem)

    @pl.when(pl.program_id(0) == 0)
    def _():
        assemble(table_ref, parts, places, units_ref)
        flatten_units(units_ref, w_ref)
        copy.start()
        turned = jnp.transpose(w_ref[:, cols:].astype(F32))
        vec_ref[...] = turned[: vec_ref.shape[0]]

    normed, _ = norm_parts(x_ref[...].astype(F32))
    a1 = (normed * vec_ref[0:1, :] + vec_ref[1:2, :]).astype(BF)
    n1_ref[...] = normed.astype(BF)
    proj = dot(a1, w_ref[:, :cols])
    queries = (proj[:, :width] + vec_ref[2:3, :]).astype(BF)
    qkv_ref[:, :width] = queries * jnp.asarray(HD**-0.5, BF)
    qkv_ref[:, width:cols] = proj[:, width:].astype(BF)
    qkv_ref[:, cols:] = fv_ref[...]

    @pl.when(pl.program_id(0) == pl.num_programs(0) - 1)
    def _():
        copy.wait()


def in_forward(table, tokens, first_values, gathered, deps=()):
    parts, places = gathered
    rows, width = tokens.shape
    half = first_values.shape[1]
    _, size, wide = parts[0].shape
    n = width // size
    block = 256
    by_rows = lambda m: pl.BlockSpec((block, m), lambda i: (i, 0))
    const = lambda *shape: pl.BlockSpec(shape, lambda i: (0, 0))
    return call(
        functools.partial(in_kernel, places=places),
        (table, tokens, first_values, *parts),
        [pl.BlockSpec(memory_space=pltpu.SMEM), by_rows(width), by_rows(half)]
        + [const_spec(p) for p in parts],
        deps,
        grid=(rows // block,),
        out_specs=[
            pl.BlockSpec(memory_space=pl.ANY),
            by_rows(width),
            by_rows(wide - LANES + half),
            const(16, width),
        ],
        out_shape=[
            jax.ShapeDtypeStruct((width, wide), BF),
            jax.ShapeDtypeStruct((rows, width), BF),
            jax.ShapeDtypeStruct((rows, wide - LANES + half), BF),
            jax.ShapeDtypeStruct((16, width), F32),
        ],
        scratch_shapes=[
            pltpu.VMEM((n, size, wide), BF),
            pltpu.VMEM((width, wide), BF),
            pltpu.SemaphoreType.DMA(()),
        ],
        compiler_params=params(),
        cost_estimate=cost(2 * rows * width * wide, 16e6),
        name="in_forward",
    )


def lanes_of(shape):
    return lax.broadcasted_iota(jnp.int32, shape, 1)


def own_lanes(e, shape):
    lane = lanes_of(shape)
    return (lane < HD) if e == 0 else (lane >= HD)


def spare(e):
    return HD if e == 0 else 0


def split3(values):
    hi = values.astype(BF).astype(F32)
    rest = values - hi
    mid = rest.astype(BF).astype(F32)
    return hi, mid, rest - mid


def augmented(vectors, e, lane, seg, filled):
    aux = jnp.where((lane == spare(e)) & seg, filled, 0.0)
    return jnp.where(own_lanes(e, lane.shape), vectors, aux).astype(BF)


def causal(block):
    rows = lax.broadcasted_iota(jnp.int32, (block, block), 0)
    return rows <= lax.broadcasted_iota(jnp.int32, (block, block), 1)


def scores_of(keys, queries, tri, lo):
    s = dot_rt(keys, queries)
    diag = jnp.where(tri, s[lo:, :], NEG)
    return diag if lo == 0 else jnp.concatenate([s[:lo, :], diag], axis=0)


def attn_fwd_kernel(bound_ref, q_ref, k_ref, v_ref, ctx_ref, lse_ref):
    rows = q_ref.shape[0]
    block = 256
    bound = bound_ref[0, 0]
    shape = (rows, LANES)
    lane = lanes_of(shape)
    place = lax.broadcasted_iota(jnp.int32, shape, 0)
    k_all = k_ref[...].astype(F32)
    q_all = q_ref[...].astype(F32)
    values = jnp.concatenate([v_ref[...], jnp.ones(shape, BF)], axis=1)
    tri = causal(block)
    ctxs = [[None, None] for _ in range(rows // block)]
    k_augs = [augmented(k_all, e, lane, place < bound, 1.0) for e in range(2)]
    q_augs = [augmented(q_all, e, lane, place >= bound, NEG) for e in range(2)]
    chains = [(j, e) for j in range(rows // block) for e in range(2)]

    def scores(j, e):
        lo, hi = j * block, (j + 1) * block
        return scores_of(k_augs[e][:hi, :], q_augs[e][lo:hi, :], tri, lo)

    def weighted(j, e, p):
        o = dot_lt(p, values[: (j + 1) * block, :])
        ctxs[j][e] = o[:, :LANES] / o[:, LANES:]

    following = scores(*chains[0])
    waiting = None
    for i, (j, e) in enumerate(chains):
        s = following
        if i + 1 < len(chains):
            following = scores(*chains[i + 1])
        peak = jnp.max(s, axis=0, keepdims=True)
        p = jnp.exp(s - peak)
        lse = peak + jnp.log(jnp.sum(p, axis=0, keepdims=True))
        lse_ref[0, e : e + 1, j * block : (j + 1) * block] = lse
        if waiting is not None:
            weighted(*waiting)
        waiting = (j, e, p.astype(BF))
    weighted(*waiting)
    first = lanes_of((block, LANES)) < HD
    for j in range(rows // block):
        ctx_ref[j * block : (j + 1) * block, :] = jnp.where(first, *ctxs[j]).astype(BF)


def attn_forward(lengths, qkv, width, deps=()):
    rows = qkv.shape[0]
    pairs = width // LANES
    half = pairs // 2
    slab = lambda off: pl.BlockSpec((rows, LANES), lambda j: (0, off + j))

    def kernel(bound_ref, q_ref, k_ref, v_ref, ctx1_ref, ctx2_ref, lse1_ref, lse2_ref, ctx_ref, lse_ref):
        attn_fwd_kernel(bound_ref, q_ref, k_ref, v_ref, ctx_ref, lse_ref)
        for k, (ctx, lse) in enumerate(((ctx1_ref, lse1_ref), (ctx2_ref, lse2_ref))):

            @pl.when(pl.program_id(0) // half == k)
            def _(ctx=ctx, lse=lse):
                ctx[...] = ctx_ref[...]
                lse[...] = lse_ref[...]

    first = lambda j: jnp.minimum(j, half - 1)
    second = lambda j: jnp.maximum(j - half, 0)
    ctx_spec = lambda of: pl.BlockSpec((rows, LANES), lambda j: (0, of(j)))
    lse_spec = lambda of: pl.BlockSpec((1, 8, rows), lambda j: (of(j), 0, 0))
    ctx_shape = jax.ShapeDtypeStruct((rows, half * LANES), BF)
    lse_shape = jax.ShapeDtypeStruct((half, 8, rows), F32)
    return call(
        kernel,
        (lengths, qkv, qkv, qkv),
        [pl.BlockSpec(memory_space=pltpu.SMEM), *(slab(c * pairs) for c in range(3))],
        deps,
        grid=(pairs,),
        out_specs=[ctx_spec(first), ctx_spec(second), lse_spec(first), lse_spec(second)],
        out_shape=[ctx_shape, ctx_shape, lse_shape, lse_shape],
        scratch_shapes=[pltpu.VMEM((rows, LANES), BF), pltpu.VMEM((1, 8, rows), F32)],
        compiler_params=params(),
        cost_estimate=cost(2 * 2 * rows * rows * 256 * H * 0.63, 9e6, rows * rows * H),
        name="attn_forward",
    )


def attn_bwd_kernel(
    bound_ref, lse_ref, q_ref, k_ref, v_ref, ctx_ref, do_ref, dq_ref, dk_ref, dv_ref, dk_acc, dv_acc
):
    rows = k_ref.shape[0]
    block = 256
    bound = bound_ref[0, 0]
    full = (rows, LANES)
    lane = lanes_of(full)
    place = lax.broadcasted_iota(jnp.int32, full, 0)
    q_all = q_ref[...].astype(F32)
    k_all = k_ref[...].astype(F32)
    v_all = v_ref[...].astype(F32)
    do_all = do_ref[...].astype(F32)
    prod = do_all * ctx_ref[...].astype(F32)
    tri = causal(block)
    dqs = [[None, None] for _ in range(rows // block)]
    k_augs, q_augs, v_augs, do_augs = [], [], [], []
    for e in range(2):
        sp = spare(e)
        own = own_lanes(e, full)
        three = (lane >= sp + 1) & (lane <= sp + 3)
        k_augs.append(augmented(k_all, e, lane, place < bound, 1.0))
        q_augs.append(augmented(q_all, e, lane, place >= bound, NEG))
        v_augs.append(jnp.where(own, v_all, jnp.where(three, 1.0, 0.0)).astype(BF))
        delta = jnp.sum(jnp.where(own, prod, 0.0), axis=-1, keepdims=True)
        d_hi, d_mid, d_lo = split3(-delta)
        do_augs.append(
            jnp.where(
                own,
                do_all,
                jnp.where(
                    lane == sp + 1,
                    d_hi,
                    jnp.where(lane == sp + 2, d_mid, jnp.where(lane == sp + 3, d_lo, 0.0)),
                ),
            ).astype(BF)
        )
    chains = [(j, e) for j in reversed(range(rows // block)) for e in range(2)]

    def products(j, e):
        lo, hi = j * block, (j + 1) * block
        s = scores_of(k_augs[e][:hi, :], q_augs[e][lo:hi, :], tri, lo)
        return s, dot_rt(v_augs[e][:hi, :], do_augs[e][lo:hi, :])

    def finish_chain(j, e, p, ds):
        lo, hi = j * block, (j + 1) * block
        dv_j = dot(p, do_augs[e][lo:hi, :])
        dk_j = dot(ds, q_augs[e][lo:hi, :])
        if j == rows // block - 1:
            dv_acc[e] = dv_j
            dk_acc[e] = dk_j
        else:
            dv_acc[e, :hi, :] += dv_j
            dk_acc[e, :hi, :] += dk_j
        dqs[j][e] = dot_lt(ds, k_augs[e][:hi, :])

    following = products(*chains[0])
    for i, (j, e) in enumerate(chains):
        s, dp = following
        if i + 1 < len(chains):
            following = products(*chains[i + 1])
        p = jnp.exp(s - lse_ref[0, e : e + 1, j * block : (j + 1) * block])
        finish_chain(j, e, p.astype(BF), (p * dp).astype(BF))
    first = lanes_of((block, LANES)) < HD
    for j in range(rows // block):
        dq_ref[j * block : (j + 1) * block, :] = (jnp.where(first, *dqs[j]) * HD**-0.5).astype(BF)
    dk_ref[...] = jnp.where(lane < HD, dk_acc[0], dk_acc[1]).astype(BF)
    dv_ref[...] = jnp.where(lane < HD, dv_acc[0], dv_acc[1]).astype(dv_ref.dtype)


def attn_backward(lengths, lse, qkv, ctx, dctx, first, count, dv_type, deps=()):
    rows, width = dctx.shape
    pairs = width // LANES
    slab = lambda off: pl.BlockSpec((rows, LANES), lambda j, off=off: (0, off + j))
    shape = lambda dtype: jax.ShapeDtypeStruct((rows, count * LANES), dtype)
    return call(
        attn_bwd_kernel,
        (lengths, lse, qkv, qkv, qkv, ctx, dctx),
        [
            pl.BlockSpec(memory_space=pltpu.SMEM),
            pl.BlockSpec((1, 8, rows), lambda j: (j, 0, 0)),
            slab(first),
            slab(pairs + first),
            slab(2 * pairs + first),
            slab(0),
            slab(first),
        ],
        deps,
        grid=(count,),
        out_specs=[slab(0)] * 3,
        out_shape=[shape(BF), shape(BF), shape(dv_type)],
        scratch_shapes=[
            pltpu.VMEM((2, rows, LANES), F32),
            pltpu.VMEM((2, rows, LANES), F32),
        ],
        compiler_params=params(),
        cost_estimate=cost(5 * 2 * rows * rows * 256 * 2 * count * 0.63, 15e6, rows * rows * 2 * count),
        name="attn_backward",
    )


def gelu_half(u, u2):
    return 0.5 + 0.5 * jnp.tanh(u * (GELU_C + (GELU_C * GELU_A) * u2))


def gelu_slope(u):
    u2 = u * u
    half = gelu_half(u, u2)
    act = u * half
    return half + (act - act * half) * (2.0 * GELU_C + (6.0 * GELU_C * GELU_A) * u2)


def ffn_kernel(
    table_ref, ctx1_ref, ctx2_ref, x_ref, dy_ref, vec_ref, *refs, places, core_bit
):
    count = len(places)
    out_parts, up_parts = refs[:count], refs[count : 2 * count]
    u_ref, mid_hbm, a2_hbm, wo_hbm, keep_hbm, send_hbm = refs[2 * count : 2 * count + 6]
    wo_units, wu_units, wo_ref, wu_ref, mid_ref, a2_ref, act_ref, stage, once_sems, sems = refs[
        2 * count + 6 :
    ]
    g = pl.program_id(0)
    last = pl.num_programs(0) - 1
    rows, width = x_ref.shape
    chunk = act_ref.shape[1]
    n = wu_units.shape[0]
    block = 256
    once = (
        pltpu.make_async_copy(mid_ref, mid_hbm, once_sems.at[0]),
        pltpu.make_async_copy(a2_ref, a2_hbm, once_sems.at[1]),
        pltpu.make_async_copy(wo_ref, wo_hbm, once_sems.at[2]),
    )

    @pl.when(g == 0)
    def _():
        assemble(table_ref, out_parts, places, wo_units)
        flatten_units(wo_units, wo_ref)
        for i in range(rows // block):
            part = slice(i * block, (i + 1) * block)
            ctx = jnp.concatenate([ctx1_ref[part, :], ctx2_ref[part, :]], axis=1)
            branch = dot(ctx, wo_ref[...]) + vec_ref[3:4, :]
            mid = x_ref[part, :].astype(F32) + branch
            mid_ref[part, :] = mid
            normed, _ = norm_parts(mid)
            a2_ref[part, :] = (normed * vec_ref[4:5, :] + vec_ref[5:6, :]).astype(BF)
        for copy in once:
            copy.start()

    assemble(table_ref, up_parts, places, wu_units)
    flatten_units(wu_units, wu_ref)
    per_row = width // chunk
    row = vec_ref[pl.ds(7 + g // per_row, 1), :]
    bias = row[:, :chunk]
    for c in range(1, per_row):
        bias = jnp.where(g % per_row == c, row[:, c * chunk : (c + 1) * chunk], bias)
    for i in range(rows // block):
        part = slice(i * block, (i + 1) * block)
        u = dot(a2_ref[part, :], wu_ref[...]) + bias
        u_ref[part, :] = u.astype(BF)
        act_ref[part, :] = (u * gelu_half(u, u * u)).astype(BF)
    result = dot_lt(act_ref[...], dy_ref[...])
    units = stage.shape[1]
    size = chunk // units
    slot = lax.rem(g, 2)
    mine = table_ref[4 * n]
    sent = lambda at, i: pltpu.make_async_copy(stage.at[at, i], keep_hbm.at[0], sems.at[at, i])

    @pl.when(g >= 2)
    def _():
        for i in range(units):
            sent(slot, i).wait()

    for i in range(units):
        stage[slot, i] = result[i * size : (i + 1) * size, :].astype(BF)
        d = g * units + i
        place = table_ref[2 * n + d]
        core = lax.rem(lax.shift_right_logical(d, core_bit), 2)

        @pl.when(core == mine)
        def _(i=i, place=place):
            pltpu.make_async_copy(stage.at[slot, i], keep_hbm.at[place], sems.at[slot, i]).start()

        @pl.when(core != mine)
        def _(i=i, place=place):
            pltpu.make_async_copy(
                stage.at[slot, i], send_hbm.at[place - n // 2], sems.at[slot, i]
            ).start()

    @pl.when(g == last)
    def _():
        for copy in once:
            copy.wait()
        for i in range(units):
            sent(1 - slot, i).wait()
            sent(slot, i).wait()


def ffn_forward(table, ctx, tokens, dy, vec, gathered, core_bit, deps=()):
    parts, places = gathered
    rows, width = tokens.shape
    _, size, wide = parts[0].shape
    hidden = wide - width
    n = width // size
    chunk = hidden // 4
    unit = hidden // n
    anywhere = pl.BlockSpec(memory_space=pl.ANY)
    halves = jax.ShapeDtypeStruct((n // 2, unit, width), BF)
    return call(
        functools.partial(ffn_kernel, places=places, core_bit=core_bit),
        (table, *ctx, tokens, dy, vec, *parts, *parts),
        [pl.BlockSpec(memory_space=pltpu.SMEM)]
        + [
            pl.BlockSpec(a.shape, lambda g: (0, 0), pipeline_mode=pl.Buffered(1))
            for a in (*ctx, tokens, dy, vec)
        ]
        + [
            pl.BlockSpec(
                (p.shape[0], size, width), lambda g: (0, 0, 0), pipeline_mode=pl.Buffered(1)
            )
            for p in parts
        ]
        + [
            pl.BlockSpec((p.shape[0], size, chunk), lambda g: (0, 0, width // chunk + g))
            for p in parts
        ],
        deps,
        grid=(hidden // chunk,),
        out_specs=[pl.BlockSpec((rows, chunk), lambda g: (0, g))] + [anywhere] * 5,
        out_shape=[
            jax.ShapeDtypeStruct((rows, hidden), BF),
            jax.ShapeDtypeStruct((rows, width), F32),
            jax.ShapeDtypeStruct((rows, width), BF),
            jax.ShapeDtypeStruct((width, width), BF),
            halves,
            halves,
        ],
        scratch_shapes=[
            pltpu.VMEM((n, size, width), BF),
            pltpu.VMEM((n, size, chunk), BF),
            pltpu.VMEM((width, width), BF),
            pltpu.VMEM((width, chunk), BF),
            pltpu.VMEM((rows, width), F32),
            pltpu.VMEM((rows, width), BF),
            pltpu.VMEM((rows, chunk), BF),
            pltpu.VMEM((2, n // 4, unit, width), BF),
            pltpu.SemaphoreType.DMA((3,)),
            pltpu.SemaphoreType.DMA((2, n // 4)),
        ],
        compiler_params=params(),
        cost_estimate=cost(2 * rows * width * (wide + hidden), 40e6, rows * hidden),
        name="ffn_forward",
    )


def out_kernel(u_ref, mid_ref, wd_ref, vec_ref, *refs):
    out_ref = refs[-1]
    u = u_ref[...].astype(F32)
    act = (u * gelu_half(u, u * u)).astype(BF)
    w_down = wd_ref[...].reshape(-1, wd_ref.shape[2])
    out_ref[...] = mid_ref[...] + dot(act, w_down) + vec_ref[6:7, :]


def out_forward(u, mid, w_down, vec, half, into=(), deps=()):
    rows, width = mid.shape
    hidden = u.shape[1]
    block = 256
    steps = rows // block // 2
    by_rows = lambda n: pl.BlockSpec((block, n), lambda i: (i + half * steps, 0))
    whole = lambda a: pl.BlockSpec(a.shape, lambda i: (0, 0))
    return call(
        out_kernel,
        (u, mid, w_down, vec, *into),
        [by_rows(hidden), by_rows(width), const_spec(w_down), whole(vec)]
        + [pl.BlockSpec(memory_space=pl.ANY)] * len(into),
        deps,
        grid=(steps,),
        out_specs=by_rows(width),
        out_shape=jax.ShapeDtypeStruct((rows, width), F32),
        input_output_aliases={4: 0} if into else {},
        compiler_params=params(),
        cost_estimate=cost(rows * width * hidden, 12e6),
        name="out_forward",
    )


def store_units(table_ref, result, keep_ref, send_ref, core_bit, put, absolute):
    half = keep_ref.shape[0]
    units = 2 * half
    size = result.shape[0] // units
    for mine in range(2):

        @pl.when(table_ref[4 * units] == mine)
        def _(mine=mine):
            for d in range(units):
                i = d
                place = table_ref[d + 2 * units * absolute]
                rows = result[i * size : (i + 1) * size, :].astype(BF)
                if ((d >> core_bit) & 1) == mine:
                    put(keep_ref, place, rows)
                else:
                    put(send_ref, place - half, rows)


def put_rows(ref, place, rows):
    ref[place] = rows


def up_grad_kernel(table_ref, dy_ref, a2_ref, wd_ref, u_ref, *refs, places):
    count = len(places)
    parts = refs[:count]
    sums_ref, da2_ref, keep_hbm, send_hbm = refs[count : count + 4]
    a2t, wu_units, wu_ref, du_ref, stage, sems = refs[count + 4 :]
    g = pl.program_id(0)
    last = pl.num_programs(0) - 1
    rows, chunk = du_ref.shape
    n, size, _ = wu_units.shape
    block = 256
    slot = lax.rem(g, 2)

    def sent(at, step):
        cols = pl.ds(pl.multiple_of(step * chunk, chunk), chunk)
        half = n // 2
        return [
            pltpu.make_async_copy(
                stage.at[at, pl.ds(i * half, half)], ref.at[:, :, cols], sems.at[at, i]
            )
            for i, ref in enumerate((keep_hbm, send_hbm))
        ]

    @pl.when(g == 0)
    def _():
        a2t[: a2_ref.shape[1], :] = jnp.transpose(a2_ref[...])
        a2t[a2_ref.shape[1] :, :] = jnp.ones((16, rows), BF)
        da2_ref[...] = jnp.zeros_like(da2_ref)

    @pl.when(g >= 2)
    def _():
        for copy in sent(slot, g - 2):
            copy.wait()

    assemble(table_ref, parts, places, wu_units)
    flatten_units(wu_units, wu_ref)
    w_down = wd_ref[...].reshape(chunk, wd_ref.shape[2])
    for i in range(rows // block):
        part = slice(i * block, (i + 1) * block)
        dh = dot_rt(dy_ref[part, :], w_down)
        du = (dh * gelu_slope(u_ref[part, :].astype(F32))).astype(BF)
        du_ref[part, :] = du
        da2_ref[part, :] += dot_rt(du, wu_ref[...])
    for c in range(0, chunk, block):
        result = dot(a2t[...], du_ref[:, c : c + block])
        sums_ref[:, c : c + block] = result[n * size : n * size + 1, :]
        for d in range(n):
            place = table_ref[2 * n + d]
            stage[slot, place, :, c : c + block] = result[d * size : (d + 1) * size, :].astype(BF)
    for copy in sent(slot, g):
        copy.start()

    @pl.when(g == last)
    def _():
        for copy in sent(1 - slot, g - 1) + sent(slot, g):
            copy.wait()


def up_grad(table, dy, a2, w_down, u, gathered, deps=()):
    parts, places = gathered
    rows, width = dy.shape
    hidden = u.shape[1]
    n, deep, _ = w_down.shape
    size = width // n
    chunk = hidden // 4
    anywhere = pl.BlockSpec(memory_space=pl.ANY)
    shape = jax.ShapeDtypeStruct((n // 2, size, hidden), BF)
    once = lambda a: pl.BlockSpec(a.shape, lambda g: (0, 0), pipeline_mode=pl.Buffered(1))
    return call(
        functools.partial(up_grad_kernel, places=places),
        (table, dy, a2, w_down, u, *parts),
        [
            pl.BlockSpec(memory_space=pltpu.SMEM),
            once(dy),
            once(a2),
            pl.BlockSpec((n // 4, deep, width), lambda g: (g, 0, 0)),
            pl.BlockSpec((rows, chunk), lambda g: (0, g)),
        ]
        + [
            pl.BlockSpec((p.shape[0], size, chunk), lambda g: (0, 0, width // chunk + g))
            for p in parts
        ],
        deps,
        grid=(hidden // chunk,),
        out_specs=[
            pl.BlockSpec((1, chunk), lambda g: (0, g)),
            pl.BlockSpec((rows, width), lambda g: (0, 0)),
            anywhere,
            anywhere,
        ],
        out_shape=[
            jax.ShapeDtypeStruct((1, hidden), F32),
            jax.ShapeDtypeStruct((rows, width), F32),
            shape,
            shape,
        ],
        scratch_shapes=[
            pltpu.VMEM((width + 16, rows), BF),
            pltpu.VMEM((n, size, chunk), BF),
            pltpu.VMEM((width, chunk), BF),
            pltpu.VMEM((rows, chunk), BF),
            pltpu.VMEM((2, n, size, chunk), BF),
            pltpu.SemaphoreType.DMA((2, 2)),
        ],
        compiler_params=params(),
        cost_estimate=cost(6 * rows * width * hidden, 25e6),
        name="up_grad",
    )


def mid_back_kernel(
    table_ref,
    da2_ref,
    w_ref,
    mid_ref,
    dy_ref,
    ctx1_ref,
    ctx2_ref,
    vec_ref,
    dmid_ref,
    dctx_ref,
    sums_ref,
    keep_ref,
    send_ref,
    acc,
    *,
    core_bit,
):
    i = pl.program_id(0)
    da2 = da2_ref[...]
    normed, rs = norm_parts(mid_ref[...])
    dy = dy_ref[...].astype(F32)
    dmid = norm_back(normed, rs, vec_ref[4:5, :], da2) + dy
    dmid_ref[...] = dmid
    dbr = dmid.astype(BF)
    dctx_ref[...] = dot_rt(dbr, w_ref[...]).astype(BF)
    total = lambda v: jnp.sum(v, axis=0, keepdims=True)
    sums = jnp.concatenate(
        [
            total(dbr.astype(F32)),
            total(da2 * normed),
            total(da2),
            total(dy),
            jnp.zeros((4, dy.shape[1]), F32),
        ],
        axis=0,
    )
    part = dot_lt(jnp.concatenate([ctx1_ref[...], ctx2_ref[...]], axis=1), dbr)

    @pl.when(i == 0)
    def _():
        sums_ref[...] = sums
        acc[...] = part

    @pl.when(i > 0)
    def _():
        sums_ref[...] += sums
        acc[...] += part

    @pl.when(i == pl.num_programs(0) - 1)
    def _():
        store_units(table_ref, acc, keep_ref, send_ref, core_bit, put_rows, True)


def mid_back(table, da2, w_out, mid, dy, ctx, vec, n, core_bit, deps=()):
    rows, width = dy.shape
    unit = width // n
    block = 256
    by_rows = lambda m: pl.BlockSpec((block, m), lambda i: (i, 0))
    whole = lambda a: pl.BlockSpec(a.shape, lambda i: (0, 0))
    units = pl.BlockSpec((n // 2, unit, width), lambda i: (0, 0, 0))
    shape = jax.ShapeDtypeStruct((n // 2, unit, width), BF)
    return call(
        functools.partial(mid_back_kernel, core_bit=core_bit),
        (table, da2, w_out, mid, dy, *ctx, vec),
        [
            pl.BlockSpec(memory_space=pltpu.SMEM),
            by_rows(width),
            whole(w_out),
            by_rows(width),
            by_rows(width),
            *(by_rows(c.shape[1]) for c in ctx),
            whole(vec),
        ],
        deps,
        grid=(rows // block,),
        out_specs=[
            by_rows(width),
            by_rows(width),
            pl.BlockSpec((8, width), lambda i: (0, 0)),
            units,
            units,
        ],
        out_shape=[
            jax.ShapeDtypeStruct((rows, width), F32),
            jax.ShapeDtypeStruct((rows, width), BF),
            jax.ShapeDtypeStruct((8, width), F32),
            shape,
            shape,
        ],
        scratch_shapes=[pltpu.VMEM((width, width), F32)],
        compiler_params=params(),
        cost_estimate=cost(4 * rows * width * width, 16e6),
        name="mid_back",
    )


def token_grad_kernel(x_ref, *refs):
    *parts, w_ref, dmid_ref, vec_ref, grad_ref = refs
    dproj = jnp.concatenate([ref[...] for ref in parts], axis=1)
    da1 = dot_rt(dproj, w_ref[:, : dproj.shape[1]])
    normed, rs = norm_parts(x_ref[...].astype(F32))
    grad_ref[...] = dmid_ref[...] + norm_back(normed, rs, vec_ref[0:1, :], da1)


def token_grad(tokens, parts, w_in, dmid, vec, deps=()):
    rows, width = tokens.shape
    block = 256
    by_rows = lambda m: pl.BlockSpec((block, m), lambda i: (i, 0))
    whole = lambda a: pl.BlockSpec(a.shape, lambda i: (0, 0))
    return call(
        token_grad_kernel,
        (tokens, *parts, w_in, dmid, vec),
        [by_rows(width)]
        + [by_rows(p.shape[1]) for p in parts]
        + [whole(w_in), by_rows(width), whole(vec)],
        deps,
        grid=(rows // block,),
        out_specs=by_rows(width),
        out_shape=jax.ShapeDtypeStruct((rows, width), F32),
        compiler_params=params(),
        cost_estimate=cost(2 * rows * width * w_in.shape[1], 17e6),
        name="token_grad",
    )


def in_grad_kernel(table_ref, n1_hbm, w_hbm, *refs, starts):
    count = len(starts)
    parts, refs = refs[:count], refs[count:]
    s2_ref, c1_ref, keep_hbm, send_hbm, n1_ref, w_ref, grads_ref, stage, in_sems, out_sems = refs
    rows, width = n1_ref.shape
    n, size, wide = stage.shape
    vec_at = wide - LANES
    pieces = [(at, min(width, vec_at - at)) for at in range(0, vec_at, width)]
    loads = [pltpu.make_async_copy(n1_hbm, n1_ref, in_sems.at[0])]
    loads.append(
        pltpu.make_async_copy(
            w_hbm.at[:, pl.ds(vec_at, LANES)], w_ref.at[:, pl.ds(vec_at, LANES)], in_sems.at[1]
        )
    )
    wanted = []
    for at, extent in pieces:
        cols = pl.ds(at, extent)
        group = [
            pltpu.make_async_copy(
                ref,
                grads_ref.at[:, pl.ds(start, ref.shape[1])],
                in_sems.at[2 + len(pieces) + i],
            )
            for i, (ref, start) in enumerate(zip(parts, starts, strict=True))
            if at <= start < at + extent
        ]
        group.append(
            pltpu.make_async_copy(
                w_hbm.at[:, cols], w_ref.at[:, cols], in_sems.at[2 + len(wanted)]
            )
        )
        wanted.append(group)
    for copy in loads + [c for group in wanted for c in group]:
        copy.start()
    for copy in loads:
        copy.wait()
    turned = jnp.transpose(n1_ref[...])
    gain = w_ref[:, vec_at : vec_at + 1].astype(F32)
    shift = w_ref[:, vec_at + 1 : vec_at + 2].astype(F32)
    dgain = jnp.zeros((width, 1), F32)
    dshift = jnp.zeros((width, 1), F32)
    places = [table_ref[d] for d in range(n)]
    sent = []

    def store(result, at, extent):
        for d in range(n):
            stage[places[d], :, at : at + extent] = result[d * size : (d + 1) * size, :].astype(BF)
        for i, ref in enumerate((keep_hbm, send_hbm)):
            copy = pltpu.make_async_copy(
                stage.at[pl.ds(i * (n // 2), n // 2), :, pl.ds(at, extent)],
                ref.at[:, :, pl.ds(at, extent)],
                out_sems.at[len(sent)],
            )
            copy.start()
            sent.append(copy)

    query_sums = None
    for (at, extent), group in zip(pieces, wanted, strict=True):
        for copy in group:
            copy.wait()
        grads = grads_ref[:, at : at + extent]
        sums = jnp.sum(grads.astype(F32), axis=0, keepdims=True)
        if at == 0:
            query_sums = sums
        weights = w_ref[:, at : at + extent].astype(F32)
        product = dot(turned, grads)
        dgain += jnp.sum(weights * product, axis=1, keepdims=True)
        dshift += jnp.sum(weights * sums, axis=1, keepdims=True)
        store(gain * product + shift * sums, at, extent)
    hidden_rows = c1_ref.shape[1] // width
    stacked = jnp.concatenate(
        [jnp.zeros((2, width), F32), query_sums, s2_ref[0:4, :]]
        + [c1_ref[0:1, g * width : (g + 1) * width] for g in range(hidden_rows)]
        + [jnp.zeros((LANES - 7 - hidden_rows, width), F32)],
        axis=0,
    )
    lane = lanes_of((width, LANES))
    own = jnp.where(lane == 0, dgain, jnp.where(lane == 1, dshift, 0.0))
    store(jnp.transpose(stacked) + own, vec_at, LANES)
    for copy in sent:
        copy.wait()


def in_grad(table, n1, w_in, parts, starts, s2, c1, deps=()):
    rows, width = n1.shape
    wide = w_in.shape[1]
    n = (table.shape[0] - 1) // 4
    pieces = -(-(wide - LANES) // width)
    shape = jax.ShapeDtypeStruct((n // 2, width // n, wide), BF)
    vmem = pl.BlockSpec(memory_space=pltpu.VMEM)
    anywhere = pl.BlockSpec(memory_space=pl.ANY)
    return call(
        functools.partial(in_grad_kernel, starts=starts),
        (table, n1, w_in, *parts, s2, c1),
        [pl.BlockSpec(memory_space=pltpu.SMEM)]
        + [anywhere] * (2 + len(parts))
        + [vmem] * 2,
        deps,
        out_specs=[anywhere] * 2,
        out_shape=[shape, shape],
        scratch_shapes=[
            pltpu.VMEM((rows, width), BF),
            pltpu.VMEM((width, wide), BF),
            pltpu.VMEM((rows, wide - LANES), BF),
            pltpu.VMEM((n, width // n, wide), BF),
            pltpu.SemaphoreType.DMA((2 + pieces + len(parts),)),
            pltpu.SemaphoreType.DMA((2 * (pieces + 1),)),
        ],
        compiler_params=pltpu.CompilerParams(vmem_limit_bytes=VMEM_LIMIT),
        cost_estimate=cost(2 * rows * width * wide, 12e6),
        name="in_grad",
    )


def stages_of(n_dp, n_fsdp):
    fsdp_bits = n_fsdp.bit_length() - 1
    dp_bits = n_dp.bit_length() - 1
    low = list(range(fsdp_bits // 2))[::-1]
    high = list(range(fsdp_bits // 2, fsdp_bits))[::-1]
    z_bits = list(range(fsdp_bits + 1, fsdp_bits + dp_bits))[::-1]
    core = fsdp_bits
    return core, ([core] + high + low + z_bits, [core] + low + high + z_bits)


def place_table(n_dp, n_fsdp):
    core, orders = stages_of(n_dp, n_fsdp)
    n = n_dp * n_fsdp
    table = np.zeros((n, 4 * n + 1), np.int32)
    for me in range(n):
        for absolute in range(2):
            base = 2 * n * absolute
            for d in range(n):
                away = d ^ me
                place = 0
                for bit in orders[(d >> core) & 1]:
                    of = d if absolute and bit > core else away
                    place = place * 2 + ((of >> bit) & 1)
                table[me, base + d] = place
                table[me, base + n + place] = d
        table[me, 4 * n] = (me >> core) & 1
    return table


def tied_columns_kernel(*refs):
    *parts, out_ref = refs
    at, size = 0, parts[0].shape[0]
    for ref in parts:
        out_ref[:size, at : at + ref.shape[1]] = ref[...]
        at += ref.shape[1]
    if out_ref.shape[0] > size:
        out_ref[size:, :] = jnp.zeros((out_ref.shape[0] - size, at), BF)


def tied_columns(parts, deps, rows):
    vmem = pl.BlockSpec(memory_space=pltpu.VMEM)
    shape = (rows, sum(p.shape[1] for p in parts))
    return call(
        tied_columns_kernel,
        parts,
        [vmem] * len(parts),
        deps,
        out_specs=vmem,
        out_shape=jax.ShapeDtypeStruct(shape, BF),
        cost_estimate=cost(0, 4 * shape[0] * shape[1]),
        name="tied_columns",
    )


def merge_kernel(*refs):
    *parts, out_ref = refs
    at = 0
    for ref in parts:
        out_ref[at : at + ref.shape[0]] = ref[:, : out_ref.shape[1]]
        at += ref.shape[0]


def merge(parts, deps, size=None):
    if not deps:
        return jnp.concatenate(parts, axis=0)
    vmem = pl.BlockSpec(memory_space=pltpu.VMEM)
    shape = (sum(p.shape[0] for p in parts), size or parts[0].shape[1], parts[0].shape[2])
    return call(
        merge_kernel,
        parts,
        [vmem] * len(parts),
        deps,
        out_specs=vmem,
        out_shape=jax.ShapeDtypeStruct(shape, BF),
        compiler_params=pltpu.CompilerParams(vmem_limit_bytes=SMALL_LIMIT),
        cost_estimate=cost(0, 4 * shape[0] * shape[1] * shape[2]),
        name="merge",
    )


class Exchange:
    def __init__(self, n_dp, n_fsdp):
        self.n = n_dp * n_fsdp
        self.count = self.n.bit_length() - 1
        self.core_bit, self.orders = stages_of(n_dp, n_fsdp)
        me = lax.axis_index("dp") * n_fsdp + lax.axis_index("fsdp")
        self.z = n_dp // 2
        self.z_groups = [list(range(c, n_dp, 2)) for c in range(2)]
        table = jnp.asarray(place_table(n_dp, n_fsdp))
        self.table = lax.dynamic_slice(table, (me, 0), (1, table.shape[1]))[0]

    def swap(self, value, stage):
        bits = [self.orders[(i >> self.core_bit) & 1][stage] for i in range(self.n)]
        return lax.ppermute(value, AXES, [(i, i ^ (1 << b)) for i, b in enumerate(bits)])

    def over_z(self, value, away):
        mask = away << (self.core_bit + 1)
        return lax.ppermute(value, AXES, [(i, i ^ mask) for i in range(self.n)])

    def over_plane(self, value, place):
        count = self.count - self.z.bit_length()

        def mask(core):
            bits = self.orders[core][1 : 1 + count]
            return sum(1 << b for k, b in enumerate(bits) if (place >> (count - 1 - k)) & 1)

        pairs = [(i, i ^ mask((i >> self.core_bit) & 1)) for i in range(self.n)]
        return lax.ppermute(value, AXES, pairs)

    def gather_z(self, rows, deps=()):
        held = rows[None]
        return merge([held] + [self.over_z(held, k) for k in range(1, self.z)], deps)

    def gather_plane(self, held, stage, deps=()):
        return merge((held, self.swap(held, stage)), deps)

    def with_core(self, parts, places):
        half = self.n // 2
        others = [self.swap(p, 0) for p in parts]
        return (
            tuple(parts) + tuple(others),
            tuple(places) + tuple(tuple(b + half for b in bases) for bases in places),
        )


class Halving:
    def __init__(self, exchange, keep, send):
        self.exchange, self.keep, self.send, self.stage = exchange, keep, send, 0

    def added(self, got, first, count):
        part = slice(first, first + count)
        return self.keep[part].astype(F32) + got[part].astype(F32)

    def step(self):
        got = self.exchange.swap(self.send, self.stage)
        self.stage += 1
        half = self.keep.shape[0] // 2
        self.keep, self.send = (self.added(got, k, half).astype(BF) for k in (0, half))
        return (self.send,)

    def to_plane(self):
        self.keep = parted(self.keep, self.exchange.swap(self.send, 0), self.exchange.z)
        return tuple(self.keep)

    def plane(self, after):
        got = [self.exchange.over_plane(k, i) for i, k in enumerate(self.keep) if i]
        self.keep = combine([self.keep[0], *got], after)
        return tuple(self.keep)

    def ask(self):
        got = self.exchange.swap(self.send, self.stage)
        self.stage += 1
        return got

    def join(self, other):
        self.keep = jnp.concatenate([self.keep, other.keep], axis=2)
        self.send = jnp.concatenate([self.send, other.send], axis=2)
        return (self.send,)

    def last(self):
        self.got = tuple(self.exchange.over_z(k, i + 1) for i, k in enumerate(self.keep[1:]))
        return self.got

def fold_both(first, second, deps):
    got = (first.ask(), second.ask())
    steps = 4

    def kernel(*refs):
        ins, outs = refs[:8], refs[8:]
        for k in range(4):
            keep, came = ins[2 * k], ins[2 * k + 1]
            outs[k][...] = (keep[...].astype(F32) + came[...].astype(F32)).astype(BF)

    ins, specs, out_specs, shapes = [], [], [], []
    for halving, came in zip((first, second), got, strict=True):
        count, size, width = halving.keep.shape
        half = count // 2
        block = half // steps
        for k in range(2):
            spec = pl.BlockSpec((block, size, width), lambda i, k=k: (i + k * steps, 0, 0))
            ins += [halving.keep, came]
            specs += [spec, spec]
            out_specs.append(pl.BlockSpec((block, size, width), lambda i: (i, 0, 0)))
            shapes.append(jax.ShapeDtypeStruct((half, size, width), BF))
    out = call(
        kernel,
        ins,
        specs,
        deps,
        grid=(steps,),
        out_specs=out_specs,
        out_shape=shapes,
        compiler_params=pltpu.CompilerParams(
            vmem_limit_bytes=SMALL_LIMIT, dimension_semantics=("arbitrary",)
        ),
        cost_estimate=cost(1e6, 12e6),
        name="fold_both",
    )
    first.keep, first.send, second.keep, second.send = out
    return (out[1], out[3])


def parted(keep, came, each):
    count, size, width = keep.shape

    def kernel(keep_ref, came_ref, *outs):
        for k, out in enumerate(outs):
            part = slice(k * each, (k + 1) * each)
            out[...] = (keep_ref[part].astype(F32) + came_ref[part].astype(F32)).astype(BF)

    vmem = pl.BlockSpec(memory_space=pltpu.VMEM)
    shape = jax.ShapeDtypeStruct((each, size, width), BF)
    return call(
        kernel,
        (keep, came),
        [vmem] * 2,
        (),
        out_specs=[vmem] * (count // each),
        out_shape=[shape] * (count // each),
        compiler_params=pltpu.CompilerParams(vmem_limit_bytes=SMALL_LIMIT),
        cost_estimate=cost(count * size * width, 6 * count * size * width),
        name="parted",
    )


def join_along_z(wide, deep, exchange, deps):
    ins = (wide.keep, wide.ask(), deep.keep, deep.ask())
    z, size, columns = wide.keep.shape
    _, tall, width = deep.keep.shape
    blocks = columns // width

    def kernel(*refs):
        wide_ref, wide_came, deep_ref, deep_came, out_ref = refs
        total = (wide_ref[0].astype(F32) + wide_came[0].astype(F32)).astype(BF)
        for b in range(blocks):
            out_ref[0, b * size : (b + 1) * size, :] = total[:, b * width : (b + 1) * width]
        total = (deep_ref[0].astype(F32) + deep_came[0].astype(F32)).astype(BF)
        out_ref[0, blocks * size :, :] = total

    one = lambda *dims: pl.BlockSpec((1, *dims), lambda i: (i, 0, 0))
    rows = blocks * size + tall
    joined = call(
        kernel,
        ins,
        [one(size, columns)] * 2 + [one(tall, width)] * 2,
        deps,
        grid=(z,),
        out_specs=one(rows, width),
        out_shape=jax.ShapeDtypeStruct((z, rows, width), BF),
        compiler_params=pltpu.CompilerParams(
            vmem_limit_bytes=SMALL_LIMIT, dimension_semantics=("arbitrary",)
        ),
        cost_estimate=cost(1e6, 5e6),
        name="join_along_z",
    )
    return joined, lax.psum_scatter(
        joined, "dp", scatter_dimension=0, tiled=True, axis_index_groups=exchange.z_groups
    )


def combine(parts, deps):
    count, size, width = parts[0].shape

    def kernel(*refs):
        ins, outs = refs[: len(parts)], refs[len(parts) :]
        for k, out in enumerate(outs):
            out[0] = sum(r[k].astype(F32) for r in ins).astype(BF)

    vmem = pl.BlockSpec(memory_space=pltpu.VMEM)
    shape = jax.ShapeDtypeStruct((1, size, width), BF)
    return call(
        kernel,
        parts,
        [vmem] * len(parts),
        deps,
        out_specs=[vmem] * count,
        out_shape=[shape] * count,
        compiler_params=pltpu.CompilerParams(vmem_limit_bytes=SMALL_LIMIT),
        cost_estimate=cost(len(parts) * count * size * width, 8 * count * size * width),
        name="combine",
    )


def finish(in_parts, others, cols, vrows, hidden, deps):
    size = in_parts[0].shape[1]
    width = others.shape[2]
    blocks = hidden // width
    tall = others.shape[1] - (blocks + 1) * size

    def kernel(*refs):
        *ins, others_ref, in_ref, vec_ref, out_ref, up_ref, down_ref = refs
        total = sum(r[0].astype(F32) for r in ins)
        in_ref[...] = total[:, :cols]
        table = jnp.concatenate([total[:, cols:], jnp.zeros((LANES - size, LANES), F32)], axis=0)
        vec_ref[...] = jnp.transpose(table)[:vrows, :size]
        for b in range(blocks):
            rows = others_ref[0, b * size : (b + 1) * size, :]
            up_ref[:, b * width : (b + 1) * width] = rows.astype(F32)
        at = blocks * size
        out_ref[...] = others_ref[0, at : at + size, :].astype(F32)
        down_ref[...] = others_ref[0, at + size :, :].astype(F32)

    vmem = pl.BlockSpec(memory_space=pltpu.VMEM)
    shape = lambda *dims: jax.ShapeDtypeStruct(dims, F32)
    return call(
        kernel,
        (*in_parts, others),
        [vmem] * (len(in_parts) + 1),
        deps,
        out_specs=[vmem] * 5,
        out_shape=[
            shape(size, cols),
            shape(vrows, size),
            shape(size, width),
            shape(size, hidden),
            shape(tall, width),
        ],
        cost_estimate=cost(1, 3e6),
        name="finish",
    )


def body(
    tokens, first_values, out_grad, lengths, in_proj, out_proj, up_proj, down_proj, vectors,
    *, n_dp, n_fsdp
):
    width = tokens.shape[1]
    cols = in_proj.shape[1]
    vrows = vectors.shape[0]
    exchange = Exchange(n_dp, n_fsdp)
    n, core_bit, table = exchange.n, exchange.core_bit, exchange.table

    z = exchange.z
    planes = exchange.count - z.bit_length()
    quarter = n // 8

    vec_t = jnp.pad(vectors.T, ((0, 0), (0, LANES - vrows)))
    early = tied_columns((out_proj, up_proj), (table,), out_proj.shape[0])[None]
    held = exchange.gather_z(jnp.concatenate([in_proj, vec_t], axis=1), (early,))
    others = [exchange.over_z(early, k) for k in range(1, z)]
    if planes == 2:
        got_a, got_b = exchange.swap(held, 1), exchange.swap(held, 2)
        got_ba = exchange.swap(merge((got_a,), tuple(others)), 2)
        in_parts = exchange.with_core(
            (held, got_b, got_a, got_ba), tuple((q * quarter,) for q in range(4))
        )
    else:
        for stage in range(planes, 0, -1):
            held = exchange.gather_plane(held, stage)
        in_parts = exchange.with_core((held,), ((0,),))

    w_down = lax.all_gather(down_proj, AXES, axis=0, tiled=False)
    half = width // LANES // 2
    held_mid = jnp.concatenate([early, *others], axis=0)
    w_in, n1, qkv, vec = in_forward(table, tokens, first_values, in_parts, (held_mid,))
    for stage in range(planes, 1, -1):
        held_mid = exchange.gather_plane(held_mid, stage, (n1,))
    ctx1, ctx2, lse1, lse2 = attn_forward(lengths, qkv, width, (held_mid,))
    got_mid = merge((exchange.swap(held_mid, 1),), (ctx1,))
    mid_parts = exchange.with_core((held_mid, got_mid), ((0,), (n // 4,)))
    ctx = (ctx1, ctx2)
    u, mid, a2, w_out, *halves = ffn_forward(
        table, ctx, tokens, out_grad, vec, mid_parts, core_bit
    )
    h_down = Halving(exchange, *halves)
    dc1, da2, *halves = up_grad(
        table, out_grad, a2, w_down, u, mid_parts, (h_down.keep,)
    )
    h_up = Halving(exchange, *halves)
    deps = h_down.step()
    dmid, dctx, sums2, *halves = mid_back(
        table, da2, w_out, mid, out_grad, ctx, vec, n, core_bit, deps
    )
    h_out = Halving(exchange, *halves)
    fold_both(h_up, h_down, (sums2,))
    h_out.step()
    deps = h_up.join(h_out)
    dq1, dk1, dv1 = attn_backward(lengths, lse1, qkv, ctx1, dctx, 0, half, BF, deps)
    for _ in range(planes - 2):
        h_down.step(), h_up.step()
    deps = h_up.step() + (dq1,)
    h_down.send = merge((h_down.send,), (dq1,))
    dq2, dk2, first_grad = attn_backward(
        lengths, lse2, qkv, ctx2, dctx, half, half, F32, deps
    )
    joined, others = join_along_z(h_up, h_down, exchange, (dq2,))
    deps = (joined,)
    split = half * LANES
    parts = (dq1, dq2, dk1, dk2, dv1)
    starts = (0, split, width, width + split, 2 * width)
    h_in = Halving(
        exchange, *in_grad(table, n1, w_in, parts, starts, sums2, dc1, deps)
    )
    deps = h_in.to_plane()
    input_grad = token_grad(tokens, parts, w_in, dmid, vec, deps)
    first = out_forward(u, mid, w_down, vec, 0, (), deps + (input_grad,))
    deps = h_in.plane((first,))
    output = out_forward(u, mid, w_down, vec, 1, (first,), deps + (others,))
    g_in, g_vec, g_out, g_up, g_down = finish(
        (h_in.keep[0], *h_in.last()), others, cols, vrows, up_proj.shape[1], (output,)
    )
    return (output, input_grad, first_grad, g_in, g_out, g_up, g_down, g_vec)


def solution(mesh):
    rows = P(AXES, None)
    cols = P(None, AXES)
    return jax.shard_map(
        functools.partial(body, n_dp=mesh.shape["dp"], n_fsdp=mesh.shape["fsdp"]),
        mesh=mesh,
        in_specs=(rows,) * 8 + (cols,),
        out_specs=(rows,) * 7 + (cols,),
        check_vma=False,
    )
```
